32 devices in a mesh: dom: 8 (over z, core), mem: 4 (over y, x).
Axes of the slice: x: 2, y: 2, z: 4, core: 2. Of those that a mesh axis runs over, the one named last changes fastest.
Arguments:
- coarse_latents: bfloat16 [4, 4096, 512], P('mem', 'dom'), may hold values from -6 to 6
- send_rows: int32 [8, 8, 128], P('dom'), may hold values from 0 to 511
- up_index: int32 [3, 16384], P(None, 'dom'), may hold values from 0 to 1023
- up_weight: float32 [3, 16384], P(None, 'dom'), may hold values from 0.2 to 1
- neighbors: int32 [6, 16384], P(None, 'dom'), may hold values from 0 to 2303, as said below
- live_counts: int32 [8], P('dom'), may hold values from 1 to 2048, 12288 in all
- area: float32 [16384], P('dom'), may hold values from 0.25 to 4.5
- fine_skip: bfloat16 [16384, 512], P('dom'), may hold values from -6 to 6
- targets: bfloat16 [83, 16384], P(None, 'dom'), may hold values from -6 to 6
- kernel_width: float32 [83], replicated, may hold values from 0.5 to 2
- w_in: bfloat16 [1024, 512], replicated, may hold values from -0.1875 to 0.1875
- w_out: bfloat16 [512, 512], replicated, may hold values from -0.25 to 0.25
- ln_gain: float32 [512], replicated, may hold values from 0.1 to 1.9
- w_head: bfloat16 [512, 83], replicated, may hold values from -0.25 to 0.25
Outputs:
- grad_latent: bfloat16 [4, 16384, 512], P('mem', 'dom')
- grad_head: float32 [8, 512, 83], P('dom')
The draws below stay inside these ranges and needn't reach their ends.
Inputs may be any that keep to these rules, and one draw needn't show every extreme that they name: neighbors[k, p] = 128 + (p % 2048) + e with -128 <= e <= 128.
All inputs are finite; a program needn't handle non-finite values. No bound on the sum of `live_counts` on one device may be relied on, other than what follows from the above.
Results may differ from the reference program's by a relative error of at most 0.015.
The reference program's roundings to bfloat16 on the way count: a program that leaves them out, or rounds other values in their place, can miss the bound.
Values may be sent and summed in bfloat16 or wider, within the bound.
No kernel may reach another device: no remote copies, remote signals or barrier semaphores. Data moves between devices by JAX's collectives and lax.ppermute only.
A program may use at most 128 MiB of HBM per device.

```python
import math
import jax
import jax.numpy as jnp
import numpy as np
from jax import lax

H = 512
HID = 512
VARS = 83
K_UP = 3
K_NB = 6
RIM = 128
SLOT = 128
FINE_DEV = 2048
C_DEV = 512
MEMBERS = 4
POINTS = 16384
COARSE = 4096
N_DOM = 8


def draw_neighbors(key, part):
    offsets = jax.random.randint(key, (K_NB, POINTS), -RIM, RIM + 1)
    local = jnp.arange(POINTS, dtype=jnp.int32) % FINE_DEV
    rows = jnp.arange(K_NB, dtype=jnp.int32)[:, None]
    offsets = jnp.where((rows == 0) & (local[None, :] == FINE_DEV - 1), RIM, offsets)
    offsets = jnp.where((rows == 1) & (local[None, :] == 0), -RIM, offsets)
    return (RIM + local[None, :] + offsets).astype(jnp.int32)


def draw_area(key, part):
    rising = 1.0 + 2.0 * jnp.arange(POINTS, dtype=jnp.float32) / POINTS
    rough = jax.random.uniform(key, (POINTS,), jnp.float32, 0.5, 1.5)
    return (rising * rough).astype(jnp.float32)


def touch_ends(drawn, rng, smallest, high):
    longest = drawn.shape.index(max(drawn.shape))
    spots = []
    for shift in (0, 1):
        where = [jax.random.randint(jax.random.fold_in(rng, axis), (), 0, length) for axis, length in enumerate(drawn.shape)]
        where[longest] = (where[longest] + shift) % drawn.shape[longest]
        spots.append(tuple(where))
    return drawn.at[spots[0]].set(smallest).at[spots[1]].set(high)


def block_levels(rng, dims, pieces, least, high):
    def one(position, blocks):
        draws = jax.random.uniform(jax.random.fold_in(jax.random.fold_in(rng, 6), position), (blocks,), jnp.float32, least / len(pieces), high / len(pieces))
        return jnp.repeat(jnp.exp(draws), dims[position] // blocks).reshape((-1,) + (1,) * (len(dims) - position - 1))

    level = one(*pieces[0])
    for cut in pieces[1:]:
        level = level * one(*cut)
    return level


def split_up(count, total, most, lean):
    loads = [(1 << 20) // math.isqrt(rank ** lean) + 1 for rank in range(2, count + 1)]
    rest, counts = total - most - (count - 1), [1] * (count - 1)
    while rest > 0:
        candidates = [i for i in range(count - 1) if counts[i] < most]
        mass, remaining = sum([loads[i] for i in candidates]), rest
        for i in candidates:
            more = min(most - counts[i], max(1, remaining * loads[i] // mass), rest)
            counts[i] = counts[i] + more
            rest = rest - more
    return np.array([most] + counts)


def ragged_sizes(own_key, amount, total, limit, skew):
    if amount == 2:
        one = jax.random.randint(own_key, (), max(1, total - limit), min(limit, total - 1) + 1)
        return jnp.stack([one, total - one])
    tallies = jnp.asarray(split_up(amount, total, limit, skew), jnp.int32)
    pairs = (amount - 1) // 2
    giver, taker = tallies[1:1 + 2 * pairs:2], tallies[2:2 + 2 * pairs:2]
    slack = jnp.minimum(giver - 1, limit - taker)
    passed = jax.random.randint(jax.random.fold_in(own_key, 1), (pairs,), 0, 1 << 20) % (slack + 1)
    tallies = tallies.at[1:1 + 2 * pairs:2].set(giver - passed).at[2:2 + 2 * pairs:2].set(taker + passed)
    return tallies[jax.random.permutation(jax.random.fold_in(own_key, 2), amount)]


def scatter_about(stream_key, dims, scale, most, split=(), held_as=jnp.bfloat16):
    values = scale * jax.random.normal(stream_key, dims, jnp.float32)
    if split:
        values = values * block_levels(stream_key, dims, split, -0.22, 0.18)
    return jnp.clip(values, -most, most).astype(held_as)


def setup_inputs(seed: int = 0) -> dict:
    key_of = jax.random.split(jax.random.key(seed), 15)
    coarse_latents = scatter_about(key_of[0], (MEMBERS, COARSE, H), 1.0, 6.0, ((0, 4), (1, 8)))
    send_rows = touch_ends(jax.random.randint(key_of[1], (N_DOM, N_DOM, SLOT), 0, C_DEV), jax.random.fold_in(key_of[1], 1), 0, C_DEV - 1).astype(jnp.int32)
    up_index = touch_ends(jax.random.randint(key_of[2], (K_UP, POINTS), 0, N_DOM * SLOT), jax.random.fold_in(key_of[2], 1), 0, (N_DOM * SLOT) - 1).astype(jnp.int32)
    up_weight = jnp.clip(0.2 + 0.8 * jax.random.uniform(key_of[3], (K_UP, POINTS), jnp.float32) ** block_levels(key_of[3], (K_UP, POINTS), ((1, 8),), -0.2, 0.2), 0.2, 1.0)
    neighbors = draw_neighbors(jax.random.fold_in(key_of[14], 71), 0)
    live_counts = ragged_sizes(key_of[5], N_DOM, N_DOM * FINE_DEV * 3 // 4, FINE_DEV, 1).astype(jnp.int32)
    area = draw_area(jax.random.fold_in(key_of[14], 71), 0)
    fine_skip = scatter_about(key_of[7], (POINTS, H), 1.0, 6.0, ((0, 8),))
    targets = scatter_about(key_of[8], (VARS, POINTS), 1.0, 6.0, ((1, 8),))
    kernel_width = jnp.clip(jnp.exp(jax.random.uniform(key_of[9], (VARS,), jnp.float32, math.log(0.5), math.log(2.0))), 0.5, 2.0)
    w_in = scatter_about(key_of[10], (2 * H, HID), (2 * H) ** -0.5, 0.1875)
    w_out = scatter_about(key_of[11], (HID, H), HID ** -0.5, 0.25)
    ln_gain = jnp.clip(1.0 + 0.18 * jax.random.normal(key_of[12], (H,), jnp.float32), 0.1, 1.9)
    w_head = scatter_about(key_of[13], (H, VARS), H ** -0.5, 0.25)
    return {"coarse_latents": coarse_latents, "send_rows": send_rows, "up_index": up_index, "up_weight": up_weight, "neighbors": neighbors, "live_counts": live_counts, "area": area, "fine_skip": fine_skip, "targets": targets, "kernel_width": kernel_width, "w_in": w_in, "w_out": w_out, "ln_gain": ln_gain, "w_head": w_head}


def slope(diff, inv_sq):
    return -(diff * inv_sq) * jnp.exp(-0.5 * diff * diff * inv_sq)

def member_pass(coarse_m, send_rows, up_index, up_weight, neighbors, fine_skip, w_in, w_out, ln_gain, w_head):
    blocks = coarse_m.reshape(N_DOM, C_DEV, H)
    sent = jax.vmap(lambda blk, rows: blk[rows])(blocks, send_rows)
    received = jnp.transpose(sent, (1, 0, 2, 3)).reshape(N_DOM, N_DOM * SLOT, H)
    index_blk = up_index.reshape(K_UP, N_DOM, FINE_DEV)
    weight_blk = up_weight.reshape(K_UP, N_DOM, FINE_DEV)
    unpooled = jnp.zeros((N_DOM, FINE_DEV, H), jnp.float32)
    for k in range(K_UP):
        picked = jax.vmap(lambda table, rows: table[rows])(received, index_blk[k])
        unpooled = unpooled + weight_blk[k][:, :, None] * picked.astype(jnp.float32)
    x = (fine_skip.reshape(N_DOM, FINE_DEV, H).astype(jnp.float32) + unpooled).astype(jnp.bfloat16)
    zero_rim = jnp.zeros((1, RIM, H), jnp.bfloat16)
    before = jnp.concatenate([zero_rim, x[:-1, FINE_DEV - RIM:]], axis=0)
    after = jnp.concatenate([x[1:, :RIM], zero_rim], axis=0)
    extended = jnp.concatenate([before, x, after], axis=1)
    nb_blk = neighbors.reshape(K_NB, N_DOM, FINE_DEV)
    total = jnp.zeros((N_DOM, FINE_DEV, H), jnp.float32)
    for k in range(K_NB):
        total = total + jax.vmap(lambda table, rows: table[rows])(extended, nb_blk[k]).astype(jnp.float32)
    agg = (total / K_NB).astype(jnp.bfloat16).reshape(POINTS, H)
    flat_x = x.reshape(POINTS, H)
    pre = jnp.dot(flat_x, w_in[:H], preferred_element_type=jnp.float32) + jnp.dot(agg, w_in[H:], preferred_element_type=jnp.float32)
    act = jax.nn.silu(pre).astype(jnp.bfloat16)
    upd = jnp.dot(act, w_out, preferred_element_type=jnp.float32)
    mean_upd = lax.optimization_barrier(jnp.mean(upd, axis=1, keepdims=True))
    centred = upd - mean_upd
    var_upd = lax.optimization_barrier(jnp.mean(centred * centred, axis=1, keepdims=True))
    hidden = (flat_x.astype(jnp.float32) + centred * lax.rsqrt(var_upd + 1e-05) * ln_gain.astype(jnp.float32)[None, :]).astype(jnp.bfloat16)
    pred = lax.dot_general(w_head, hidden, (((0,), (1,)), ((), ())), preferred_element_type=jnp.float32).astype(jnp.bfloat16)
    return (hidden, pred)

def reference(coarse_latents, send_rows, up_index, up_weight, neighbors, live_counts, area, fine_skip, targets, kernel_width, w_in, w_out, ln_gain, w_head):

    def forward(coarse_m):
        return member_pass(coarse_m, send_rows, up_index, up_weight, neighbors, fine_skip, w_in, w_out, ln_gain, w_head)
    preds = lax.map(lambda c: forward(c)[1], coarse_latents)
    inv_sq = (1.0 / (kernel_width.astype(jnp.float32) * kernel_width.astype(jnp.float32)))[:, None]
    place = jnp.arange(POINTS, dtype=jnp.int32)
    live = (place % FINE_DEV < live_counts[place // FINE_DEV]).astype(jnp.float32)
    weight = (area.astype(jnp.float32) * live)[None, :]
    target_f = targets.astype(jnp.float32)

    def score_one(pred_i):
        pred_f = pred_i.astype(jnp.float32)

        def add_member(j, acc):
            other = lax.dynamic_index_in_dim(preds, j, 0, keepdims=False).astype(jnp.float32)
            return acc + slope(pred_f - other, inv_sq)
        acc = lax.fori_loop(0, MEMBERS, add_member, jnp.zeros((VARS, POINTS), jnp.float32))
        return (weight * (acc / MEMBERS - slope(pred_f - target_f, inv_sq))).astype(jnp.bfloat16)
    gscores = lax.map(score_one, preds)

    def backward(carry, pair):
        coarse_m, gscore = pair
        hidden, unused = forward(coarse_m)
        grad_m = lax.dot_general(gscore, w_head, (((0,), (1,)), ((), ())), preferred_element_type=jnp.float32).astype(jnp.bfloat16)
        hidden_blk = hidden.reshape(N_DOM, FINE_DEV, H).astype(jnp.float32)
        score_blk = gscore.reshape(VARS, N_DOM, FINE_DEV).astype(jnp.float32)
        head_term = jnp.einsum('dph,vdp->dhv', hidden_blk, score_blk)
        return (carry + head_term, grad_m)
    head_total, grad_latent = lax.scan(backward, jnp.zeros((N_DOM, H, VARS), jnp.float32), (coarse_latents, gscores))
    return (grad_latent, head_total * (1.0 / math.sqrt(MEMBERS * FINE_DEV)))
```

```python
import functools
import math

import jax
import jax.numpy as jnp
from jax import lax
from jax.experimental import pallas as pl
from jax.experimental.pallas import tpu as pltpu
from jax.sharding import PartitionSpec as P

RIM = 128
MIB = 1024 * 1024
F32 = jnp.float32
BF16 = jnp.bfloat16
VMEM = pltpu.VMEM


def dot(a, b):
    return jnp.dot(a, b, preferred_element_type=F32)


def dot_of(a, b, da, db):
    return lax.dot_general(a, b, (((da,), (db,)), ((), ())), preferred_element_type=F32)


def params(mib):
    return pltpu.CompilerParams(vmem_limit_bytes=mib * MIB)


def cost(flops, nbytes, trans=0):
    return pl.CostEstimate(flops=flops, bytes_accessed=nbytes, transcendentals=trans)


def columns(rows):
    pad = -rows.shape[0] % 8
    if pad:
        rows = jnp.concatenate([rows, jnp.zeros((pad, rows.shape[1]), rows.dtype)], axis=0)
    return rows.T


def slope(diff, inv_sq):
    return -(diff * inv_sq) * jnp.exp(-0.5 * diff * diff * inv_sq)


def xor_permute(value, axis, step):
    count = lax.axis_size(axis)
    return lax.ppermute(value, axis, [(i, i ^ step) for i in range(count)])


def pick_kernel(send_ref, coarse_ref, *outs):
    me = lax.axis_index("dom")
    rows = jnp.concatenate([send_ref[0, pl.ds(me ^ s, 1), :] for s in range(len(outs))], axis=0)
    cols = columns(rows.astype(F32))
    table = coarse_ref[0]
    spots = lax.broadcasted_iota(jnp.int32, (rows.shape[1], table.shape[0]), 1).astype(F32)
    for s, out in enumerate(outs):
        hot = (cols[:, s : s + 1] == spots).astype(F32).astype(BF16)
        out[...] = dot(hot, table).astype(BF16)


def pick(send_rows, coarse):
    _, count, slots = send_rows.shape
    width = coarse.shape[2]
    return pl.pallas_call(
        pick_kernel,
        out_shape=[jax.ShapeDtypeStruct((slots, width), BF16)] * count,
        in_specs=[pl.BlockSpec(memory_space=VMEM)] * 2,
        out_specs=[pl.BlockSpec(memory_space=VMEM)] * count,
        compiler_params=params(16),
        cost_estimate=cost(2 * count * slots * coarse.shape[1] * width, 2 * MIB),
        name="pick",
    )(send_rows, coarse)


def spread_kernel(tile, index_ref, weight_ref, nb_ref, high_ref, low_ref, count_ref):
    me = lax.axis_index("dom")
    t = pl.program_id(0)
    slots = high_ref.shape[1]
    index = (index_ref[...] ^ (me * 128)).astype(F32)
    cols = columns(jnp.concatenate([index, weight_ref[...]], axis=0))
    k_up = index.shape[0]
    spots = lax.broadcasted_iota(jnp.int32, (tile, slots), 1).astype(F32)
    total = jnp.zeros((tile, slots), F32)
    for k in range(k_up):
        total = total + jnp.where(cols[:, k : k + 1] == spots, cols[:, k_up + k : k_up + k + 1], 0.0)
    high = total.astype(BF16)
    high_ref[...] = high
    low_ref[...] = (total - high.astype(F32)).astype(BF16)
    near = columns((nb_ref[...] - t * tile).astype(F32))
    span = count_ref.shape[2]
    places = lax.broadcasted_iota(jnp.int32, (tile, span), 1).astype(F32)
    counts = jnp.zeros((tile, span), F32)
    for k in range(nb_ref.shape[0]):
        counts = counts + jnp.where(near[:, k : k + 1] == places, 1.0, 0.0)
    count_ref[0] = counts.astype(BF16)


def spread(up_index, up_weight, neighbors, slots, tile):
    k_up, rows = up_index.shape
    k_nb = neighbors.shape[0]
    steps = rows // tile
    span = tile + 2 * RIM
    return pl.pallas_call(
        functools.partial(spread_kernel, tile),
        grid=(steps,),
        out_shape=[
            jax.ShapeDtypeStruct((rows, slots), BF16),
            jax.ShapeDtypeStruct((rows, slots), BF16),
            jax.ShapeDtypeStruct((steps, tile, span), BF16),
        ],
        in_specs=[
            pl.BlockSpec((k_up, tile), lambda t: (0, t)),
            pl.BlockSpec((k_up, tile), lambda t: (0, t)),
            pl.BlockSpec((k_nb, tile), lambda t: (0, t)),
        ],
        out_specs=[
            pl.BlockSpec((tile, slots), lambda t: (t, 0)),
            pl.BlockSpec((tile, slots), lambda t: (t, 0)),
            pl.BlockSpec((1, tile, span), lambda t: (t, 0, 0)),
        ],
        compiler_params=params(24),
        cost_estimate=cost(40 * rows * slots, 4 * rows * slots),
        name="spread",
    )(up_index, up_weight, neighbors)


def unpool_kernel(parts, high_ref, low_ref, skip_ref, *refs):
    tables, (x_ref, first_ref, last_ref) = refs[:parts], refs[parts:]
    t = pl.program_id(0)
    table = jnp.concatenate([r[...] for r in tables], axis=0)
    total = dot(high_ref[...], table) + dot(low_ref[...], table)
    x = (skip_ref[...].astype(F32) + total).astype(BF16)
    x_ref[...] = x

    @pl.when(t == 0)
    def _():
        first_ref[...] = x[:RIM]

    @pl.when(t == pl.num_programs(0) - 1)
    def _():
        last_ref[...] = x[x.shape[0] - RIM :]


def unpool(high, low, skip, tables, tile):
    rows, width = skip.shape
    slots = high.shape[1]
    count = len(tables)
    edge = jax.ShapeDtypeStruct((RIM, width), BF16)
    return pl.pallas_call(
        functools.partial(unpool_kernel, count),
        grid=(rows // tile,),
        out_shape=[jax.ShapeDtypeStruct((rows, width), BF16), edge, edge],
        in_specs=[
            pl.BlockSpec((tile, slots), lambda t: (t, 0)),
            pl.BlockSpec((tile, slots), lambda t: (t, 0)),
            pl.BlockSpec((tile, width), lambda t: (t, 0)),
        ]
        + [pl.BlockSpec(r.shape, lambda t: (0, 0)) for r in tables],
        out_specs=[
            pl.BlockSpec((tile, width), lambda t: (t, 0)),
            pl.BlockSpec((RIM, width), lambda t: (0, 0)),
            pl.BlockSpec((RIM, width), lambda t: (0, 0)),
        ],
        compiler_params=params(24),
        cost_estimate=cost(4 * rows * slots * width, 16 * MIB),
        name="unpool",
    )(high, low, skip, *tables)


def update_kernel(chunk, members, rimmed, x_ref, count_ref, w_in_ref, w_out_ref, gain_ref, head_ref, *refs):
    if rimmed:
        before_ref, after_ref, *refs = refs
    h_ref, preds = refs[0], refs[1:]
    me = lax.axis_index("mem")
    tiles, tile, _ = count_ref.shape
    rows, width = x_ref.shape
    gain = gain_ref[...]
    for s in range(members):
        t = lax.rem(1 + chunk * members + (me ^ s), tiles)
        start = pl.multiple_of(t * tile, tile)
        above = pl.multiple_of(jnp.maximum(start - RIM, 0), RIM)
        below = pl.multiple_of(jnp.minimum(start + tile, rows - RIM), RIM)
        x = x_ref[pl.ds(start, tile), :]
        top = x_ref[pl.ds(above, RIM), :]
        bottom = x_ref[pl.ds(below, RIM), :]
        if rimmed:
            top = jnp.where(t == 0, before_ref[...], top)
            bottom = jnp.where(t == tiles - 1, after_ref[...], bottom)
        window = jnp.concatenate([top, x, bottom], axis=0)
        agg = (dot(count_ref[t], window) * (1.0 / 6.0)).astype(BF16)
        pre = dot(x, w_in_ref[:width, :]) + dot(agg, w_in_ref[width:, :])
        act = (0.5 * pre * (1.0 + jnp.tanh(0.5 * pre))).astype(BF16)
        upd = dot(act, w_out_ref[...])
        mean = jnp.mean(upd, axis=1, keepdims=True)
        centred = upd - mean
        var = jnp.mean(centred * centred, axis=1, keepdims=True)
        h = (x.astype(F32) + centred * lax.rsqrt(var + 1e-05) * gain).astype(BF16)
        h_ref[pl.ds(s * tile, tile), :] = h
        preds[s][...] = dot_of(head_ref[...], h, 1, 1).astype(BF16)


def update(chunk, members, x, counts, w_in, w_out, gain, head, rims):
    tiles, tile, _ = counts.shape
    width = x.shape[1]
    points = members * tile
    operands = (x, counts, w_in, w_out, gain, head) + rims
    return pl.pallas_call(
        functools.partial(update_kernel, chunk, members, bool(rims)),
        out_shape=[jax.ShapeDtypeStruct((points, width), BF16)]
        + [jax.ShapeDtypeStruct((head.shape[0], tile), BF16)] * members,
        in_specs=[pl.BlockSpec(memory_space=VMEM)] * len(operands),
        out_specs=[pl.BlockSpec(memory_space=VMEM)] * (1 + members),
        compiler_params=params(32),
        cost_estimate=cost(points * width * width * 10, 8 * MIB, points * width),
        name="update",
    )(*operands)


def score_kernel(members, chunk, tiles, inv_ref, weight_ref, target_ref, *refs):
    preds, outs = refs[:members], refs[members:]
    t = lax.rem(1 + chunk * members + lax.axis_index("mem"), tiles)
    inv_sq = inv_ref[...]
    weight = weight_ref[pl.ds(t, 1), :]
    target = target_ref[t].astype(F32)
    values = [r[...].astype(F32) for r in preds]
    sums = [jnp.zeros(v.shape, F32) for v in values]
    for i in range(members):
        for j in range(i + 1, members):
            phi = slope(values[i] - values[j], inv_sq)
            sums[i] = sums[i] + phi
            sums[j] = sums[j] - phi
    for i in range(members):
        outs[i][...] = (weight * (sums[i] * (1.0 / members) - slope(values[i] - target, inv_sq))).astype(BF16)


def score(chunk, inv_sq, weight, target, preds):
    members = len(preds)
    tiles = target.shape[0]
    return pl.pallas_call(
        functools.partial(score_kernel, members, chunk, tiles),
        out_shape=[jax.ShapeDtypeStruct(preds[0].shape, BF16)] * members,
        in_specs=[pl.BlockSpec(memory_space=VMEM)] * (3 + members),
        out_specs=[pl.BlockSpec(memory_space=VMEM)] * members,
        compiler_params=params(16),
        cost_estimate=cost(10 * preds[0].size * members * members, MIB, preds[0].size * members * members),
        name="score",
    )(inv_sq, weight, target, *preds)


def head_kernel(chunks, members, *refs):
    hidden, scores, out = refs[:chunks], refs[chunks:-1], refs[-1]
    tile = scores[0].shape[1]
    total = jnp.zeros(out.shape, F32)
    for c in range(chunks):
        for s in range(members):
            total = total + dot(scores[c * members + s][...], hidden[c][s * tile : (s + 1) * tile, :])
    out[...] = total.astype(BF16)


def head_terms(members, hidden, scores):
    width = hidden[0].shape[1]
    return pl.pallas_call(
        functools.partial(head_kernel, len(hidden), members),
        out_shape=jax.ShapeDtypeStruct((scores[0].shape[0], width), BF16),
        in_specs=[pl.BlockSpec(memory_space=VMEM)] * (len(hidden) + len(scores)),
        out_specs=pl.BlockSpec(memory_space=VMEM),
        compiler_params=params(16),
        cost_estimate=cost(2 * scores[0].size * len(scores) * width, 3 * MIB),
        name="head_terms",
    )(*hidden, *scores)


def latent_kernel(chunks, members, head_ref, *refs):
    scores, out = refs[:-1], refs[-1]
    me = lax.axis_index("mem")
    tile = scores[0].shape[1]
    tiles = chunks * members
    for c in range(chunks):
        for s in range(members):
            t = lax.rem(1 + c * members + (me ^ s), tiles)
            rows = pl.ds(pl.multiple_of(t * tile, tile), tile)
            out[0, rows, :] = dot_of(scores[c * members + s][...], head_ref[...], 0, 0).astype(BF16)


def latent_grad(chunks, members, head, scores):
    rows, width = scores[0].shape[1] * len(scores), head.shape[1]
    return pl.pallas_call(
        functools.partial(latent_kernel, chunks, members),
        out_shape=jax.ShapeDtypeStruct((1, rows, width), BF16),
        in_specs=[pl.BlockSpec(memory_space=VMEM)] * (1 + len(scores)),
        out_specs=pl.BlockSpec(memory_space=VMEM),
        compiler_params=params(16),
        cost_estimate=cost(2 * scores[0].size * len(scores) * width, 3 * MIB),
        name="latent_grad",
    )(head, *scores)


def total_kernel(scale, *refs):
    terms, out = refs[:-1], refs[-1]
    total = terms[0][...].astype(F32)
    for term in terms[1:]:
        total = total + term[...].astype(F32)
    out[0] = (total * scale).T[:, : out.shape[2]]


def head_total(terms, num_vars, scale):
    return pl.pallas_call(
        functools.partial(total_kernel, scale),
        out_shape=jax.ShapeDtypeStruct((1, terms[0].shape[1], num_vars), F32),
        in_specs=[pl.BlockSpec(memory_space=VMEM)] * len(terms),
        out_specs=pl.BlockSpec(memory_space=VMEM),
        compiler_params=params(16),
        cost_estimate=cost(terms[0].size * len(terms), MIB),
        name="head_total",
    )(*terms)


def shards(
    coarse_latents,
    send_rows,
    up_index,
    up_weight,
    neighbors,
    live_counts,
    area,
    fine_skip,
    targets,
    kernel_width,
    w_in,
    w_out,
    ln_gain,
    w_head,
):
    dom_count = lax.axis_size("dom")
    members = lax.axis_size("mem")
    rows, width = fine_skip.shape
    num_vars = w_head.shape[1]
    padded = num_vars + -num_vars % 16
    tile = min(256, rows // members)
    tiles = rows // tile
    chunks = tiles // members

    outgoing = pick(send_rows, coarse_latents)
    tables = [outgoing[0]] + [None] * (dom_count - 1)
    for s in range(dom_count - 1, 0, -1):
        tables[s] = xor_permute(outgoing[s], "dom", s)

    high, low, counts = spread(up_index, up_weight, neighbors, dom_count * send_rows.shape[2], tile)
    pad = padded - num_vars
    head = jnp.pad(w_head.T, ((0, pad), (0, 0)))
    inv_sq = jnp.pad(1.0 / (kernel_width * kernel_width), (0, pad))[:, None]
    target = jnp.pad(targets, ((0, pad), (0, 0))).reshape(padded, tiles, tile).transpose(1, 0, 2)
    local = jnp.arange(rows, dtype=jnp.int32)
    weight = (area * (local < live_counts[0]).astype(F32)).reshape(tiles, tile)
    gain = ln_gain[None, :]

    x, first, last = unpool(high, low, fine_skip, tables, tile)
    up = [(i, i + 1) for i in range(dom_count - 1)]
    before = lax.ppermute(last, "dom", up)
    after = lax.ppermute(first, "dom", [(j, i) for i, j in up])

    hidden, scores = [], []
    for c in range(chunks):
        rims = (before, after) if c == chunks - 1 else ()
        h, *preds = update(c, members, x, counts, w_in, w_out, gain, head, rims)
        hidden.append(h)
        preds = [preds[0]] + [xor_permute(preds[s], "mem", s) for s in range(1, members)]
        got = score(c, inv_sq, weight, target, preds)
        scores += [got[0]] + [xor_permute(got[s], "mem", s) for s in range(1, members)]
    term = head_terms(members, hidden, scores)
    terms = [term] + [xor_permute(term, "mem", s) for s in range(1, members)]
    grad_latent = latent_grad(chunks, members, head, scores)
    scale = 1.0 / math.sqrt(members * rows)
    return (grad_latent, head_total(terms, num_vars, scale))


def solution(mesh):
    return jax.shard_map(
        shards,
        mesh=mesh,
        in_specs=(
            P("mem", "dom", None),
            P("dom", None, None),
            P(None, "dom"),
            P(None, "dom"),
            P(None, "dom"),
            P("dom"),
            P("dom"),
            P("dom", None),
            P(None, "dom"),
            P(),
            P(),
            P(),
            P(),
            P(),
        ),
        out_specs=(P("mem", "dom", None), P("dom", None, None)),
        check_vma=False,
    )
```

```python
import functools
import math

import jax
import jax.numpy as jnp
from jax import lax
from jax.experimental import pallas as pl
from jax.experimental.pallas import tpu as pltpu
from jax.sharding import PartitionSpec as P

RIM = 128
MIB = 1024 * 1024
F32 = jnp.float32
BF16 = jnp.bfloat16
VMEM = pltpu.VMEM


def dot(a, b):
    return jnp.dot(a, b, preferred_element_type=F32)


def dot_of(a, b, da, db):
    return lax.dot_general(a, b, (((da,), (db,)), ((), ())), preferred_element_type=F32)


def params(mib):
    return pltpu.CompilerParams(vmem_limit_bytes=mib * MIB)


def cost(flops, nbytes, trans=0):
    return pl.CostEstimate(flops=flops, bytes_accessed=nbytes, transcendentals=trans)


def columns(rows):
    pad = -rows.shape[0] % 8
    if pad:
        rows = jnp.concatenate([rows, jnp.zeros((pad, rows.shape[1]), rows.dtype)], axis=0)
    return rows.T


def slope(diff, inv_sq):
    return -(diff * inv_sq) * jnp.exp(-0.5 * diff * diff * inv_sq)


def xor_permute(value, axis, step):
    count = lax.axis_size(axis)
    return lax.ppermute(value, axis, [(i, i ^ step) for i in range(count)])


def pick_kernel(send_ref, coarse_ref, *refs):
    outs, (rows_ref, table_ref, sems) = refs[:-3], refs[-3:]
    copies = [
        pltpu.make_async_copy(send_ref, rows_ref, sems.at[0]),
        pltpu.make_async_copy(coarse_ref, table_ref, sems.at[1]),
    ]
    for copy in copies:
        copy.start()
    me = lax.axis_index("dom")
    copies[0].wait()
    rows = jnp.concatenate([rows_ref[0, pl.ds(me ^ s, 1), :] for s in range(len(outs))], axis=0)
    cols = columns(rows.astype(F32))
    spots = lax.broadcasted_iota(jnp.int32, (rows.shape[1], table_ref.shape[1]), 1).astype(F32)
    copies[1].wait()
    table = table_ref[0]
    for s in reversed(range(len(outs))):
        hot = (cols[:, s : s + 1] == spots).astype(F32).astype(BF16)
        outs[s][...] = dot(hot, table).astype(BF16)


def pick(send_rows, coarse):
    _, count, slots = send_rows.shape
    width = coarse.shape[2]
    return pl.pallas_call(
        pick_kernel,
        out_shape=[jax.ShapeDtypeStruct((slots, width), BF16)] * count,
        in_specs=[pl.BlockSpec(memory_space=pl.ANY)] * 2,
        out_specs=[pl.BlockSpec(memory_space=VMEM)] * count,
        scratch_shapes=[
            VMEM(send_rows.shape, jnp.int32),
            VMEM(coarse.shape, BF16),
            pltpu.SemaphoreType.DMA((2,)),
        ],
        compiler_params=params(16),
        cost_estimate=cost(2 * count * slots * coarse.shape[1] * width, 2 * MIB),
        name="pick",
    )(send_rows, coarse)


def spread_kernel(tile, index_ref, weight_ref, nb_ref, head_in_ref, spread_ref, count_ref, head_ref):
    me = lax.axis_index("dom")
    rows, slots = spread_ref.shape
    span = count_ref.shape[2]
    part = 32
    head_ref[...] = jnp.zeros(head_ref.shape, BF16)
    head_ref[: head_in_ref.shape[0], :] = head_in_ref[...]
    zero, one = jnp.zeros((), BF16), jnp.ones((), BF16)
    spots = lax.broadcasted_iota(jnp.int16, (part, slots), 1)
    places = lax.broadcasted_iota(jnp.int16, (part, span), 1)

    def narrow(value):
        return columns(value.astype(F32)).astype(jnp.int32).astype(jnp.int16)

    def step(t, carry):
        start = pl.multiple_of(t * tile, tile)
        lanes = pl.ds(start, tile)
        index = narrow(index_ref[:, lanes] ^ (me * 128))
        weight = columns(weight_ref[:, lanes]).astype(BF16)
        near = narrow(nb_ref[:, lanes] - start)
        for r in range(0, tile, part):
            total = jnp.zeros((part, slots), BF16)
            for k in range(index_ref.shape[0]):
                total = total + jnp.where(index[r : r + part, k : k + 1] == spots, weight[r : r + part, k : k + 1], zero)
            spread_ref[pl.ds(pl.multiple_of(start + r, part), part), :] = total
            counts = jnp.zeros((part, span), BF16)
            for k in range(nb_ref.shape[0]):
                counts = counts + jnp.where(near[r : r + part, k : k + 1] == places, one, zero)
            count_ref[t, r : r + part, :] = counts
        return carry

    lax.fori_loop(0, rows // tile, step, 0)


def spread(up_index, up_weight, neighbors, head, slots, tile, padded):
    rows = up_index.shape[1]
    steps = rows // tile
    span = tile + 2 * RIM
    return pl.pallas_call(
        functools.partial(spread_kernel, tile),
        out_shape=[
            jax.ShapeDtypeStruct((rows, slots), BF16),
            jax.ShapeDtypeStruct((steps, tile, span), BF16),
            jax.ShapeDtypeStruct((padded, head.shape[1]), BF16),
        ],
        in_specs=[pl.BlockSpec(memory_space=VMEM)] * 4,
        out_specs=[pl.BlockSpec(memory_space=VMEM)] * 3,
        compiler_params=params(16),
        cost_estimate=cost(40 * rows * slots, 4 * rows * slots),
        name="spread",
    )(up_index, up_weight, neighbors, head)


def early_kernel(begin, end, tile, spread_ref, skip_ref, *refs):
    tables, out = refs[:-1], refs[-1]
    table = jnp.concatenate([r[...] for r in tables], axis=0)

    def step(t, carry):
        rows = pl.ds(pl.multiple_of(t * tile, tile), tile)
        out[rows, :] = skip_ref[rows, :].astype(F32) + dot(spread_ref[rows, begin:end], table)
        return carry

    lax.fori_loop(0, out.shape[0] // tile, step, 0)


def early(spread_rows, skip, begin, end, tables, tile):
    rows, width = skip.shape
    operands = (spread_rows, skip, *tables)
    return pl.pallas_call(
        functools.partial(early_kernel, begin, end, tile),
        out_shape=jax.ShapeDtypeStruct((rows, width), F32),
        in_specs=[pl.BlockSpec(memory_space=VMEM)] * len(operands),
        out_specs=pl.BlockSpec(memory_space=VMEM),
        compiler_params=params(16),
        cost_estimate=cost(2 * rows * (end - begin) * width, 8 * MIB),
        name="early",
    )(*operands)


def late_kernel(begin, end, tile, sum_ref, spread_ref, *refs):
    tables, (x_ref, inner_ref, outer_ref) = refs[:-3], refs[-3:]
    table = jnp.concatenate([r[...] for r in tables], axis=0)
    count = x_ref.shape[0]

    def step(t, carry):
        rows = pl.ds(pl.multiple_of(t * tile, tile), tile)
        x_ref[rows, :] = (sum_ref[rows, :] + dot(spread_ref[rows, begin:end], table)).astype(BF16)
        return carry

    lax.fori_loop(0, count // tile, step, 0)
    odd = lax.rem(lax.axis_index("dom"), 2) == 1
    first, last = x_ref[:RIM, :], x_ref[count - RIM :, :]
    inner_ref[...] = jnp.where(odd, first, last)
    outer_ref[...] = jnp.where(odd, last, first)


def late(sums, spread_rows, begin, end, tables, tile):
    rows, width = sums.shape
    operands = (sums, spread_rows, *tables)
    edge = jax.ShapeDtypeStruct((RIM, width), BF16)
    return pl.pallas_call(
        functools.partial(late_kernel, begin, end, tile),
        out_shape=[jax.ShapeDtypeStruct((rows, width), BF16), edge, edge],
        in_specs=[pl.BlockSpec(memory_space=VMEM)] * len(operands),
        out_specs=[pl.BlockSpec(memory_space=VMEM)] * 3,
        compiler_params=params(16),
        cost_estimate=cost(2 * rows * (end - begin) * width, 8 * MIB),
        name="late",
    )(*operands)


def tile_update(x, window, counts, w_in_ref, w_out_ref, gain_ref, head_ref):
    width = x.shape[1]
    agg = (dot(counts, window) * (1.0 / 6.0)).astype(BF16)
    pre = dot(x, w_in_ref[:width, :]) + dot(agg, w_in_ref[width:, :])
    act = (0.5 * pre * (1.0 + jnp.tanh(0.5 * pre))).astype(BF16)
    upd = dot(act, w_out_ref[...])
    mean = jnp.mean(upd, axis=1, keepdims=True)
    centred = upd - mean
    var = jnp.mean(centred * centred, axis=1, keepdims=True)
    h = (x.astype(F32) + centred * lax.rsqrt(var + 1e-05) * gain_ref[...]).astype(BF16)
    return h, dot_of(head_ref[...], h, 1, 1).astype(BF16)


def inner_kernel(x_ref, count_ref, w_in_ref, w_out_ref, gain_ref, head_ref, h_ref, pred_ref):
    tiles, tile, _ = count_ref.shape
    for t in range(1, tiles - 1):
        x = x_ref[t * tile : (t + 1) * tile, :]
        window = x_ref[t * tile - RIM : (t + 1) * tile + RIM, :]
        h, pred = tile_update(x, window, count_ref[t], w_in_ref, w_out_ref, gain_ref, head_ref)
        h_ref[(t - 1) * tile : t * tile, :] = h
        pred_ref[t - 1] = pred


def outer_kernel(members, x_ref, count_ref, w_in_ref, w_out_ref, gain_ref, head_ref, inner_ref, outer_ref, done_ref, h_ref, *refs):
    outs, all_ref = refs[:-1], refs[-1]
    tiles, tile, _ = count_ref.shape
    odd = lax.rem(lax.axis_index("dom"), 2) == 1
    inner, outer = inner_ref[...], outer_ref[...]
    before, after = jnp.where(odd, inner, outer), jnp.where(odd, outer, inner)
    rows = tiles * tile
    for place, t in enumerate((0, tiles - 1)):
        x = x_ref[t * tile : (t + 1) * tile, :]
        if t == 0:
            window = jnp.concatenate([before, x_ref[: tile + RIM, :]], axis=0)
        else:
            window = jnp.concatenate([x_ref[rows - tile - RIM :, :], after], axis=0)
        h, pred = tile_update(x, window, count_ref[t], w_in_ref, w_out_ref, gain_ref, head_ref)
        h_ref[place * tile : (place + 1) * tile, :] = h
        all_ref[t] = pred
    all_ref[1 : tiles - 1] = done_ref[...]
    me = lax.axis_index("mem")
    per = tiles // members
    for s, out in enumerate(outs):
        for k in range(per):
            out[:, k * tile : (k + 1) * tile] = all_ref[(me ^ s) * per + k]


def update_call(kernel, operands, out_shape, scratch, flops, name):
    return pl.pallas_call(
        kernel,
        out_shape=out_shape,
        in_specs=[pl.BlockSpec(memory_space=VMEM)] * len(operands),
        out_specs=[pl.BlockSpec(memory_space=VMEM)] * len(out_shape),
        scratch_shapes=scratch,
        compiler_params=params(24),
        cost_estimate=cost(flops, 8 * MIB),
        name=name,
    )(*operands)


def update(members, x, counts, w_in, w_out, gain, head, inner, outer):
    tiles, tile, _ = counts.shape
    width = x.shape[1]
    padded = head.shape[0]
    shared = (x, counts, w_in, w_out, gain, head)
    h_mid, pred_mid = update_call(
        inner_kernel,
        shared,
        [
            jax.ShapeDtypeStruct(((tiles - 2) * tile, width), BF16),
            jax.ShapeDtypeStruct((tiles - 2, padded, tile), BF16),
        ],
        [],
        (tiles - 2) * tile * width * width * 10,
        "inner",
    )
    h_end, *preds = update_call(
        functools.partial(outer_kernel, members),
        shared + (inner, outer, pred_mid),
        [jax.ShapeDtypeStruct((2 * tile, width), BF16)]
        + [jax.ShapeDtypeStruct((padded, tiles // members * tile), BF16)] * members,
        [VMEM((tiles, padded, tile), BF16)],
        2 * tile * width * width * 10,
        "outer",
    )
    return h_mid, h_end, preds


def score_kernel(members, live_ref, kw_ref, area_ref, target_ref, *refs):
    preds, outs, (kw_rows, target) = refs[:members], refs[members:-2], refs[-2:]
    num_vars = target_ref.shape[0]
    padded, piece = target.shape
    start = pl.multiple_of(lax.axis_index("mem") * piece, piece)
    lanes = pl.ds(start, piece)
    kw_rows[...] = jnp.ones(kw_rows.shape, F32)
    kw_rows[0:1, :num_vars] = kw_ref[...]
    width = kw_rows[...].T[:padded, 0:1]
    inv_sq = 1.0 / (width * width)
    target[...] = jnp.zeros(target.shape, F32)
    target[:num_vars, :] = target_ref[:, lanes].astype(F32)
    place = start + lax.broadcasted_iota(jnp.int32, (1, piece), 1)
    weight = jnp.where(place < live_ref[0], area_ref[:, lanes], 0.0)
    values = [r[...].astype(F32) for r in preds]
    sums = [jnp.zeros(v.shape, F32) for v in values]
    for i in range(members):
        for j in range(i + 1, members):
            phi = slope(values[i] - values[j], inv_sq)
            sums[i] = sums[i] + phi
            sums[j] = sums[j] - phi
    for i in range(members):
        total = sums[i] * (1.0 / members) - slope(values[i] - target[...], inv_sq)
        outs[i][...] = (weight * total).astype(BF16)


def score(live_counts, kernel_width, area, targets, preds):
    members = len(preds)
    shape = preds[0].shape
    return pl.pallas_call(
        functools.partial(score_kernel, members),
        out_shape=[jax.ShapeDtypeStruct(shape, BF16)] * members,
        in_specs=[pl.BlockSpec(memory_space=pltpu.SMEM)] + [pl.BlockSpec(memory_space=VMEM)] * (3 + members),
        out_specs=[pl.BlockSpec(memory_space=VMEM)] * members,
        scratch_shapes=[VMEM((8, 128), F32), VMEM(shape, F32)],
        compiler_params=params(16),
        cost_estimate=cost(10 * preds[0].size * members * members, MIB, preds[0].size * members * members),
        name="score",
    )(live_counts, kernel_width, area, targets, *preds)


def head_kernel(members, mid_ref, end_ref, *refs):
    scores, (out, all_ref) = refs[:-2], refs[-2:]
    tiles, _, tile = all_ref.shape
    me = lax.axis_index("mem")
    per = tiles // members
    for s in range(members):
        for k in range(per):
            all_ref[(me ^ s) * per + k] = scores[s][:, k * tile : (k + 1) * tile]
    total = dot(all_ref[0], end_ref[:tile, :]) + dot(all_ref[tiles - 1], end_ref[tile:, :])
    for t in range(1, tiles - 1):
        total = total + dot(all_ref[t], mid_ref[(t - 1) * tile : t * tile, :])
    out[...] = total.astype(BF16)


def head_terms(members, mid, end, scores):
    width = end.shape[1]
    tile = end.shape[0] // 2
    tiles = members * scores[0].shape[1] // tile
    padded = scores[0].shape[0]
    return pl.pallas_call(
        functools.partial(head_kernel, members),
        out_shape=[
            jax.ShapeDtypeStruct((padded, width), BF16),
            jax.ShapeDtypeStruct((tiles, padded, tile), BF16),
        ],
        in_specs=[pl.BlockSpec(memory_space=VMEM)] * (2 + members),
        out_specs=[pl.BlockSpec(memory_space=VMEM)] * 2,
        compiler_params=params(16),
        cost_estimate=cost(2 * padded * tiles * tile * width, 3 * MIB),
        name="head_terms",
    )(mid, end, *scores)


def latent_kernel(head_ref, score_ref, out):
    tile = score_ref.shape[2]
    for t in range(score_ref.shape[0]):
        out[0, t * tile : (t + 1) * tile, :] = dot_of(score_ref[t], head_ref[...], 0, 0).astype(BF16)


def latent_grad(head, scores):
    tiles, padded, tile = scores.shape
    width = head.shape[1]
    return pl.pallas_call(
        latent_kernel,
        out_shape=jax.ShapeDtypeStruct((1, tiles * tile, width), BF16),
        in_specs=[pl.BlockSpec(memory_space=VMEM)] * 2,
        out_specs=pl.BlockSpec(memory_space=VMEM),
        compiler_params=params(16),
        cost_estimate=cost(2 * scores.size * width, 3 * MIB),
        name="latent_grad",
    )(head, scores)


def total_kernel(scale, *refs):
    terms, out = refs[:-1], refs[-1]
    total = terms[0][...].astype(F32)
    for term in terms[1:]:
        total = total + term[...].astype(F32)
    out[0] = (total * scale)[: out.shape[1], :]


def head_total(terms, num_vars, scale):
    return pl.pallas_call(
        functools.partial(total_kernel, scale),
        out_shape=jax.ShapeDtypeStruct((1, num_vars, terms[0].shape[1]), F32),
        in_specs=[pl.BlockSpec(memory_space=VMEM)] * len(terms),
        out_specs=pl.BlockSpec(memory_space=VMEM),
        compiler_params=params(16),
        cost_estimate=cost(terms[0].size * len(terms), MIB),
        name="head_total",
    )(*terms)


def shards(
    coarse_latents,
    send_rows,
    up_index,
    up_weight,
    neighbors,
    live_counts,
    area,
    fine_skip,
    targets,
    kernel_width,
    w_in,
    w_out,
    ln_gain,
    w_head,
):
    dom_count = lax.axis_size("dom")
    members = lax.axis_size("mem")
    slots = send_rows.shape[2]
    rows, width = fine_skip.shape
    num_vars = w_head.shape[1]
    padded = num_vars + -num_vars % 16
    tile = min(256, rows // members)

    outgoing = pick(send_rows, coarse_latents)
    tables = [outgoing[0]] + [None] * (dom_count - 1)
    for s in range(1, dom_count):
        tables[s] = xor_permute(outgoing[s], "dom", s)

    spread_rows, counts, head = spread(
        up_index, up_weight, neighbors, w_head.T, dom_count * slots, tile, padded
    )
    split = dom_count - 2
    sums = early(spread_rows, fine_skip, 0, split * slots, tables[:split], tile)
    x, inner, outer = late(sums, spread_rows, split * slots, dom_count * slots, tables[split:], tile)
    inner = xor_permute(inner, "dom", 1)
    pairs = [(i, i + 1) for i in range(1, dom_count - 1, 2)]
    outer = lax.ppermute(outer, "dom", pairs + [(j, i) for i, j in pairs])

    mid, end, preds = update(members, x, counts, w_in, w_out, ln_gain[None, :], head, inner, outer)
    preds = [preds[0]] + [xor_permute(preds[s], "mem", s) for s in range(1, members)]
    scores = score(live_counts, kernel_width[None, :], area[None, :], targets, preds)
    scores = [scores[0]] + [xor_permute(scores[s], "mem", s) for s in range(1, members)]
    term, by_tile = head_terms(members, mid, end, scores)
    terms = [term] + [xor_permute(term, "mem", s) for s in range(1, members)]
    grad_latent = latent_grad(head, by_tile)
    scale = 1.0 / math.sqrt(members * rows)
    return (grad_latent, head_total(terms, num_vars, scale).transpose(0, 2, 1))


def solution(mesh):
    return jax.shard_map(
        shards,
        mesh=mesh,
        in_specs=(
            P("mem", "dom", None),
            P("dom", None, None),
            P(None, "dom"),
            P(None, "dom"),
            P(None, "dom"),
            P("dom"),
            P("dom"),
            P("dom", None),
            P(None, "dom"),
            P(),
            P(),
            P(),
            P(),
            P(),
        ),
        out_specs=(P("mem", "dom", None), P("dom", None, None)),
        check_vma=False,
    )
```

```python
import functools
import math

import jax
import jax.numpy as jnp
from jax import lax
from jax.experimental import pallas as pl
from jax.experimental.pallas import tpu as pltpu
from jax.sharding import PartitionSpec as P

RIM = 128
MIB = 1024 * 1024
F32 = jnp.float32
BF16 = jnp.bfloat16
VMEM = pltpu.VMEM


def dot(a, b):
    return jnp.dot(a, b, preferred_element_type=F32)


def dot_of(a, b, da, db):
    return lax.dot_general(a, b, (((da,), (db,)), ((), ())), preferred_element_type=F32)


def params(mib):
    return pltpu.CompilerParams(vmem_limit_bytes=mib * MIB)


def cost(flops, nbytes, trans=0):
    return pl.CostEstimate(flops=flops, bytes_accessed=nbytes, transcendentals=trans)


def columns(rows):
    pad = -rows.shape[0] % 8
    if pad:
        rows = jnp.concatenate([rows, jnp.zeros((pad, rows.shape[1]), rows.dtype)], axis=0)
    return rows.T


def in_hbm(*values):
    return [pltpu.with_memory_space_constraint(v, pltpu.HBM) for v in values]


def fetch(pairs, sems):
    copies = [pltpu.make_async_copy(src, dst, sems.at[i]) for i, (src, dst) in enumerate(pairs)]
    for copy in copies:
        copy.start()
    for copy in copies:
        copy.wait()


def slope(diff, inv_sq):
    return -(diff * inv_sq) * jnp.exp(-0.5 * diff * diff * inv_sq)


def xor_permute(value, axis, step):
    count = lax.axis_size(axis)
    return lax.ppermute(value, axis, [(i, i ^ step) for i in range(count)])


def picked(rows, table, outs):
    cols = columns(rows.astype(F32))
    spots = lax.broadcasted_iota(jnp.int32, (rows.shape[1], table.shape[0]), 1).astype(F32)
    hot = [(cols[:, k : k + 1] == spots).astype(F32).astype(BF16) for k in range(rows.shape[0])]
    found = dot(jnp.concatenate(hot, axis=0), table).astype(BF16)
    start = 0
    for out in outs:
        out[...] = found[start : start + out.shape[0], :]
        start += out.shape[0]


def send_rows_of(ref, steps):
    me = lax.axis_index("dom")
    return jnp.concatenate([ref[0, pl.ds(me ^ s, 1), :] for s in steps], axis=0)


def pick_kernel(steps, send_ref, coarse_ref, *refs):
    outs, (rows_ref, table_ref, sems) = refs[:-3], refs[-3:]
    fetch([(send_ref, rows_ref), (coarse_ref, table_ref)], sems)
    picked(send_rows_of(rows_ref, steps), table_ref[0], outs)


def pick(send_rows, coarse, groups):
    _, count, slots = send_rows.shape
    steps = [s for group in groups for s in group]
    width = coarse.shape[2]
    return pl.pallas_call(
        functools.partial(pick_kernel, steps),
        out_shape=[jax.ShapeDtypeStruct((len(group) * slots, width), BF16) for group in groups],
        in_specs=[pl.BlockSpec(memory_space=pltpu.HBM)] * 2,
        out_specs=[pl.BlockSpec(memory_space=VMEM)] * len(groups),
        scratch_shapes=[
            VMEM(send_rows.shape, jnp.int32),
            VMEM(coarse.shape, BF16),
            pltpu.SemaphoreType.DMA((2,)),
        ],
        compiler_params=params(16),
        cost_estimate=cost(2 * count * slots * coarse.shape[1] * width, 2 * MIB),
        name="pick",
    )(*in_hbm(send_rows, coarse))


def best_scale(weight):
    best = scale = jnp.ones((1, weight.shape[1]), F32)
    for c in range(16):
        factor = 1.0 + 0.0017 * c
        part = weight * (1.0 / factor)
        miss = part - part.astype(BF16).astype(F32)
        miss = miss * miss
        miss = miss[0:1] + miss[1:2] + miss[2:3]
        scale = jnp.where(miss < best, factor, scale)
        best = jnp.minimum(miss, best)
    return scale


def spread_kernel(tile, steps, *refs):
    sources, (first_ref, last_ref, scale_ref, count_ref, head_ref), held, sems = refs[:4], refs[5:10], refs[10:-1], refs[-1]
    fetch(list(zip(sources, held)), sems)
    index_ref, weight_ref, nb_ref, head_in_ref = held
    me = lax.axis_index("dom")
    rows, cut = first_ref.shape
    slots = cut + last_ref.shape[1]
    span = count_ref.shape[2]
    part = 32
    head_ref[...] = jnp.zeros(head_ref.shape, BF16)
    head_ref[: head_in_ref.shape[0], :] = head_in_ref[...]
    zero, one = jnp.zeros((), BF16), jnp.ones((), BF16)
    spots = lax.broadcasted_iota(jnp.int16, (part, slots), 1)
    places = lax.broadcasted_iota(jnp.int16, (part, span), 1)

    def narrow(value):
        return columns(value.astype(F32)).astype(jnp.int32).astype(jnp.int16)

    def step(t, carry):
        start = pl.multiple_of(t * tile, tile)
        lanes = pl.ds(start, tile)
        wanted = index_ref[:, lanes]
        step_of = lax.shift_right_logical(wanted, 7) ^ me
        place = jnp.zeros(wanted.shape, jnp.int32)
        for i, s in enumerate(steps):
            place = jnp.where(step_of == s, i * 128, place)
        found = place + (wanted & 127)
        i0, i1, i2 = found[0:1], found[1:2], found[2:3]
        w = weight_ref[:, lanes]
        w0, w1, w2 = w[0:1], w[1:2], w[2:3]
        same01, same02, same12 = i0 == i1, i0 == i2, (i1 == i2) & (i0 != i1)
        w0 = w0 + jnp.where(same01, w1, 0.0) + jnp.where(same02, w2, 0.0)
        w1 = jnp.where(same01, 0.0, w1 + jnp.where(same12, w2, 0.0))
        w2 = jnp.where(same02 | same12, 0.0, w2)
        i1 = jnp.where(same01, -1, i1)
        i2 = jnp.where(same02 | same12, -1, i2)
        index = narrow(jnp.concatenate([i0, i1, i2], axis=0))
        w = jnp.concatenate([w0, w1, w2], axis=0)
        scale = best_scale(w)
        scale_ref[:, lanes] = scale
        weight = columns(w / scale).astype(BF16)
        near = narrow(nb_ref[:, lanes] - start)
        for r in range(0, tile, part):
            here = slice(r, r + part)
            rows_here = pl.ds(pl.multiple_of(start + r, part), part)
            total = jnp.zeros((part, slots), BF16)
            for k in range(3):
                total = jnp.where(index[here, k : k + 1] == spots, weight[here, k : k + 1], total)
            first_ref[rows_here, :] = total[:, :cut]
            last_ref[rows_here, :] = total[:, cut:]
            counts = jnp.zeros((part, span), BF16)
            for k in range(nb_ref.shape[0]):
                counts = counts + jnp.where(near[here, k : k + 1] == places, one, zero)
            count_ref[t, here, :] = counts
        return carry

    lax.fori_loop(0, rows // tile, step, 0)


def spread(token, up_index, up_weight, neighbors, head, steps, slots, split, tile, padded):
    rows = up_index.shape[1]
    tiles = rows // tile
    span = tile + 2 * RIM
    cut, total = split * slots, len(steps) * slots
    return pl.pallas_call(
        functools.partial(spread_kernel, tile, steps),
        out_shape=[
            jax.ShapeDtypeStruct((rows, cut), BF16),
            jax.ShapeDtypeStruct((rows, total - cut), BF16),
            jax.ShapeDtypeStruct((1, rows), F32),
            jax.ShapeDtypeStruct((tiles, tile, span), BF16),
            jax.ShapeDtypeStruct((padded, head.shape[1]), BF16),
        ],
        in_specs=[pl.BlockSpec(memory_space=pltpu.HBM)] * 4 + [pl.BlockSpec(memory_space=VMEM)],
        out_specs=[pl.BlockSpec(memory_space=VMEM)] * 5,
        scratch_shapes=[VMEM(v.shape, v.dtype) for v in (up_index, up_weight, neighbors, head)]
        + [pltpu.SemaphoreType.DMA((4,))],
        compiler_params=params(16),
        cost_estimate=cost(1, 1),
        name="spread",
    )(*in_hbm(up_index, up_weight, neighbors, head), token)


def pack_kernel(other_ref, *refs):
    count = len(refs) // 2
    for i in range(count):
        mine, out = refs[i], refs[count + i]
        slots = mine.shape[0]
        out[:slots, :] = mine[...]
        out[slots:, :] = other_ref[(i + 1) * slots : (i + 2) * slots, :]


def pack(other, mine):
    slots, width = mine[0].shape
    return pl.pallas_call(
        pack_kernel,
        out_shape=[jax.ShapeDtypeStruct((2 * slots, width), BF16)] * len(mine),
        in_specs=[pl.BlockSpec(memory_space=VMEM)] * (1 + len(mine)),
        out_specs=[pl.BlockSpec(memory_space=VMEM)] * len(mine),
        compiler_params=params(16),
        cost_estimate=cost(1, 1),
        name="pack",
    )(other, *mine)


def early_kernel(tile, spread_ref, own_ref, one_ref, *refs):
    tables, out = refs[:-1], refs[-1]
    parts = [own_ref[...], one_ref[: own_ref.shape[0], :]] + [r[...] for r in tables]
    table = jnp.concatenate(parts, axis=0)

    def step(t, carry):
        rows = pl.ds(pl.multiple_of(t * tile, tile), tile)
        out[rows, :] = dot(spread_ref[rows, :], table)
        return carry

    lax.fori_loop(0, out.shape[0] // tile, step, 0, unroll=4)


def early(spread_rows, tables, tile):
    rows, width = spread_rows.shape[0], tables[0].shape[1]
    return pl.pallas_call(
        functools.partial(early_kernel, tile),
        out_shape=jax.ShapeDtypeStruct((rows, width), F32),
        in_specs=[pl.BlockSpec(memory_space=VMEM)] * (1 + len(tables)),
        out_specs=pl.BlockSpec(memory_space=VMEM),
        compiler_params=params(16),
        cost_estimate=cost(1, 1),
        name="early",
    )(spread_rows, *tables)


def late_kernel(tile, sum_ref, spread_ref, scale_ref, skip_ref, *refs):
    tables, (x_ref, inner_ref, outer_ref) = refs[:-3], refs[-3:]
    table = jnp.concatenate([r[...] for r in tables], axis=0)
    count = x_ref.shape[0]

    def step(t, carry):
        start = pl.multiple_of(t * tile, tile)
        rows = pl.ds(start, tile)
        scale = columns(scale_ref[:, rows])[:, 0:1]
        unpooled = scale * (sum_ref[rows, :] + dot(spread_ref[rows, :], table))
        x_ref[rows, :] = (skip_ref[rows, :].astype(F32) + unpooled).astype(BF16)
        return carry

    lax.fori_loop(0, count // tile, step, 0, unroll=4)
    odd = lax.rem(lax.axis_index("dom"), 2) == 1
    first, last = x_ref[:RIM, :], x_ref[count - RIM :, :]
    inner_ref[...] = jnp.where(odd, first, last)
    outer_ref[...] = jnp.where(odd, last, first)


def late(sums, spread_rows, scale, skip, tables, tile):
    rows, width = sums.shape
    operands = (sums, spread_rows, scale, skip, *tables)
    edge = jax.ShapeDtypeStruct((RIM, width), BF16)
    return pl.pallas_call(
        functools.partial(late_kernel, tile),
        out_shape=[jax.ShapeDtypeStruct((rows, width), BF16), edge, edge],
        in_specs=[pl.BlockSpec(memory_space=VMEM)] * len(operands),
        out_specs=[pl.BlockSpec(memory_space=VMEM)] * 3,
        compiler_params=params(16),
        cost_estimate=cost(2 * spread_rows.size * width, 8 * MIB),
        name="late",
    )(*operands)


def staged_update(x_ref, count_ref, w_in_ref, w_out_ref, gain_ref, head_ref, windows, places, agg_ref, act_ref, h_ref):
    tile = count_ref.shape[1]
    width = x_ref.shape[1]
    spans = [slice(i * tile, (i + 1) * tile) for i in range(len(places))]
    rows = [slice(t * tile, (t + 1) * tile) for t in places]
    for here, t, window in zip(spans, places, windows):
        agg_ref[here, :] = (dot(count_ref[t], window()) * (1.0 / 6.0)).astype(BF16)
    for here, there in zip(spans, rows):
        pre = dot(x_ref[there, :], w_in_ref[:width, :]) + dot(agg_ref[here, :], w_in_ref[width:, :])
        act_ref[here, :] = (0.5 * pre * (1.0 + jnp.tanh(0.5 * pre))).astype(BF16)
    for here, there in zip(spans, rows):
        upd = dot(act_ref[here, :], w_out_ref[...])
        mean = jnp.mean(upd, axis=1, keepdims=True)
        centred = upd - mean
        var = jnp.mean(centred * centred, axis=1, keepdims=True)
        change = centred * lax.rsqrt(var + 1e-05) * gain_ref[...]
        h_ref[here, :] = (x_ref[there, :].astype(F32) + change).astype(BF16)
    return [dot_of(head_ref[...], h_ref[here, :], 1, 1).astype(BF16) for here in spans]


def inner_kernel(x_ref, count_ref, w_in_ref, w_out_ref, gain_ref, head_ref, h_ref, pred_ref, agg_ref, act_ref):
    tiles, tile, _ = count_ref.shape
    places = range(1, tiles - 1)

    def window(t):
        return lambda: x_ref[t * tile - RIM : (t + 1) * tile + RIM, :]

    preds = staged_update(
        x_ref, count_ref, w_in_ref, w_out_ref, gain_ref, head_ref,
        [window(t) for t in places], places, agg_ref, act_ref, h_ref,
    )
    for i, pred in enumerate(preds):
        pred_ref[i] = pred


def outer_kernel(members, x_ref, count_ref, w_in_ref, w_out_ref, gain_ref, head_ref, inner_ref, outer_ref, done_ref, h_ref, *refs):
    outs, (all_ref, agg_ref, act_ref) = refs[:-3], refs[-3:]
    tiles, tile, _ = count_ref.shape
    odd = lax.rem(lax.axis_index("dom"), 2) == 1
    inner, outer = inner_ref[...], outer_ref[...]
    before, after = jnp.where(odd, inner, outer), jnp.where(odd, outer, inner)
    rows = tiles * tile
    windows = [
        lambda: jnp.concatenate([before, x_ref[: tile + RIM, :]], axis=0),
        lambda: jnp.concatenate([x_ref[rows - tile - RIM :, :], after], axis=0),
    ]
    preds = staged_update(
        x_ref, count_ref, w_in_ref, w_out_ref, gain_ref, head_ref,
        windows, (0, tiles - 1), agg_ref, act_ref, h_ref,
    )
    all_ref[0] = preds[0]
    all_ref[tiles - 1] = preds[1]
    all_ref[1 : tiles - 1] = done_ref[...]
    me = lax.axis_index("mem")
    per = tiles // members
    for s, out in enumerate(outs):
        for k in range(per):
            out[:, k * tile : (k + 1) * tile] = all_ref[(me ^ s) * per + k]


def update_call(kernel, operands, out_shape, scratch, flops, name):
    return pl.pallas_call(
        kernel,
        out_shape=out_shape,
        in_specs=[pl.BlockSpec(memory_space=VMEM)] * len(operands),
        out_specs=[pl.BlockSpec(memory_space=VMEM)] * len(out_shape),
        scratch_shapes=scratch,
        compiler_params=params(24),
        cost_estimate=cost(flops, 8 * MIB),
        name=name,
    )(*operands)


def update(members, x, counts, w_in, w_out, gain, head, inner, outer):
    tiles, tile, _ = counts.shape
    width = x.shape[1]
    padded = head.shape[0]
    shared = (x, counts, w_in, w_out, gain, head)
    h_mid, pred_mid = update_call(
        inner_kernel,
        shared,
        [
            jax.ShapeDtypeStruct(((tiles - 2) * tile, width), BF16),
            jax.ShapeDtypeStruct((tiles - 2, padded, tile), BF16),
        ],
        [VMEM(((tiles - 2) * tile, width), BF16)] * 2,
        (tiles - 2) * tile * width * width * 10,
        "inner",
    )
    h_end, *preds = update_call(
        functools.partial(outer_kernel, members),
        shared + (inner, outer, pred_mid),
        [jax.ShapeDtypeStruct((2 * tile, width), BF16)]
        + [jax.ShapeDtypeStruct((padded, tiles // members * tile), BF16)] * members,
        [VMEM((tiles, padded, tile), BF16)] + [VMEM((2 * tile, width), BF16)] * 2,
        2 * tile * width * width * 10,
        "outer",
    )
    return h_mid, h_end, preds


def score_kernel(members, live_ref, kw_ref, area_ref, target_ref, *refs):
    preds, outs, (kw_rows, target) = refs[:members], refs[members:-2], refs[-2:]
    num_vars = target_ref.shape[0]
    padded, piece = target.shape
    start = pl.multiple_of(lax.axis_index("mem") * piece, piece)
    lanes = pl.ds(start, piece)
    kw_rows[...] = jnp.ones(kw_rows.shape, F32)
    kw_rows[0:1, :num_vars] = kw_ref[...]
    width = kw_rows[...].T[:padded, 0:1]
    inv_sq = 1.0 / (width * width)
    target[...] = jnp.zeros(target.shape, F32)
    target[:num_vars, :] = target_ref[:, lanes].astype(F32)
    place = start + lax.broadcasted_iota(jnp.int32, (1, piece), 1)
    weight = jnp.where(place < live_ref[0], area_ref[:, lanes], 0.0)
    values = [r[...].astype(F32) for r in preds]
    sums = [jnp.zeros(v.shape, F32) for v in values]
    for i in range(members):
        for j in range(i + 1, members):
            phi = slope(values[i] - values[j], inv_sq)
            sums[i] = sums[i] + phi
            sums[j] = sums[j] - phi
    for i in range(members):
        total = sums[i] * (1.0 / members) - slope(values[i] - target[...], inv_sq)
        outs[i][...] = (weight * total).astype(BF16)


def score(live_counts, kernel_width, area, targets, preds):
    members = len(preds)
    shape = preds[0].shape
    return pl.pallas_call(
        functools.partial(score_kernel, members),
        out_shape=[jax.ShapeDtypeStruct(shape, BF16)] * members,
        in_specs=[pl.BlockSpec(memory_space=pltpu.SMEM)] + [pl.BlockSpec(memory_space=VMEM)] * (3 + members),
        out_specs=[pl.BlockSpec(memory_space=VMEM)] * members,
        scratch_shapes=[VMEM((8, 128), F32), VMEM(shape, F32)],
        compiler_params=params(16),
        cost_estimate=cost(10 * preds[0].size * members * members, MIB, preds[0].size * members * members),
        name="score",
    )(live_counts, kernel_width, area, targets, *preds)


def head_kernel(members, mid_ref, end_ref, *refs):
    scores, (out, all_ref) = refs[:-2], refs[-2:]
    tiles, _, tile = all_ref.shape
    me = lax.axis_index("mem")
    per = tiles // members
    for s in range(members):
        for k in range(per):
            all_ref[(me ^ s) * per + k] = scores[s][:, k * tile : (k + 1) * tile]
    total = dot(all_ref[0], end_ref[:tile, :]) + dot(all_ref[tiles - 1], end_ref[tile:, :])
    for t in range(1, tiles - 1):
        total = total + dot(all_ref[t], mid_ref[(t - 1) * tile : t * tile, :])
    out[...] = total.astype(BF16)


def head_terms(members, mid, end, scores):
    width = end.shape[1]
    tile = end.shape[0] // 2
    tiles = members * scores[0].shape[1] // tile
    padded = scores[0].shape[0]
    return pl.pallas_call(
        functools.partial(head_kernel, members),
        out_shape=[
            jax.ShapeDtypeStruct((padded, width), BF16),
            jax.ShapeDtypeStruct((tiles, padded, tile), BF16),
        ],
        in_specs=[pl.BlockSpec(memory_space=VMEM)] * (2 + members),
        out_specs=[pl.BlockSpec(memory_space=VMEM)] * 2,
        compiler_params=params(16),
        cost_estimate=cost(2 * padded * tiles * tile * width, 3 * MIB),
        name="head_terms",
    )(mid, end, *scores)


def latent_kernel(head_ref, score_ref, out):
    tile = score_ref.shape[2]
    for t in range(score_ref.shape[0]):
        out[0, t * tile : (t + 1) * tile, :] = dot_of(score_ref[t], head_ref[...], 0, 0).astype(BF16)


def latent_grad(head, scores):
    tiles, padded, tile = scores.shape
    width = head.shape[1]
    return pl.pallas_call(
        latent_kernel,
        out_shape=jax.ShapeDtypeStruct((1, tiles * tile, width), BF16),
        in_specs=[pl.BlockSpec(memory_space=VMEM)] * 2,
        out_specs=pl.BlockSpec(memory_space=VMEM),
        compiler_params=params(16),
        cost_estimate=cost(2 * scores.size * width, 3 * MIB),
        name="latent_grad",
    )(head, scores)


def total_kernel(scale, *refs):
    terms, out = refs[:-1], refs[-1]
    total = terms[0][...].astype(F32)
    for term in terms[1:]:
        total = total + term[...].astype(F32)
    out[:, 0, :] = (total * scale)[: out.shape[0], :]


def head_total(terms, num_vars, scale):
    return pl.pallas_call(
        functools.partial(total_kernel, scale),
        out_shape=jax.ShapeDtypeStruct((num_vars, 1, terms[0].shape[1]), F32),
        in_specs=[pl.BlockSpec(memory_space=VMEM)] * len(terms),
        out_specs=pl.BlockSpec(memory_space=VMEM),
        compiler_params=params(16),
        cost_estimate=cost(terms[0].size * len(terms), MIB),
        name="head_total",
    )(*terms)


def shards(
    coarse_latents,
    send_rows,
    up_index,
    up_weight,
    neighbors,
    live_counts,
    area,
    fine_skip,
    targets,
    kernel_width,
    w_in,
    w_out,
    ln_gain,
    w_head,
):
    dom_count = lax.axis_size("dom")
    members = lax.axis_size("mem")
    slots = send_rows.shape[2]
    rows, width = fine_skip.shape
    num_vars = w_head.shape[1]
    padded = num_vars + -num_vars % 8
    tile = min(256, rows // members)

    even = list(range(4, dom_count, 2))
    groups = [[0], [1] + [s + 1 for s in even], [2], [3]] + [[s] for s in even]
    steps = list(range(dom_count))
    own, one, two, three, *far = pick(send_rows, coarse_latents, groups)
    one = xor_permute(one, "dom", 1)
    far = [xor_permute(v, "dom", s) for v, s in zip(pack(one, far), even)]
    two, three = xor_permute(two, "dom", 2), xor_permute(three, "dom", 3)
    first_rows, last_rows, scale, counts, head = spread(
        own, up_index, up_weight, neighbors, w_head.T, steps, slots, 4, tile, padded
    )
    sums = early(first_rows, [own, one, two, three], tile)
    x, inner, outer = late(sums, last_rows, scale, fine_skip, far, tile)
    inner = xor_permute(inner, "dom", 1)
    pairs = [(i, i + 1) for i in range(1, dom_count - 1, 2)]
    outer = lax.ppermute(outer, "dom", pairs + [(j, i) for i, j in pairs])

    mid, end, preds = update(members, x, counts, w_in, w_out, ln_gain[None, :], head, inner, outer)
    preds = [preds[0]] + [xor_permute(preds[s], "mem", s) for s in range(1, members)]
    scores = score(live_counts, kernel_width[None, :], area[None, :], targets, preds)
    scores = [scores[0]] + [xor_permute(scores[s], "mem", s) for s in range(1, members)]
    term, by_tile = head_terms(members, mid, end, scores)
    terms = [term] + [xor_permute(term, "mem", s) for s in range(1, members)]
    grad_latent = latent_grad(head, by_tile)
    factor = 1.0 / math.sqrt(members * rows)
    return (grad_latent, head_total(terms, num_vars, factor).transpose(1, 2, 0))


def solution(mesh):
    return jax.shard_map(
        shards,
        mesh=mesh,
        in_specs=(
            P("mem", "dom", None),
            P("dom", None, None),
            P(None, "dom"),
            P(None, "dom"),
            P(None, "dom"),
            P("dom"),
            P("dom"),
            P("dom", None),
            P(None, "dom"),
            P(),
            P(),
            P(),
            P(),
            P(),
        ),
        out_specs=(P("mem", "dom", None), P("dom", None, None)),
        check_vma=False,
    )
```

```python
import functools
import math

import jax
import jax.numpy as jnp
from jax import lax
from jax.experimental import pallas as pl
from jax.experimental.pallas import tpu as pltpu
from jax.sharding import PartitionSpec as P

RIM = 128
MIB = 1024 * 1024
F32 = jnp.float32
BF16 = jnp.bfloat16
VMEM = pltpu.VMEM


def dot(a, b):
    return jnp.dot(a, b, preferred_element_type=F32)


def dot_of(a, b, da, db):
    return lax.dot_general(a, b, (((da,), (db,)), ((), ())), preferred_element_type=F32)


def params(mib):
    return pltpu.CompilerParams(vmem_limit_bytes=mib * MIB)


def cost(flops, nbytes, trans=0):
    return pl.CostEstimate(flops=flops, bytes_accessed=nbytes, transcendentals=trans)


def columns(rows):
    pad = -rows.shape[0] % 8
    if pad:
        rows = jnp.concatenate([rows, jnp.zeros((pad, rows.shape[1]), rows.dtype)], axis=0)
    return rows.T


def in_hbm(*values):
    return [pltpu.with_memory_space_constraint(v, pltpu.HBM) for v in values]


def fetch(pairs, sems):
    copies = [pltpu.make_async_copy(src, dst, sems.at[i]) for i, (src, dst) in enumerate(pairs)]
    for copy in copies:
        copy.start()
    for copy in copies:
        copy.wait()


def slope(diff, inv_sq):
    return -(diff * inv_sq) * jnp.exp(-0.5 * diff * diff * inv_sq)


def xor_permute(value, axis, step):
    count = lax.axis_size(axis)
    return lax.ppermute(value, axis, [(i, i ^ step) for i in range(count)])


def picked(rows, table, outs):
    cols = columns(rows.astype(F32))
    spots = lax.broadcasted_iota(jnp.int32, (rows.shape[1], table.shape[0]), 1).astype(F32)
    hot = [(cols[:, k : k + 1] == spots).astype(F32).astype(BF16) for k in range(rows.shape[0])]
    found = dot(jnp.concatenate(hot, axis=0), table).astype(BF16)
    start = 0
    for out in outs:
        out[...] = found[start : start + out.shape[0], :]
        start += out.shape[0]


def send_rows_of(ref, steps):
    me = lax.axis_index("dom")
    return jnp.concatenate([ref[0, pl.ds(me ^ s, 1), :] for s in steps], axis=0)


def first_pick_kernel(steps, send_ref, coarse_ref, out, rows_ref, table_ref, sems):
    fetch([(send_ref, rows_ref), (coarse_ref, table_ref)], sems)
    picked(send_rows_of(rows_ref, steps), table_ref[0], [out])


def first_pick(send_rows, coarse, steps):
    slots, width = send_rows.shape[2], coarse.shape[2]
    return pl.pallas_call(
        functools.partial(first_pick_kernel, steps),
        out_shape=[
            jax.ShapeDtypeStruct((len(steps) * slots, width), BF16),
            jax.ShapeDtypeStruct(send_rows.shape, jnp.int32),
            jax.ShapeDtypeStruct(coarse.shape, BF16),
        ],
        in_specs=[pl.BlockSpec(memory_space=pltpu.HBM)] * 2,
        out_specs=[pl.BlockSpec(memory_space=VMEM)] * 3,
        scratch_shapes=[pltpu.SemaphoreType.DMA((2,))],
        compiler_params=params(8),
        cost_estimate=cost(1, 1),
        name="pick_first",
    )(*in_hbm(send_rows, coarse))


def pick_kernel(steps, rows_ref, table_ref, *outs):
    picked(send_rows_of(rows_ref, steps), table_ref[0], outs)


def pick(rows, table, groups):
    slots, width = rows.shape[2], table.shape[2]
    steps = [s for group in groups for s in group]
    return pl.pallas_call(
        functools.partial(pick_kernel, steps),
        out_shape=[jax.ShapeDtypeStruct((len(group) * slots, width), BF16) for group in groups],
        in_specs=[pl.BlockSpec(memory_space=VMEM)] * 2,
        out_specs=[pl.BlockSpec(memory_space=VMEM)] * len(groups),
        compiler_params=params(8),
        cost_estimate=cost(1, 1),
        name="pick",
    )(rows, table)


def best_scale(weight, counted):
    best = scale = jnp.ones((1, weight.shape[1]), F32)
    for c in range(24):
        factor = 1.0 + 0.0017 * c
        part = weight * (1.0 / factor)
        miss = jnp.where(counted, part - part.astype(BF16).astype(F32), 0.0)
        miss = miss * miss
        miss = miss[0:1] + miss[1:2] + miss[2:3]
        scale = jnp.where(miss < best, factor, scale)
        best = jnp.minimum(miss, best)
    return scale


def spread_kernel(tile, steps, live_ref, *refs):
    sources, outs, scratch = refs[:7], refs[8:16], refs[16:]
    first_ref, last_ref, scale_ref, count_ref, head_ref, area_ref, inv_ref, target_ref = outs
    held, kw_rows, sems = scratch[:7], scratch[7], scratch[8]
    fetch(list(zip(sources, held)), sems)
    index_ref, weight_ref, nb_ref, head_in_ref, area_in_ref, target_in_ref, kw_ref = held
    padded, piece = target_ref.shape
    num_vars = target_in_ref.shape[0]
    start = pl.multiple_of(lax.axis_index("mem") * piece, piece)
    place = start + lax.broadcasted_iota(jnp.int32, (1, piece), 1)
    area_ref[...] = jnp.where(place < live_ref[0], area_in_ref[:, pl.ds(start, piece)], 0.0)
    kw_rows[...] = jnp.ones(kw_rows.shape, F32)
    kw_rows[0:1, :num_vars] = kw_ref[...]
    width = kw_rows[...].T[:padded, 0:1]
    inv_ref[...] = 1.0 / (width * width)
    target_ref[...] = jnp.zeros(target_ref.shape, F32)
    target_ref[:num_vars, :] = target_in_ref[:, pl.ds(start, piece)].astype(F32)
    me = lax.axis_index("dom")
    rows = first_ref.shape[0]
    cut = first_ref.shape[1] // 2
    slots = cut + last_ref.shape[1]
    span = count_ref.shape[2]
    part = 32
    head_ref[...] = jnp.zeros(head_ref.shape, BF16)
    head_ref[: head_in_ref.shape[0], :] = head_in_ref[...]
    zero, one = jnp.zeros((), BF16), jnp.ones((), BF16)
    spots = lax.broadcasted_iota(jnp.int16, (part, slots), 1)
    places = lax.broadcasted_iota(jnp.int16, (part, span), 1)

    def narrow(value):
        return columns(value.astype(F32)).astype(jnp.int32).astype(jnp.int16)

    def step(t, carry):
        start = pl.multiple_of(t * tile, tile)
        lanes = pl.ds(start, tile)
        wanted = index_ref[:, lanes]
        step_of = lax.shift_right_logical(wanted, 7) ^ me
        place = jnp.zeros(wanted.shape, jnp.int32)
        for i, s in enumerate(steps):
            place = jnp.where(step_of == s, i * 128, place)
        found = place + (wanted & 127)
        i0, i1, i2 = found[0:1], found[1:2], found[2:3]
        w = weight_ref[:, lanes]
        w0, w1, w2 = w[0:1], w[1:2], w[2:3]
        same01, same02, same12 = i0 == i1, i0 == i2, (i1 == i2) & (i0 != i1)
        w0 = w0 + jnp.where(same01, w1, 0.0) + jnp.where(same02, w2, 0.0)
        w1 = jnp.where(same01, 0.0, w1 + jnp.where(same12, w2, 0.0))
        w2 = jnp.where(same02 | same12, 0.0, w2)
        i1 = jnp.where(same01, -1, i1)
        i2 = jnp.where(same02 | same12, -1, i2)
        found = jnp.concatenate([i0, i1, i2], axis=0)
        w = jnp.concatenate([w0, w1, w2], axis=0)
        scale = best_scale(w, found >= cut)
        scale_ref[:, lanes] = scale
        index = narrow(found)
        weight = columns(w / scale)
        high = weight.astype(BF16)
        low = (weight - high.astype(F32)).astype(BF16)
        near = narrow(nb_ref[:, lanes] - start)
        for r in range(0, tile, part):
            here = slice(r, r + part)
            rows_here = pl.ds(pl.multiple_of(start + r, part), part)
            total = jnp.zeros((part, slots), BF16)
            rest = jnp.zeros((part, cut), BF16)
            for k in range(3):
                hit = index[here, k : k + 1] == spots
                total = jnp.where(hit, high[here, k : k + 1], total)
                rest = jnp.where(hit[:, :cut], low[here, k : k + 1], rest)
            first_ref[rows_here, :cut] = total[:, :cut]
            first_ref[rows_here, cut:] = rest
            last_ref[rows_here, :] = total[:, cut:]
            counts = jnp.zeros((part, span), BF16)
            for k in range(nb_ref.shape[0]):
                counts = counts + jnp.where(near[here, k : k + 1] == places, one, zero)
            count_ref[t, here, :] = counts
        return carry

    lax.fori_loop(0, rows // tile, step, 0)


def spread(token, live_counts, sources, steps, slots, split, tile, padded, piece):
    up_index, head = sources[0], sources[3]
    rows = up_index.shape[1]
    tiles = rows // tile
    span = tile + 2 * RIM
    cut, total = split * slots, len(steps) * slots
    return pl.pallas_call(
        functools.partial(spread_kernel, tile, steps),
        out_shape=[
            jax.ShapeDtypeStruct((rows, 2 * cut), BF16),
            jax.ShapeDtypeStruct((rows, total - cut), BF16),
            jax.ShapeDtypeStruct((1, rows), F32),
            jax.ShapeDtypeStruct((tiles, tile, span), BF16),
            jax.ShapeDtypeStruct((padded, head.shape[1]), BF16),
            jax.ShapeDtypeStruct((1, piece), F32),
            jax.ShapeDtypeStruct((padded, 1), F32),
            jax.ShapeDtypeStruct((padded, piece), F32),
        ],
        in_specs=[pl.BlockSpec(memory_space=pltpu.SMEM)]
        + [pl.BlockSpec(memory_space=pltpu.HBM)] * 7
        + [pl.BlockSpec(memory_space=VMEM)],
        out_specs=[pl.BlockSpec(memory_space=VMEM)] * 8,
        scratch_shapes=[VMEM(v.shape, v.dtype) for v in sources]
        + [VMEM((8, 128), F32), pltpu.SemaphoreType.DMA((7,))],
        compiler_params=params(16),
        cost_estimate=cost(1, 1),
        name="spread",
    )(live_counts, *in_hbm(*sources), token)


def pack_kernel(other_ref, *refs):
    count = len(refs) // 2
    for i in range(count):
        mine, out = refs[i], refs[count + i]
        slots = mine.shape[0]
        out[:slots, :] = mine[...]
        out[slots:, :] = other_ref[(i + 1) * slots : (i + 2) * slots, :]


def pack(other, mine):
    slots, width = mine[0].shape
    return pl.pallas_call(
        pack_kernel,
        out_shape=[jax.ShapeDtypeStruct((2 * slots, width), BF16)] * len(mine),
        in_specs=[pl.BlockSpec(memory_space=VMEM)] * (1 + len(mine)),
        out_specs=[pl.BlockSpec(memory_space=VMEM)] * len(mine),
        compiler_params=params(16),
        cost_estimate=cost(1, 1),
        name="pack",
    )(other, *mine)


def early_kernel(tile, spread_ref, own_ref, one_ref, *refs):
    tables, out = refs[:-1], refs[-1]
    parts = [own_ref[...], one_ref[: own_ref.shape[0], :]] + [r[...] for r in tables]
    table = jnp.concatenate(parts + parts, axis=0)

    def step(t, carry):
        rows = pl.ds(pl.multiple_of(t * tile, tile), tile)
        out[rows, :] = dot(spread_ref[rows, :], table)
        return carry

    lax.fori_loop(0, out.shape[0] // tile, step, 0, unroll=4)


def early(spread_rows, tables, tile):
    rows, width = spread_rows.shape[0], tables[0].shape[1]
    return pl.pallas_call(
        functools.partial(early_kernel, tile),
        out_shape=jax.ShapeDtypeStruct((rows, width), F32),
        in_specs=[pl.BlockSpec(memory_space=VMEM)] * (1 + len(tables)),
        out_specs=pl.BlockSpec(memory_space=VMEM),
        compiler_params=params(16),
        cost_estimate=cost(1, 1),
        name="early",
    )(spread_rows, *tables)


def late_kernel(tile, sum_ref, spread_ref, scale_ref, skip_ref, *refs):
    tables, (x_ref, inner_ref, outer_ref) = refs[:-3], refs[-3:]
    table = jnp.concatenate([r[...] for r in tables], axis=0)
    count = x_ref.shape[0]

    def step(t, carry):
        start = pl.multiple_of(t * tile, tile)
        rows = pl.ds(start, tile)
        scale = columns(scale_ref[:, rows])[:, 0:1]
        unpooled = scale * (sum_ref[rows, :] + dot(spread_ref[rows, :], table))
        x_ref[rows, :] = (skip_ref[rows, :].astype(F32) + unpooled).astype(BF16)
        return carry

    lax.fori_loop(0, count // tile, step, 0, unroll=4)
    odd = lax.rem(lax.axis_index("dom"), 2) == 1
    first, last = x_ref[:RIM, :], x_ref[count - RIM :, :]
    inner_ref[...] = jnp.where(odd, first, last)
    outer_ref[...] = jnp.where(odd, last, first)


def late(sums, spread_rows, scale, skip, tables, tile):
    rows, width = sums.shape
    operands = (sums, spread_rows, scale, skip, *tables)
    edge = jax.ShapeDtypeStruct((RIM, width), BF16)
    return pl.pallas_call(
        functools.partial(late_kernel, tile),
        out_shape=[jax.ShapeDtypeStruct((rows, width), BF16), edge, edge],
        in_specs=[pl.BlockSpec(memory_space=VMEM)] * len(operands),
        out_specs=[pl.BlockSpec(memory_space=VMEM)] * 3,
        compiler_params=params(16),
        cost_estimate=cost(2 * spread_rows.size * width, 8 * MIB),
        name="late",
    )(*operands)


def staged_update(x_ref, count_ref, w_in_ref, w_out_ref, gain_ref, head_ref, windows, places, agg_ref, act_ref, h_ref):
    tile = count_ref.shape[1]
    width = x_ref.shape[1]
    spans = [slice(i * tile, (i + 1) * tile) for i in range(len(places))]
    rows = [slice(t * tile, (t + 1) * tile) for t in places]
    for here, t, window in zip(spans, places, windows):
        agg_ref[here, :] = (dot(count_ref[t], window()) * (1.0 / 6.0)).astype(BF16)
    for here, there in zip(spans, rows):
        pre = dot(x_ref[there, :], w_in_ref[:width, :]) + dot(agg_ref[here, :], w_in_ref[width:, :])
        act_ref[here, :] = (0.5 * pre * (1.0 + jnp.tanh(0.5 * pre))).astype(BF16)
    for here, there in zip(spans, rows):
        upd = dot(act_ref[here, :], w_out_ref[...])
        mean = jnp.mean(upd, axis=1, keepdims=True)
        centred = upd - mean
        var = jnp.mean(centred * centred, axis=1, keepdims=True)
        change = centred * lax.rsqrt(var + 1e-05) * gain_ref[...]
        h_ref[here, :] = (x_ref[there, :].astype(F32) + change).astype(BF16)
    return [dot_of(head_ref[...], h_ref[here, :], 1, 1).astype(BF16) for here in spans]


def inner_kernel(x_ref, count_ref, w_in_ref, w_out_ref, gain_ref, head_ref, h_ref, pred_ref, agg_ref, act_ref):
    tiles, tile, _ = count_ref.shape
    places = range(1, tiles - 1)

    def window(t):
        return lambda: x_ref[t * tile - RIM : (t + 1) * tile + RIM, :]

    preds = staged_update(
        x_ref, count_ref, w_in_ref, w_out_ref, gain_ref, head_ref,
        [window(t) for t in places], places, agg_ref, act_ref, h_ref,
    )
    for i, pred in enumerate(preds):
        pred_ref[i] = pred


def outer_kernel(members, x_ref, count_ref, w_in_ref, w_out_ref, gain_ref, head_ref, inner_ref, outer_ref, done_ref, h_ref, *refs):
    outs, (all_ref, agg_ref, act_ref) = refs[:-3], refs[-3:]
    tiles, tile, _ = count_ref.shape
    odd = lax.rem(lax.axis_index("dom"), 2) == 1
    inner, outer = inner_ref[...], outer_ref[...]
    before, after = jnp.where(odd, inner, outer), jnp.where(odd, outer, inner)
    rows = tiles * tile
    windows = [
        lambda: jnp.concatenate([before, x_ref[: tile + RIM, :]], axis=0),
        lambda: jnp.concatenate([x_ref[rows - tile - RIM :, :], after], axis=0),
    ]
    preds = staged_update(
        x_ref, count_ref, w_in_ref, w_out_ref, gain_ref, head_ref,
        windows, (0, tiles - 1), agg_ref, act_ref, h_ref,
    )
    all_ref[0] = preds[0]
    all_ref[tiles - 1] = preds[1]
    all_ref[1 : tiles - 1] = done_ref[...]
    me = lax.axis_index("mem")
    per = tiles // members
    for s, out in enumerate(outs):
        for k in range(per):
            out[:, k * tile : (k + 1) * tile] = all_ref[(me ^ s) * per + k]


def update_call(kernel, operands, out_shape, scratch, flops, name):
    return pl.pallas_call(
        kernel,
        out_shape=out_shape,
        in_specs=[pl.BlockSpec(memory_space=VMEM)] * len(operands),
        out_specs=[pl.BlockSpec(memory_space=VMEM)] * len(out_shape),
        scratch_shapes=scratch,
        compiler_params=params(24),
        cost_estimate=cost(flops, 8 * MIB),
        name=name,
    )(*operands)


def update(members, x, counts, w_in, w_out, gain, head, inner, outer):
    tiles, tile, _ = counts.shape
    width = x.shape[1]
    padded = head.shape[0]
    shared = (x, counts, w_in, w_out, gain, head)
    h_mid, pred_mid = update_call(
        inner_kernel,
        shared,
        [
            jax.ShapeDtypeStruct(((tiles - 2) * tile, width), BF16),
            jax.ShapeDtypeStruct((tiles - 2, padded, tile), BF16),
        ],
        [VMEM(((tiles - 2) * tile, width), BF16)] * 2,
        (tiles - 2) * tile * width * width * 10,
        "inner",
    )
    h_end, *preds = update_call(
        functools.partial(outer_kernel, members),
        shared + (inner, outer, pred_mid),
        [jax.ShapeDtypeStruct((2 * tile, width), BF16)]
        + [jax.ShapeDtypeStruct((padded, tiles // members * tile), BF16)] * members,
        [VMEM((tiles, padded, tile), BF16)] + [VMEM((2 * tile, width), BF16)] * 2,
        2 * tile * width * width * 10,
        "outer",
    )
    return h_mid, h_end, preds


def score_kernel(members, weight_ref, inv_ref, target_ref, *refs):
    preds, outs = refs[:members], refs[members:]
    inv_sq, weight = inv_ref[...], weight_ref[...]
    values = [r[...].astype(F32) for r in preds]
    sums = [jnp.zeros(v.shape, F32) for v in values]
    for i in range(members):
        for j in range(i + 1, members):
            phi = slope(values[i] - values[j], inv_sq)
            sums[i] = sums[i] + phi
            sums[j] = sums[j] - phi
    for i in range(members):
        total = sums[i] * (1.0 / members) - slope(values[i] - target_ref[...], inv_sq)
        outs[i][...] = (weight * total).astype(BF16)


def score(weight, inv_sq, target, preds):
    members = len(preds)
    shape = preds[0].shape
    return pl.pallas_call(
        functools.partial(score_kernel, members),
        out_shape=[jax.ShapeDtypeStruct(shape, BF16)] * members,
        in_specs=[pl.BlockSpec(memory_space=VMEM)] * (3 + members),
        out_specs=[pl.BlockSpec(memory_space=VMEM)] * members,
        compiler_params=params(16),
        cost_estimate=cost(10 * preds[0].size * members * members, MIB, preds[0].size * members * members),
        name="score",
    )(weight, inv_sq, target, *preds)


def head_kernel(members, mid_ref, end_ref, *refs):
    scores, (out, all_ref) = refs[:-2], refs[-2:]
    tiles, _, tile = all_ref.shape
    me = lax.axis_index("mem")
    per = tiles // members
    for s in range(members):
        for k in range(per):
            all_ref[(me ^ s) * per + k] = scores[s][:, k * tile : (k + 1) * tile]
    total = dot(all_ref[0], end_ref[:tile, :]) + dot(all_ref[tiles - 1], end_ref[tile:, :])
    for t in range(1, tiles - 1):
        total = total + dot(all_ref[t], mid_ref[(t - 1) * tile : t * tile, :])
    out[...] = total.astype(BF16)


def head_terms(members, mid, end, scores):
    width = end.shape[1]
    tile = end.shape[0] // 2
    tiles = members * scores[0].shape[1] // tile
    padded = scores[0].shape[0]
    return pl.pallas_call(
        functools.partial(head_kernel, members),
        out_shape=[
            jax.ShapeDtypeStruct((padded, width), BF16),
            jax.ShapeDtypeStruct((tiles, padded, tile), BF16),
        ],
        in_specs=[pl.BlockSpec(memory_space=VMEM)] * (2 + members),
        out_specs=[pl.BlockSpec(memory_space=VMEM)] * 2,
        compiler_params=params(16),
        cost_estimate=cost(2 * padded * tiles * tile * width, 3 * MIB),
        name="head_terms",
    )(mid, end, *scores)


def latent_kernel(head_ref, score_ref, out):
    tile = score_ref.shape[2]
    for t in range(score_ref.shape[0]):
        out[0, t * tile : (t + 1) * tile, :] = dot_of(score_ref[t], head_ref[...], 0, 0).astype(BF16)


def latent_grad(head, scores):
    tiles, padded, tile = scores.shape
    width = head.shape[1]
    return pl.pallas_call(
        latent_kernel,
        out_shape=jax.ShapeDtypeStruct((1, tiles * tile, width), BF16),
        in_specs=[pl.BlockSpec(memory_space=VMEM)] * 2,
        out_specs=pl.BlockSpec(memory_space=VMEM),
        compiler_params=params(16),
        cost_estimate=cost(2 * scores.size * width, 3 * MIB),
        name="latent_grad",
    )(head, scores)


def total_kernel(scale, *refs):
    terms, out = refs[:-1], refs[-1]
    total = terms[0][...].astype(F32)
    for term in terms[1:]:
        total = total + term[...].astype(F32)
    out[:, 0, :] = (total * scale)[: out.shape[0], :]


def head_total(terms, num_vars, scale):
    return pl.pallas_call(
        functools.partial(total_kernel, scale),
        out_shape=jax.ShapeDtypeStruct((num_vars, 1, terms[0].shape[1]), F32),
        in_specs=[pl.BlockSpec(memory_space=VMEM)] * len(terms),
        out_specs=pl.BlockSpec(memory_space=VMEM),
        compiler_params=params(16),
        cost_estimate=cost(terms[0].size * len(terms), MIB),
        name="head_total",
    )(*terms)


def shards(
    coarse_latents,
    send_rows,
    up_index,
    up_weight,
    neighbors,
    live_counts,
    area,
    fine_skip,
    targets,
    kernel_width,
    w_in,
    w_out,
    ln_gain,
    w_head,
):
    dom_count = lax.axis_size("dom")
    members = lax.axis_size("mem")
    slots = send_rows.shape[2]
    rows, width = fine_skip.shape
    num_vars = w_head.shape[1]
    padded = num_vars + -num_vars % 8
    tile = min(256, rows // members)

    even = list(range(4, dom_count, 2))
    steps = list(range(dom_count))
    one, sent, table = first_pick(send_rows, coarse_latents, [1] + [s + 1 for s in even])
    one = xor_permute(one, "dom", 1)
    own, two, three, *far = pick(sent, table, [[0], [2], [3]] + [[s] for s in even])
    far = [xor_permute(v, "dom", s) for v, s in zip(pack(one, far), even)]
    two, three = xor_permute(two, "dom", 2), xor_permute(three, "dom", 3)
    sources = (up_index, up_weight, neighbors, w_head.T, area[None, :], targets, kernel_width[None, :])
    first_rows, last_rows, scale, counts, head, weight, inv_sq, target = spread(
        own, live_counts, sources, steps, slots, 4, tile, padded, rows // members
    )
    sums = early(first_rows, [own, one, two, three], tile)
    x, inner, outer = late(sums, last_rows, scale, fine_skip, far, tile)
    inner = xor_permute(inner, "dom", 1)
    pairs = [(i, i + 1) for i in range(1, dom_count - 1, 2)]
    outer = lax.ppermute(outer, "dom", pairs + [(j, i) for i, j in pairs])

    mid, end, preds = update(members, x, counts, w_in, w_out, ln_gain[None, :], head, inner, outer)
    preds = [preds[0]] + [xor_permute(preds[s], "mem", s) for s in range(1, members)]
    scores = score(weight, inv_sq, target, preds)
    scores = [scores[0]] + [xor_permute(scores[s], "mem", s) for s in range(1, members)]
    term, by_tile = head_terms(members, mid, end, scores)
    terms = [term] + [xor_permute(term, "mem", s) for s in range(1, members)]
    grad_latent = latent_grad(head, by_tile)
    factor = 1.0 / math.sqrt(members * rows)
    return (grad_latent, head_total(terms, num_vars, factor).transpose(1, 2, 0))


def solution(mesh):
    return jax.shard_map(
        shards,
        mesh=mesh,
        in_specs=(
            P("mem", "dom", None),
            P("dom", None, None),
            P(None, "dom"),
            P(None, "dom"),
            P(None, "dom"),
            P("dom"),
            P("dom"),
            P("dom", None),
            P(None, "dom"),
            P(),
            P(),
            P(),
            P(),
            P(),
        ),
        out_specs=(P("mem", "dom", None), P("dom", None, None)),
        check_vma=False,
    )
```

```python
import functools
import math

import jax
import jax.numpy as jnp
from jax import lax
from jax.experimental import pallas as pl
from jax.experimental.pallas import tpu as pltpu
from jax.sharding import PartitionSpec as P

RIM = 128
MIB = 1024 * 1024
F32 = jnp.float32
BF16 = jnp.bfloat16
VMEM = pltpu.VMEM


def dot(a, b):
    return jnp.dot(a, b, preferred_element_type=F32)


def dot_of(a, b, da, db):
    return lax.dot_general(a, b, (((da,), (db,)), ((), ())), preferred_element_type=F32)


def params(mib):
    return pltpu.CompilerParams(vmem_limit_bytes=mib * MIB)


def cost(flops, nbytes, trans=0):
    return pl.CostEstimate(flops=flops, bytes_accessed=nbytes, transcendentals=trans)


def columns(rows):
    pad = -rows.shape[0] % 8
    if pad:
        rows = jnp.concatenate([rows, jnp.zeros((pad, rows.shape[1]), rows.dtype)], axis=0)
    return rows.T


def in_hbm(*values):
    return [pltpu.with_memory_space_constraint(v, pltpu.HBM) for v in values]


def fetch(pairs, sems):
    copies = [pltpu.make_async_copy(src, dst, sems.at[i]) for i, (src, dst) in enumerate(pairs)]
    for copy in copies:
        copy.start()
    for copy in copies:
        copy.wait()


def slope(diff, inv_width):
    ratio = diff * inv_width
    return ratio * jnp.exp(ratio * ratio * -0.5)


def xor_permute(value, axis, step):
    count = lax.axis_size(axis)
    return lax.ppermute(value, axis, [(i, i ^ step) for i in range(count)])


def mem_trade(steps, values):
    return [v if s == 0 else xor_permute(v, "mem", s) for s, v in zip(steps, values)]


def mem_steps(members):
    return [0] + list(range(members - 1, 0, -1))


def one_hot(rows, length):
    cols = columns(rows.astype(F32))
    spots = lax.broadcasted_iota(jnp.int32, (rows.shape[1], length), 1).astype(F32)
    hot = [(cols[:, k : k + 1] == spots).astype(F32).astype(BF16) for k in range(rows.shape[0])]
    return jnp.concatenate(hot, axis=0)


def picked(rows, table, outs):
    found = dot(one_hot(rows, table.shape[0]), table).astype(BF16)
    start = 0
    for out in outs:
        out[...] = found[start : start + out.shape[0], :]
        start += out.shape[0]


def send_rows_of(ref, steps):
    me = lax.axis_index("dom")
    return jnp.concatenate([ref[0, pl.ds(me ^ s, 1), :] for s in steps], axis=0)


def first_pick_kernel(steps, send_ref, coarse_ref, out, rows_ref, table_ref, sems):
    rows_copy = pltpu.make_async_copy(send_ref, rows_ref, sems.at[0])
    table_copy = pltpu.make_async_copy(coarse_ref, table_ref, sems.at[1])
    rows_copy.start()
    table_copy.start()
    rows_copy.wait()
    hot = one_hot(send_rows_of(rows_ref, steps), table_ref.shape[1])
    table_copy.wait()
    out[...] = dot(hot, table_ref[0]).astype(BF16)


def first_pick(send_rows, coarse, steps):
    slots, width = send_rows.shape[2], coarse.shape[2]
    return pl.pallas_call(
        functools.partial(first_pick_kernel, steps),
        out_shape=[
            jax.ShapeDtypeStruct((len(steps) * slots, width), BF16),
            jax.ShapeDtypeStruct(send_rows.shape, jnp.int32),
            jax.ShapeDtypeStruct(coarse.shape, BF16),
        ],
        in_specs=[pl.BlockSpec(memory_space=pltpu.HBM)] * 2,
        out_specs=[pl.BlockSpec(memory_space=VMEM)] * 3,
        scratch_shapes=[pltpu.SemaphoreType.DMA((2,))],
        compiler_params=params(8),
        cost_estimate=cost(1, 1),
        name="pick_first",
    )(*in_hbm(send_rows, coarse))


def pick_kernel(steps, rows_ref, table_ref, *outs):
    picked(send_rows_of(rows_ref, steps), table_ref[0], outs)


def pick(rows, table, groups):
    slots, width = rows.shape[2], table.shape[2]
    steps = [s for group in groups for s in group]
    return pl.pallas_call(
        functools.partial(pick_kernel, steps),
        out_shape=[jax.ShapeDtypeStruct((len(group) * slots, width), BF16) for group in groups],
        in_specs=[pl.BlockSpec(memory_space=VMEM)] * 2,
        out_specs=[pl.BlockSpec(memory_space=VMEM)] * len(groups),
        compiler_params=params(8),
        cost_estimate=cost(1, 1),
        name="pick",
    )(rows, table)


def best_scale(weight, counted):
    best = scale = jnp.ones((1, weight.shape[1]), F32)
    for c in range(24):
        factor = 1.0 + 0.0017 * c
        part = weight * (1.0 / factor)
        miss = jnp.where(counted, part - part.astype(BF16).astype(F32), 0.0)
        miss = miss * miss
        miss = miss[0:1] + miss[1:2] + miss[2:3]
        scale = jnp.where(miss < best, factor, scale)
        best = jnp.minimum(miss, best)
    return scale


def spread_kernel(tile, steps, live_ref, *refs):
    sources, outs, scratch = refs[:7], refs[8:16], refs[16:]
    first_ref, last_ref, scale_ref, count_ref, head_ref, area_ref, inv_ref, target_ref = outs
    held, kw_rows, sems = scratch[:7], scratch[7], scratch[8]
    fetch(list(zip(sources, held)), sems)
    index_ref, weight_ref, nb_ref, head_in_ref, area_in_ref, target_in_ref, kw_ref = held
    padded, piece = target_ref.shape
    num_vars = target_in_ref.shape[0]
    start = pl.multiple_of(lax.axis_index("mem") * piece, piece)
    place = start + lax.broadcasted_iota(jnp.int32, (1, piece), 1)
    area_ref[...] = jnp.where(place < live_ref[0], area_in_ref[:, pl.ds(start, piece)], 0.0)
    kw_rows[...] = jnp.ones(kw_rows.shape, F32)
    kw_rows[0:1, :num_vars] = kw_ref[...]
    width = kw_rows[...].T[:padded, 0:1]
    inv_ref[...] = 1.0 / width
    target_ref[...] = jnp.zeros(target_ref.shape, F32)
    target_ref[:num_vars, :] = target_in_ref[:, pl.ds(start, piece)].astype(F32)
    me = lax.axis_index("dom")
    rows = first_ref.shape[0]
    cut = first_ref.shape[1] // 2
    slots = cut + last_ref.shape[1]
    span = count_ref.shape[2]
    part = 32
    head_ref[...] = jnp.zeros(head_ref.shape, BF16)
    head_ref[: head_in_ref.shape[0], :] = head_in_ref[...]
    zero, one = jnp.zeros((), BF16), jnp.ones((), BF16)
    spots = lax.broadcasted_iota(jnp.int16, (part, slots), 1)
    places = lax.broadcasted_iota(jnp.int16, (part, span), 1)

    def narrow(value):
        return columns(value.astype(F32)).astype(jnp.int32).astype(jnp.int16)

    def step(t, carry):
        start = pl.multiple_of(t * tile, tile)
        lanes = pl.ds(start, tile)
        wanted = index_ref[:, lanes]
        step_of = lax.shift_right_logical(wanted, 7) ^ me
        place = jnp.zeros(wanted.shape, jnp.int32)
        for i, s in enumerate(steps):
            place = jnp.where(step_of == s, i * 128, place)
        found = place + (wanted & 127)
        i0, i1, i2 = found[0:1], found[1:2], found[2:3]
        w = weight_ref[:, lanes]
        w0, w1, w2 = w[0:1], w[1:2], w[2:3]
        same01, same02, same12 = i0 == i1, i0 == i2, (i1 == i2) & (i0 != i1)
        w0 = w0 + jnp.where(same01, w1, 0.0) + jnp.where(same02, w2, 0.0)
        w1 = jnp.where(same01, 0.0, w1 + jnp.where(same12, w2, 0.0))
        w2 = jnp.where(same02 | same12, 0.0, w2)
        i1 = jnp.where(same01, -1, i1)
        i2 = jnp.where(same02 | same12, -1, i2)
        found = jnp.concatenate([i0, i1, i2], axis=0)
        w = jnp.concatenate([w0, w1, w2], axis=0)
        scale = best_scale(w, found >= cut)
        scale_ref[:, lanes] = scale
        index = narrow(found)
        weight = columns(w / scale)
        high = weight.astype(BF16)
        low = (weight - high.astype(F32)).astype(BF16)
        near = narrow(nb_ref[:, lanes] - start)
        for r in range(0, tile, part):
            here = slice(r, r + part)
            rows_here = pl.ds(pl.multiple_of(start + r, part), part)
            total = jnp.zeros((part, slots), BF16)
            rest = jnp.zeros((part, cut), BF16)
            for k in range(3):
                hit = index[here, k : k + 1] == spots
                total = jnp.where(hit, high[here, k : k + 1], total)
                rest = jnp.where(hit[:, :cut], low[here, k : k + 1], rest)
            first_ref[rows_here, :cut] = total[:, :cut]
            first_ref[rows_here, cut:] = rest
            last_ref[rows_here, :] = total[:, cut:]
            counts = jnp.zeros((part, span), BF16)
            for k in range(nb_ref.shape[0]):
                counts = counts + jnp.where(near[here, k : k + 1] == places, one, zero)
            count_ref[t, here, :] = counts
        return carry

    lax.fori_loop(0, rows // tile, step, 0)


def spread(token, live_counts, sources, steps, slots, split, tile, padded, piece):
    up_index, head = sources[0], sources[3]
    rows = up_index.shape[1]
    tiles = rows // tile
    span = tile + 2 * RIM
    cut, total = split * slots, len(steps) * slots
    return pl.pallas_call(
        functools.partial(spread_kernel, tile, steps),
        out_shape=[
            jax.ShapeDtypeStruct((rows, 2 * cut), BF16),
            jax.ShapeDtypeStruct((rows, total - cut), BF16),
            jax.ShapeDtypeStruct((1, rows), F32),
            jax.ShapeDtypeStruct((tiles, tile, span), BF16),
            jax.ShapeDtypeStruct((padded, head.shape[1]), BF16),
            jax.ShapeDtypeStruct((1, piece), F32),
            jax.ShapeDtypeStruct((padded, 1), F32),
            jax.ShapeDtypeStruct((padded, piece), F32),
        ],
        in_specs=[pl.BlockSpec(memory_space=pltpu.SMEM)]
        + [pl.BlockSpec(memory_space=pltpu.HBM)] * 7
        + [pl.BlockSpec(memory_space=VMEM)],
        out_specs=[pl.BlockSpec(memory_space=VMEM)] * 8,
        scratch_shapes=[VMEM(v.shape, v.dtype) for v in sources]
        + [VMEM((8, 128), F32), pltpu.SemaphoreType.DMA((7,))],
        compiler_params=params(16),
        cost_estimate=cost(1, 1),
        name="spread",
    )(live_counts, *in_hbm(*sources), token)


def pack_kernel(other_ref, *refs):
    count = len(refs) // 2
    for i in range(count):
        mine, out = refs[i], refs[count + i]
        slots = mine.shape[0]
        out[:slots, :] = mine[...]
        out[slots:, :] = other_ref[(i + 1) * slots : (i + 2) * slots, :]


def pack(other, mine):
    slots, width = mine[0].shape
    return pl.pallas_call(
        pack_kernel,
        out_shape=[jax.ShapeDtypeStruct((2 * slots, width), BF16)] * len(mine),
        in_specs=[pl.BlockSpec(memory_space=VMEM)] * (1 + len(mine)),
        out_specs=[pl.BlockSpec(memory_space=VMEM)] * len(mine),
        compiler_params=params(16),
        cost_estimate=cost(1, 1),
        name="pack",
    )(other, *mine)


def early_kernel(tile, spread_ref, scale_ref, skip_ref, own_ref, one_ref, *refs):
    tables, out = refs[:-1], refs[-1]
    parts = [own_ref[...], one_ref[: own_ref.shape[0], :]] + [r[...] for r in tables]
    table = jnp.concatenate(parts + parts, axis=0)

    def step(t, carry):
        start = pl.multiple_of(t * tile, tile)
        rows = pl.ds(start, tile)
        scale = columns(scale_ref[:, rows])[:, 0:1]
        out[rows, :] = skip_ref[rows, :].astype(F32) + scale * dot(spread_ref[rows, :], table)
        return carry

    lax.fori_loop(0, out.shape[0] // tile, step, 0, unroll=4)


def early(spread_rows, scale, skip, tables, tile):
    return pl.pallas_call(
        functools.partial(early_kernel, tile),
        out_shape=jax.ShapeDtypeStruct(skip.shape, F32),
        in_specs=[pl.BlockSpec(memory_space=VMEM)] * (3 + len(tables)),
        out_specs=pl.BlockSpec(memory_space=VMEM),
        compiler_params=params(16),
        cost_estimate=cost(1, 1),
        name="early",
    )(spread_rows, scale, skip, *tables)


def late_kernel(tile, sum_ref, spread_ref, scale_ref, *refs):
    tables, (x_ref, inner_ref, outer_ref) = refs[:-3], refs[-3:]
    table = jnp.concatenate([r[...] for r in tables], axis=0)
    count = x_ref.shape[0]

    def step(t, carry):
        start = pl.multiple_of(t * tile, tile)
        rows = pl.ds(start, tile)
        scale = columns(scale_ref[:, rows])[:, 0:1]
        x_ref[rows, :] = (sum_ref[rows, :] + scale * dot(spread_ref[rows, :], table)).astype(BF16)
        return carry

    lax.fori_loop(0, count // tile, step, 0, unroll=count // tile)
    odd = lax.rem(lax.axis_index("dom"), 2) == 1
    first, last = x_ref[:RIM, :], x_ref[count - RIM :, :]
    inner_ref[...] = jnp.where(odd, first, last)
    outer_ref[...] = jnp.where(odd, last, first)


def late(sums, spread_rows, scale, tables, tile):
    rows, width = sums.shape
    operands = (sums, spread_rows, scale, *tables)
    edge = jax.ShapeDtypeStruct((RIM, width), BF16)
    return pl.pallas_call(
        functools.partial(late_kernel, tile),
        out_shape=[jax.ShapeDtypeStruct((rows, width), BF16), edge, edge],
        in_specs=[pl.BlockSpec(memory_space=VMEM)] * len(operands),
        out_specs=[pl.BlockSpec(memory_space=VMEM)] * 3,
        compiler_params=params(16),
        cost_estimate=cost(2 * spread_rows.size * width, 8 * MIB),
        name="late",
    )(*operands)


def staged_update(x_ref, count_ref, w_in_ref, w_out_ref, gain_ref, head_ref, windows, places, agg_ref, act_ref, h_ref):
    tile = count_ref.shape[1]
    width = x_ref.shape[1]
    spans = [slice(i * tile, (i + 1) * tile) for i in range(len(places))]
    rows = [slice(t * tile, (t + 1) * tile) for t in places]
    for here, t, window in zip(spans, places, windows):
        agg_ref[here, :] = (dot(count_ref[t], window()) * (1.0 / 6.0)).astype(BF16)
    for here, there in zip(spans, rows):
        pre = dot(x_ref[there, :], w_in_ref[:width, :]) + dot(agg_ref[here, :], w_in_ref[width:, :])
        act_ref[here, :] = (0.5 * pre * (1.0 + jnp.tanh(0.5 * pre))).astype(BF16)
    for here, there in zip(spans, rows):
        upd = dot(act_ref[here, :], w_out_ref[...])
        mean = jnp.mean(upd, axis=1, keepdims=True)
        centred = upd - mean
        var = jnp.mean(centred * centred, axis=1, keepdims=True)
        change = centred * lax.rsqrt(var + 1e-05) * gain_ref[...]
        h_ref[here, :] = (x_ref[there, :].astype(F32) + change).astype(BF16)
    return [dot_of(head_ref[...], h_ref[here, :], 1, 1).astype(BF16) for here in spans]


def inner_kernel(x_ref, count_ref, w_in_ref, w_out_ref, gain_ref, head_ref, h_ref, pred_ref, agg_ref, act_ref):
    tiles, tile, _ = count_ref.shape
    places = range(1, tiles - 1)

    def window(t):
        return lambda: x_ref[t * tile - RIM : (t + 1) * tile + RIM, :]

    preds = staged_update(
        x_ref, count_ref, w_in_ref, w_out_ref, gain_ref, head_ref,
        [window(t) for t in places], places, agg_ref, act_ref, h_ref,
    )
    for i, pred in enumerate(preds):
        pred_ref[i] = pred


def outer_kernel(members, x_ref, count_ref, w_in_ref, w_out_ref, gain_ref, head_ref, inner_ref, outer_ref, done_ref, h_ref, *refs):
    outs, (all_ref, agg_ref, act_ref) = refs[:-3], refs[-3:]
    tiles, tile, _ = count_ref.shape
    odd = lax.rem(lax.axis_index("dom"), 2) == 1
    inner, outer = inner_ref[...], outer_ref[...]
    before, after = jnp.where(odd, inner, outer), jnp.where(odd, outer, inner)
    rows = tiles * tile
    windows = [
        lambda: jnp.concatenate([before, x_ref[: tile + RIM, :]], axis=0),
        lambda: jnp.concatenate([x_ref[rows - tile - RIM :, :], after], axis=0),
    ]
    preds = staged_update(
        x_ref, count_ref, w_in_ref, w_out_ref, gain_ref, head_ref,
        windows, (0, tiles - 1), agg_ref, act_ref, h_ref,
    )
    all_ref[0] = preds[0]
    all_ref[tiles - 1] = preds[1]
    all_ref[1 : tiles - 1] = done_ref[...]
    me = lax.axis_index("mem")
    per = tiles // members
    for s, out in zip(mem_steps(members), outs):
        for k in range(per):
            out[:, k * tile : (k + 1) * tile] = all_ref[(me ^ s) * per + k]


def update_call(kernel, operands, out_shape, scratch, flops, name):
    return pl.pallas_call(
        kernel,
        out_shape=out_shape,
        in_specs=[pl.BlockSpec(memory_space=VMEM)] * len(operands),
        out_specs=[pl.BlockSpec(memory_space=VMEM)] * len(out_shape),
        scratch_shapes=scratch,
        compiler_params=params(24),
        cost_estimate=cost(flops, 8 * MIB),
        name=name,
    )(*operands)


def update(members, x, counts, w_in, w_out, gain, head, inner, outer):
    tiles, tile, _ = counts.shape
    width = x.shape[1]
    padded = head.shape[0]
    shared = (x, counts, w_in, w_out, gain, head)
    h_mid, pred_mid = update_call(
        inner_kernel,
        shared,
        [
            jax.ShapeDtypeStruct(((tiles - 2) * tile, width), BF16),
            jax.ShapeDtypeStruct((tiles - 2, padded, tile), BF16),
        ],
        [VMEM(((tiles - 2) * tile, width), BF16)] * 2,
        (tiles - 2) * tile * width * width * 10,
        "inner",
    )
    h_end, *preds = update_call(
        functools.partial(outer_kernel, members),
        shared + (inner, outer, pred_mid),
        [jax.ShapeDtypeStruct((2 * tile, width), BF16)]
        + [jax.ShapeDtypeStruct((padded, tiles // members * tile), BF16)] * members,
        [VMEM((tiles, padded, tile), BF16)] + [VMEM((2 * tile, width), BF16)] * 2,
        2 * tile * width * width * 10,
        "outer",
    )
    return h_mid, h_end, preds


def score_kernel(members, weight_ref, inv_ref, target_ref, *refs):
    preds, outs = refs[:members], refs[members:]
    inv_width, weight = inv_ref[...], weight_ref[...]
    weight = weight * -inv_width
    values = [r[...].astype(F32) for r in preds]
    sums = [jnp.zeros(v.shape, F32) for v in values]
    for i in range(members):
        for j in range(i + 1, members):
            phi = slope(values[i] - values[j], inv_width)
            sums[i] = sums[i] + phi
            sums[j] = sums[j] - phi
    for i in range(members):
        total = sums[i] * (1.0 / members) - slope(values[i] - target_ref[...], inv_width)
        outs[i][...] = (weight * total).astype(BF16)


def score(weight, inv_width, target, preds):
    members = len(preds)
    shape = preds[0].shape
    return pl.pallas_call(
        functools.partial(score_kernel, members),
        out_shape=[jax.ShapeDtypeStruct(shape, BF16)] * members,
        in_specs=[pl.BlockSpec(memory_space=VMEM)] * (3 + members),
        out_specs=[pl.BlockSpec(memory_space=VMEM)] * members,
        compiler_params=params(16),
        cost_estimate=cost(10 * preds[0].size * members * members, MIB, preds[0].size * members * members),
        name="score",
    )(weight, inv_width, target, *preds)


def head_kernel(members, mid_ref, end_ref, *refs):
    scores, (out, all_ref) = refs[:-2], refs[-2:]
    tiles, _, tile = all_ref.shape
    me = lax.axis_index("mem")
    per = tiles // members
    for s, value in zip(mem_steps(members), scores):
        for k in range(per):
            all_ref[(me ^ s) * per + k] = value[:, k * tile : (k + 1) * tile]
    total = dot(all_ref[0], end_ref[:tile, :]) + dot(all_ref[tiles - 1], end_ref[tile:, :])
    for t in range(1, tiles - 1):
        total = total + dot(all_ref[t], mid_ref[(t - 1) * tile : t * tile, :])
    out[...] = total.astype(BF16)


def head_terms(members, mid, end, scores):
    width = end.shape[1]
    tile = end.shape[0] // 2
    tiles = members * scores[0].shape[1] // tile
    padded = scores[0].shape[0]
    return pl.pallas_call(
        functools.partial(head_kernel, members),
        out_shape=[
            jax.ShapeDtypeStruct((padded, width), BF16),
            jax.ShapeDtypeStruct((tiles, padded, tile), BF16),
        ],
        in_specs=[pl.BlockSpec(memory_space=VMEM)] * (2 + members),
        out_specs=[pl.BlockSpec(memory_space=VMEM)] * 2,
        compiler_params=params(16),
        cost_estimate=cost(2 * padded * tiles * tile * width, 3 * MIB),
        name="head_terms",
    )(mid, end, *scores)


def latent_kernel(head_ref, score_ref, out):
    tile = score_ref.shape[2]
    for t in range(score_ref.shape[0]):
        out[0, t * tile : (t + 1) * tile, :] = dot_of(score_ref[t], head_ref[...], 0, 0).astype(BF16)


def latent_grad(head, scores):
    tiles, padded, tile = scores.shape
    width = head.shape[1]
    return pl.pallas_call(
        latent_kernel,
        out_shape=jax.ShapeDtypeStruct((1, tiles * tile, width), BF16),
        in_specs=[pl.BlockSpec(memory_space=VMEM)] * 2,
        out_specs=pl.BlockSpec(memory_space=VMEM),
        compiler_params=params(16),
        cost_estimate=cost(2 * scores.size * width, 3 * MIB),
        name="latent_grad",
    )(head, scores)


def total_kernel(scale, *refs):
    terms, out = refs[:-1], refs[-1]
    total = terms[0][...].astype(F32)
    for term in terms[1:]:
        total = total + term[...].astype(F32)
    out[:, 0, :] = (total * scale)[: out.shape[0], :]


def head_total(terms, num_vars, scale):
    return pl.pallas_call(
        functools.partial(total_kernel, scale),
        out_shape=jax.ShapeDtypeStruct((num_vars, 1, terms[0].shape[1]), F32),
        in_specs=[pl.BlockSpec(memory_space=VMEM)] * len(terms),
        out_specs=pl.BlockSpec(memory_space=VMEM),
        compiler_params=params(16),
        cost_estimate=cost(terms[0].size * len(terms), MIB),
        name="head_total",
    )(*terms)


def shards(
    coarse_latents,
    send_rows,
    up_index,
    up_weight,
    neighbors,
    live_counts,
    area,
    fine_skip,
    targets,
    kernel_width,
    w_in,
    w_out,
    ln_gain,
    w_head,
):
    dom_count = lax.axis_size("dom")
    members = lax.axis_size("mem")
    slots = send_rows.shape[2]
    rows, width = fine_skip.shape
    num_vars = w_head.shape[1]
    padded = num_vars + -num_vars % 8
    tile = min(256, rows // members)

    even = list(range(4, dom_count, 2))
    steps = list(range(dom_count))
    one, sent, table = first_pick(send_rows, coarse_latents, [1] + [s + 1 for s in even])
    one = xor_permute(one, "dom", 1)
    own, two, three, *far = pick(sent, table, [[0], [2], [3]] + [[s] for s in even])
    far = [xor_permute(v, "dom", s) for v, s in zip(pack(one, far), even)]
    two, three = xor_permute(two, "dom", 2), xor_permute(three, "dom", 3)
    sources = (up_index, up_weight, neighbors, w_head.T, area[None, :], targets, kernel_width[None, :])
    first_rows, last_rows, scale, counts, head, weight, inv_width, target = spread(
        own, live_counts, sources, steps, slots, 4, tile, padded, rows // members
    )
    sums = early(first_rows, scale, fine_skip, [own, one, two, three], tile)
    x, inner, outer = late(sums, last_rows, scale, far, tile)
    pairs = [(i, i + 1) for i in range(1, dom_count - 1, 2)]
    outer = lax.ppermute(outer, "dom", pairs + [(j, i) for i, j in pairs])
    inner = xor_permute(inner, "dom", 1)

    mid, end, preds = update(members, x, counts, w_in, w_out, ln_gain[None, :], head, inner, outer)
    trade = functools.partial(mem_trade, mem_steps(members))
    preds = trade(preds)
    scores = trade(score(weight, inv_width, target, preds))
    term, by_tile = head_terms(members, mid, end, scores)
    terms = trade([term] * members)
    grad_latent = latent_grad(head, by_tile)
    factor = 1.0 / math.sqrt(members * rows)
    return (grad_latent, head_total(terms, num_vars, factor).transpose(1, 2, 0))


def solution(mesh):
    return jax.shard_map(
        shards,
        mesh=mesh,
        in_specs=(
            P("mem", "dom", None),
            P("dom", None, None),
            P(None, "dom"),
            P(None, "dom"),
            P(None, "dom"),
            P("dom"),
            P("dom"),
            P("dom", None),
            P(None, "dom"),
            P(),
            P(),
            P(),
            P(),
            P(),
        ),
        out_specs=(P("mem", "dom", None), P("dom", None, None)),
        check_vma=False,
    )
```

```python
import functools
import math

import jax
import jax.numpy as jnp
from jax import lax
from jax.experimental import pallas as pl
from jax.experimental.pallas import tpu as pltpu
from jax.sharding import PartitionSpec as P

RIM = 128
MIB = 1024 * 1024
F32 = jnp.float32
BF16 = jnp.bfloat16
VMEM = pltpu.VMEM


def dot(a, b):
    return jnp.dot(a, b, preferred_element_type=F32)


def dot_of(a, b, da, db):
    return lax.dot_general(a, b, (((da,), (db,)), ((), ())), preferred_element_type=F32)


def params(mib):
    return pltpu.CompilerParams(vmem_limit_bytes=mib * MIB)


def cost(flops, nbytes, trans=0):
    return pl.CostEstimate(flops=flops, bytes_accessed=nbytes, transcendentals=trans)


def columns(rows):
    pad = -rows.shape[0] % 8
    if pad:
        rows = jnp.concatenate([rows, jnp.zeros((pad, rows.shape[1]), rows.dtype)], axis=0)
    return rows.T


def in_hbm(*values):
    return [pltpu.with_memory_space_constraint(v, pltpu.HBM) for v in values]


def fetch(pairs, sems):
    copies = [pltpu.make_async_copy(src, dst, sems.at[i]) for i, (src, dst) in enumerate(pairs)]
    for copy in copies:
        copy.start()
    for copy in copies:
        copy.wait()


def slope(diff, inv_width):
    ratio = diff * inv_width
    return ratio * jnp.exp(ratio * ratio * -0.5)


def xor_permute(value, axis, step):
    count = lax.axis_size(axis)
    return lax.ppermute(value, axis, [(i, i ^ step) for i in range(count)])


def mem_trade(steps, values):
    return [v if s == 0 else xor_permute(v, "mem", s) for s, v in zip(steps, values)]


def mem_steps(members):
    return [0] + list(range(members - 1, 0, -1))


def one_hot(rows, length):
    cols = columns(rows.astype(F32))
    spots = lax.broadcasted_iota(jnp.int32, (rows.shape[1], length), 1).astype(F32)
    hot = [(cols[:, k : k + 1] == spots).astype(F32).astype(BF16) for k in range(rows.shape[0])]
    return jnp.concatenate(hot, axis=0)


def picked(rows, table, outs):
    found = dot(one_hot(rows, table.shape[0]), table).astype(BF16)
    start = 0
    for out in outs:
        out[...] = found[start : start + out.shape[0], :]
        start += out.shape[0]


def send_rows_of(ref, steps):
    me = lax.axis_index("dom")
    return jnp.concatenate([ref[0, pl.ds(me ^ s, 1), :] for s in steps], axis=0)


def first_pick_kernel(steps, send_ref, coarse_ref, out, rows_ref, table_ref, sems):
    rows_copy = pltpu.make_async_copy(send_ref, rows_ref, sems.at[0])
    table_copy = pltpu.make_async_copy(coarse_ref, table_ref, sems.at[1])
    rows_copy.start()
    table_copy.start()
    rows_copy.wait()
    hot = one_hot(send_rows_of(rows_ref, steps), table_ref.shape[1])
    table_copy.wait()
    out[...] = dot(hot, table_ref[0]).astype(BF16)


def first_pick(send_rows, coarse, steps):
    slots, width = send_rows.shape[2], coarse.shape[2]
    return pl.pallas_call(
        functools.partial(first_pick_kernel, steps),
        out_shape=[
            jax.ShapeDtypeStruct((len(steps) * slots, width), BF16),
            jax.ShapeDtypeStruct(send_rows.shape, jnp.int32),
            jax.ShapeDtypeStruct(coarse.shape, BF16),
        ],
        in_specs=[pl.BlockSpec(memory_space=pltpu.HBM)] * 2,
        out_specs=[pl.BlockSpec(memory_space=VMEM)] * 3,
        scratch_shapes=[pltpu.SemaphoreType.DMA((2,))],
        compiler_params=params(8),
        cost_estimate=cost(1, 1),
        name="pick_first",
    )(*in_hbm(send_rows, coarse))


def pick_kernel(steps, rows_ref, table_ref, *outs):
    picked(send_rows_of(rows_ref, steps), table_ref[0], outs)


def pick(rows, table, groups):
    slots, width = rows.shape[2], table.shape[2]
    steps = [s for group in groups for s in group]
    return pl.pallas_call(
        functools.partial(pick_kernel, steps),
        out_shape=[jax.ShapeDtypeStruct((len(group) * slots, width), BF16) for group in groups],
        in_specs=[pl.BlockSpec(memory_space=VMEM)] * 2,
        out_specs=[pl.BlockSpec(memory_space=VMEM)] * len(groups),
        compiler_params=params(8),
        cost_estimate=cost(1, 1),
        name="pick",
    )(rows, table)


def best_scale(weight, counted):
    best = scale = jnp.ones((1, weight.shape[1]), F32)
    for c in range(24):
        factor = 1.0 + 0.0017 * c
        part = weight * (1.0 / factor)
        miss = jnp.where(counted, part - part.astype(BF16).astype(F32), 0.0)
        miss = miss * miss
        miss = miss[0:1] + miss[1:2] + miss[2:3]
        scale = jnp.where(miss < best, factor, scale)
        best = jnp.minimum(miss, best)
    return scale


def spread_kernel(tile, steps, live_ref, *refs):
    sources, outs, scratch = refs[:7], refs[8:17], refs[17:]
    first_ref, mid_ref, last_ref, scale_ref, count_ref, head_ref, area_ref, inv_ref, target_ref = outs
    held, kw_rows, sems = scratch[:7], scratch[7], scratch[8]
    fetch(list(zip(sources, held)), sems)
    index_ref, weight_ref, nb_ref, head_in_ref, area_in_ref, target_in_ref, kw_ref = held
    padded, piece = target_ref.shape
    num_vars = target_in_ref.shape[0]
    start = pl.multiple_of(lax.axis_index("mem") * piece, piece)
    place = start + lax.broadcasted_iota(jnp.int32, (1, piece), 1)
    area_ref[...] = jnp.where(place < live_ref[0], area_in_ref[:, pl.ds(start, piece)], 0.0)
    kw_rows[...] = jnp.ones(kw_rows.shape, F32)
    kw_rows[0:1, :num_vars] = kw_ref[...]
    width = kw_rows[...].T[:padded, 0:1]
    inv_ref[...] = 1.0 / width
    target_ref[...] = jnp.zeros(target_ref.shape, F32)
    target_ref[:num_vars, :] = target_in_ref[:, pl.ds(start, piece)].astype(F32)
    me = lax.axis_index("dom")
    rows = first_ref.shape[0]
    near = first_ref.shape[1] // 2
    cut = near + mid_ref.shape[1] // 2
    slots = cut + last_ref.shape[1]
    span = count_ref.shape[2]
    part = 32
    head_ref[...] = jnp.zeros(head_ref.shape, BF16)
    head_ref[: head_in_ref.shape[0], :] = head_in_ref[...]
    zero, one = jnp.zeros((), BF16), jnp.ones((), BF16)
    spots = lax.broadcasted_iota(jnp.int16, (part, slots), 1)
    places = lax.broadcasted_iota(jnp.int16, (part, span), 1)

    def narrow(value):
        return columns(value.astype(F32)).astype(jnp.int32).astype(jnp.int16)

    def step(t, carry):
        start = pl.multiple_of(t * tile, tile)
        lanes = pl.ds(start, tile)
        wanted = index_ref[:, lanes]
        step_of = lax.shift_right_logical(wanted, 7) ^ me
        place = jnp.zeros(wanted.shape, jnp.int32)
        for i, s in enumerate(steps):
            place = jnp.where(step_of == s, i * 128, place)
        found = place + (wanted & 127)
        i0, i1, i2 = found[0:1], found[1:2], found[2:3]
        w = weight_ref[:, lanes]
        w0, w1, w2 = w[0:1], w[1:2], w[2:3]
        same01, same02, same12 = i0 == i1, i0 == i2, (i1 == i2) & (i0 != i1)
        w0 = w0 + jnp.where(same01, w1, 0.0) + jnp.where(same02, w2, 0.0)
        w1 = jnp.where(same01, 0.0, w1 + jnp.where(same12, w2, 0.0))
        w2 = jnp.where(same02 | same12, 0.0, w2)
        i1 = jnp.where(same01, -1, i1)
        i2 = jnp.where(same02 | same12, -1, i2)
        found = jnp.concatenate([i0, i1, i2], axis=0)
        w = jnp.concatenate([w0, w1, w2], axis=0)
        scale = best_scale(w, found >= cut)
        scale_ref[:, lanes] = scale
        index = narrow(found)
        weight = columns(w / scale)
        high = weight.astype(BF16)
        low = (weight - high.astype(F32)).astype(BF16)
        around = narrow(nb_ref[:, lanes] - start)
        for r in range(0, tile, part):
            here = slice(r, r + part)
            rows_here = pl.ds(pl.multiple_of(start + r, part), part)
            total = jnp.zeros((part, slots), BF16)
            rest = jnp.zeros((part, cut), BF16)
            for k in range(3):
                hit = index[here, k : k + 1] == spots
                total = jnp.where(hit, high[here, k : k + 1], total)
                rest = jnp.where(hit[:, :cut], low[here, k : k + 1], rest)
            first_ref[rows_here, :near] = total[:, :near]
            first_ref[rows_here, near:] = rest[:, :near]
            mid_ref[rows_here, : cut - near] = total[:, near:cut]
            mid_ref[rows_here, cut - near :] = rest[:, near:]
            last_ref[rows_here, :] = total[:, cut:]
            counts = jnp.zeros((part, span), BF16)
            for k in range(nb_ref.shape[0]):
                counts = counts + jnp.where(around[here, k : k + 1] == places, one, zero)
            count_ref[t, here, :] = counts
        return carry

    lax.fori_loop(0, rows // tile, step, 0)


def spread(token, live_counts, sources, steps, slots, near, split, tile, padded, piece):
    up_index, head = sources[0], sources[3]
    rows = up_index.shape[1]
    tiles = rows // tile
    span = tile + 2 * RIM
    cut, total = split * slots, len(steps) * slots
    return pl.pallas_call(
        functools.partial(spread_kernel, tile, steps),
        out_shape=[
            jax.ShapeDtypeStruct((rows, 2 * near * slots), BF16),
            jax.ShapeDtypeStruct((rows, 2 * (cut - near * slots)), BF16),
            jax.ShapeDtypeStruct((rows, total - cut), BF16),
            jax.ShapeDtypeStruct((1, rows), F32),
            jax.ShapeDtypeStruct((tiles, tile, span), BF16),
            jax.ShapeDtypeStruct((padded, head.shape[1]), BF16),
            jax.ShapeDtypeStruct((1, piece), F32),
            jax.ShapeDtypeStruct((padded, 1), F32),
            jax.ShapeDtypeStruct((padded, piece), F32),
        ],
        in_specs=[pl.BlockSpec(memory_space=pltpu.SMEM)]
        + [pl.BlockSpec(memory_space=pltpu.HBM)] * 7
        + [pl.BlockSpec(memory_space=VMEM)],
        out_specs=[pl.BlockSpec(memory_space=VMEM)] * 9,
        scratch_shapes=[VMEM(v.shape, v.dtype) for v in sources]
        + [VMEM((8, 128), F32), pltpu.SemaphoreType.DMA((7,))],
        compiler_params=params(16),
        cost_estimate=cost(1, 1),
        name="spread",
    )(live_counts, *in_hbm(*sources), token)


def pack_kernel(other_ref, *refs):
    count = len(refs) // 2
    for i in range(count):
        mine, out = refs[i], refs[count + i]
        slots = mine.shape[0]
        out[:slots, :] = mine[...]
        out[slots:, :] = other_ref[(i + 1) * slots : (i + 2) * slots, :]


def pack(other, mine):
    slots, width = mine[0].shape
    return pl.pallas_call(
        pack_kernel,
        out_shape=[jax.ShapeDtypeStruct((2 * slots, width), BF16)] * len(mine),
        in_specs=[pl.BlockSpec(memory_space=VMEM)] * (1 + len(mine)),
        out_specs=[pl.BlockSpec(memory_space=VMEM)] * len(mine),
        compiler_params=params(16),
        cost_estimate=cost(1, 1),
        name="pack",
    )(other, *mine)


def part_kernel(tile, lengths, spread_ref, scale_ref, base_ref, *refs):
    tables, out = refs[:-1], refs[-1]
    parts = [r[:length, :] for r, length in zip(tables, lengths)]
    table = jnp.concatenate(parts + parts, axis=0)

    def step(t, carry):
        start = pl.multiple_of(t * tile, tile)
        rows = pl.ds(start, tile)
        scale = columns(scale_ref[:, rows])[:, 0:1]
        out[rows, :] = base_ref[rows, :].astype(F32) + scale * dot(spread_ref[rows, :], table)
        return carry

    lax.fori_loop(0, out.shape[0] // tile, step, 0, unroll=4)


def add_part(spread_rows, scale, base, tables, lengths, tile, name):
    return pl.pallas_call(
        functools.partial(part_kernel, tile, lengths),
        out_shape=jax.ShapeDtypeStruct(base.shape, F32),
        in_specs=[pl.BlockSpec(memory_space=VMEM)] * (3 + len(tables)),
        out_specs=pl.BlockSpec(memory_space=VMEM),
        compiler_params=params(16),
        cost_estimate=cost(1, 1),
        name=name,
    )(spread_rows, scale, base, *tables)


def late_kernel(tile, sum_ref, spread_ref, scale_ref, *refs):
    tables, (x_ref, inner_ref, outer_ref) = refs[:-3], refs[-3:]
    table = jnp.concatenate([r[...] for r in tables], axis=0)
    count = x_ref.shape[0]

    def step(t, carry):
        start = pl.multiple_of(t * tile, tile)
        rows = pl.ds(start, tile)
        scale = columns(scale_ref[:, rows])[:, 0:1]
        x_ref[rows, :] = (sum_ref[rows, :] + scale * dot(spread_ref[rows, :], table)).astype(BF16)
        return carry

    lax.fori_loop(0, count // tile, step, 0, unroll=count // tile)
    odd = lax.rem(lax.axis_index("dom"), 2) == 1
    first, last = x_ref[:RIM, :], x_ref[count - RIM :, :]
    inner_ref[...] = jnp.where(odd, first, last)
    outer_ref[...] = jnp.where(odd, last, first)


def late(sums, spread_rows, scale, tables, tile):
    rows, width = sums.shape
    operands = (sums, spread_rows, scale, *tables)
    edge = jax.ShapeDtypeStruct((RIM, width), BF16)
    return pl.pallas_call(
        functools.partial(late_kernel, tile),
        out_shape=[jax.ShapeDtypeStruct((rows, width), BF16), edge, edge],
        in_specs=[pl.BlockSpec(memory_space=VMEM)] * len(operands),
        out_specs=[pl.BlockSpec(memory_space=VMEM)] * 3,
        compiler_params=params(16),
        cost_estimate=cost(2 * spread_rows.size * width, 8 * MIB),
        name="late",
    )(*operands)


def staged_update(x_ref, count_ref, w_in_ref, w_out_ref, gain_ref, head_ref, windows, places, agg_ref, act_ref, h_ref):
    tile = count_ref.shape[1]
    width = x_ref.shape[1]
    spans = [slice(i * tile, (i + 1) * tile) for i in range(len(places))]
    rows = [slice(t * tile, (t + 1) * tile) for t in places]
    for here, t, window in zip(spans, places, windows):
        agg_ref[here, :] = (dot(count_ref[t], window()) * (1.0 / 6.0)).astype(BF16)
    for here, there in zip(spans, rows):
        pre = dot(x_ref[there, :], w_in_ref[:width, :]) + dot(agg_ref[here, :], w_in_ref[width:, :])
        act_ref[here, :] = (0.5 * pre * (1.0 + jnp.tanh(0.5 * pre))).astype(BF16)
    for here, there in zip(spans, rows):
        upd = dot(act_ref[here, :], w_out_ref[...])
        mean = jnp.mean(upd, axis=1, keepdims=True)
        centred = upd - mean
        var = jnp.mean(centred * centred, axis=1, keepdims=True)
        change = centred * lax.rsqrt(var + 1e-05) * gain_ref[...]
        h_ref[here, :] = (x_ref[there, :].astype(F32) + change).astype(BF16)
    return [dot_of(head_ref[...], h_ref[here, :], 1, 1).astype(BF16) for here in spans]


def inner_kernel(x_ref, count_ref, w_in_ref, w_out_ref, gain_ref, head_ref, h_ref, pred_ref, agg_ref, act_ref):
    tiles, tile, _ = count_ref.shape
    places = range(1, tiles - 1)

    def window(t):
        return lambda: x_ref[t * tile - RIM : (t + 1) * tile + RIM, :]

    preds = staged_update(
        x_ref, count_ref, w_in_ref, w_out_ref, gain_ref, head_ref,
        [window(t) for t in places], places, agg_ref, act_ref, h_ref,
    )
    for i, pred in enumerate(preds):
        pred_ref[i] = pred


def outer_kernel(members, x_ref, count_ref, w_in_ref, w_out_ref, gain_ref, head_ref, inner_ref, outer_ref, done_ref, h_ref, *refs):
    outs, (all_ref, agg_ref, act_ref) = refs[:-3], refs[-3:]
    tiles, tile, _ = count_ref.shape
    odd = lax.rem(lax.axis_index("dom"), 2) == 1
    inner, outer = inner_ref[...], outer_ref[...]
    before, after = jnp.where(odd, inner, outer), jnp.where(odd, outer, inner)
    rows = tiles * tile
    windows = [
        lambda: jnp.concatenate([before, x_ref[: tile + RIM, :]], axis=0),
        lambda: jnp.concatenate([x_ref[rows - tile - RIM :, :], after], axis=0),
    ]
    preds = staged_update(
        x_ref, count_ref, w_in_ref, w_out_ref, gain_ref, head_ref,
        windows, (0, tiles - 1), agg_ref, act_ref, h_ref,
    )
    all_ref[0] = preds[0]
    all_ref[tiles - 1] = preds[1]
    all_ref[1 : tiles - 1] = done_ref[...]
    me = lax.axis_index("mem")
    per = tiles // members
    for s, out in zip(mem_steps(members), outs):
        for k in range(per):
            out[:, k * tile : (k + 1) * tile] = all_ref[(me ^ s) * per + k]


def update_call(kernel, operands, out_shape, scratch, flops, name):
    return pl.pallas_call(
        kernel,
        out_shape=out_shape,
        in_specs=[pl.BlockSpec(memory_space=VMEM)] * len(operands),
        out_specs=[pl.BlockSpec(memory_space=VMEM)] * len(out_shape),
        scratch_shapes=scratch,
        compiler_params=params(24),
        cost_estimate=cost(flops, 8 * MIB),
        name=name,
    )(*operands)


def update(members, x, counts, w_in, w_out, gain, head, inner, outer):
    tiles, tile, _ = counts.shape
    width = x.shape[1]
    padded = head.shape[0]
    shared = (x, counts, w_in, w_out, gain, head)
    h_mid, pred_mid = update_call(
        inner_kernel,
        shared,
        [
            jax.ShapeDtypeStruct(((tiles - 2) * tile, width), BF16),
            jax.ShapeDtypeStruct((tiles - 2, padded, tile), BF16),
        ],
        [VMEM(((tiles - 2) * tile, width), BF16)] * 2,
        (tiles - 2) * tile * width * width * 10,
        "inner",
    )
    h_end, *preds = update_call(
        functools.partial(outer_kernel, members),
        shared + (inner, outer, pred_mid),
        [jax.ShapeDtypeStruct((2 * tile, width), BF16)]
        + [jax.ShapeDtypeStruct((padded, tiles // members * tile), BF16)] * members,
        [VMEM((tiles, padded, tile), BF16)] + [VMEM((2 * tile, width), BF16)] * 2,
        2 * tile * width * width * 10,
        "outer",
    )
    return h_mid, h_end, preds


def score_kernel(members, weight_ref, inv_ref, target_ref, *refs):
    preds, outs = refs[:members], refs[members:]
    inv_width, weight = inv_ref[...], weight_ref[...]
    weight = weight * -inv_width
    values = [r[...].astype(F32) for r in preds]
    sums = [jnp.zeros(v.shape, F32) for v in values]
    for i in range(members):
        for j in range(i + 1, members):
            phi = slope(values[i] - values[j], inv_width)
            sums[i] = sums[i] + phi
            sums[j] = sums[j] - phi
    for i in range(members):
        total = sums[i] * (1.0 / members) - slope(values[i] - target_ref[...], inv_width)
        outs[i][...] = (weight * total).astype(BF16)


def score(weight, inv_width, target, preds):
    members = len(preds)
    shape = preds[0].shape
    return pl.pallas_call(
        functools.partial(score_kernel, members),
        out_shape=[jax.ShapeDtypeStruct(shape, BF16)] * members,
        in_specs=[pl.BlockSpec(memory_space=VMEM)] * (3 + members),
        out_specs=[pl.BlockSpec(memory_space=VMEM)] * members,
        compiler_params=params(16),
        cost_estimate=cost(10 * preds[0].size * members * members, MIB, preds[0].size * members * members),
        name="score",
    )(weight, inv_width, target, *preds)


def head_kernel(members, mid_ref, end_ref, *refs):
    scores, (out, all_ref) = refs[:-2], refs[-2:]
    tiles, _, tile = all_ref.shape
    me = lax.axis_index("mem")
    per = tiles // members
    for s, value in zip(mem_steps(members), scores):
        for k in range(per):
            all_ref[(me ^ s) * per + k] = value[:, k * tile : (k + 1) * tile]
    total = dot(all_ref[0], end_ref[:tile, :]) + dot(all_ref[tiles - 1], end_ref[tile:, :])
    for t in range(1, tiles - 1):
        total = total + dot(all_ref[t], mid_ref[(t - 1) * tile : t * tile, :])
    out[...] = total.astype(BF16)


def head_terms(members, mid, end, scores):
    width = end.shape[1]
    tile = end.shape[0] // 2
    tiles = members * scores[0].shape[1] // tile
    padded = scores[0].shape[0]
    return pl.pallas_call(
        functools.partial(head_kernel, members),
        out_shape=[
            jax.ShapeDtypeStruct((padded, width), BF16),
            jax.ShapeDtypeStruct((tiles, padded, tile), BF16),
        ],
        in_specs=[pl.BlockSpec(memory_space=VMEM)] * (2 + members),
        out_specs=[pl.BlockSpec(memory_space=VMEM)] * 2,
        compiler_params=params(16),
        cost_estimate=cost(2 * padded * tiles * tile * width, 3 * MIB),
        name="head_terms",
    )(mid, end, *scores)


def latent_kernel(head_ref, score_ref, out):
    tile = score_ref.shape[2]
    for t in range(score_ref.shape[0]):
        out[0, t * tile : (t + 1) * tile, :] = dot_of(score_ref[t], head_ref[...], 0, 0).astype(BF16)


def latent_grad(head, scores):
    tiles, padded, tile = scores.shape
    width = head.shape[1]
    return pl.pallas_call(
        latent_kernel,
        out_shape=jax.ShapeDtypeStruct((1, tiles * tile, width), BF16),
        in_specs=[pl.BlockSpec(memory_space=VMEM)] * 2,
        out_specs=pl.BlockSpec(memory_space=VMEM),
        compiler_params=params(16),
        cost_estimate=cost(2 * scores.size * width, 3 * MIB),
        name="latent_grad",
    )(head, scores)


def total_kernel(scale, *refs):
    terms, out = refs[:-1], refs[-1]
    total = terms[0][...].astype(F32)
    for term in terms[1:]:
        total = total + term[...].astype(F32)
    out[:, 0, :] = (total * scale)[: out.shape[0], :]


def head_total(terms, num_vars, scale):
    return pl.pallas_call(
        functools.partial(total_kernel, scale),
        out_shape=jax.ShapeDtypeStruct((num_vars, 1, terms[0].shape[1]), F32),
        in_specs=[pl.BlockSpec(memory_space=VMEM)] * len(terms),
        out_specs=pl.BlockSpec(memory_space=VMEM),
        compiler_params=params(16),
        cost_estimate=cost(terms[0].size * len(terms), MIB),
        name="head_total",
    )(*terms)


def shards(
    coarse_latents,
    send_rows,
    up_index,
    up_weight,
    neighbors,
    live_counts,
    area,
    fine_skip,
    targets,
    kernel_width,
    w_in,
    w_out,
    ln_gain,
    w_head,
):
    dom_count = lax.axis_size("dom")
    members = lax.axis_size("mem")
    slots = send_rows.shape[2]
    rows, width = fine_skip.shape
    num_vars = w_head.shape[1]
    padded = num_vars + -num_vars % 8
    tile = min(256, rows // members)

    even = list(range(4, dom_count, 2))
    steps = list(range(dom_count))
    one, sent, table = first_pick(send_rows, coarse_latents, [1] + [s + 1 for s in even])
    one = xor_permute(one, "dom", 1)
    own, two, three, *far = pick(sent, table, [[0], [2], [3]] + [[s] for s in even])
    far = [xor_permute(v, "dom", s) for v, s in zip(pack(one, far), even)]
    two, three = xor_permute(two, "dom", 2), xor_permute(three, "dom", 3)
    sources = (up_index, up_weight, neighbors, w_head.T, area[None, :], targets, kernel_width[None, :])
    split = dom_count - 2
    first_rows, mid_rows, last_rows, scale, counts, head, weight, inv_width, target = spread(
        own, live_counts, sources, steps, slots, 4, split, tile, padded, rows // members
    )
    sums = add_part(first_rows, scale, fine_skip, [own, one, two, three], [slots] * 4, tile, "early")
    sums = add_part(mid_rows, scale, sums, far[:-1], [2 * slots] * (len(far) - 1), tile, "middle")
    x, inner, outer = late(sums, last_rows, scale, far[-1:], tile)
    pairs = [(i, i + 1) for i in range(1, dom_count - 1, 2)]
    outer = lax.ppermute(outer, "dom", pairs + [(j, i) for i, j in pairs])
    inner = xor_permute(inner, "dom", 1)

    mid, end, preds = update(members, x, counts, w_in, w_out, ln_gain[None, :], head, inner, outer)
    trade = functools.partial(mem_trade, mem_steps(members))
    preds = trade(preds)
    scores = trade(score(weight, inv_width, target, preds))
    term, by_tile = head_terms(members, mid, end, scores)
    terms = trade([term] * members)
    grad_latent = latent_grad(head, by_tile)
    factor = 1.0 / math.sqrt(members * rows)
    return (grad_latent, head_total(terms, num_vars, factor).transpose(1, 2, 0))


def solution(mesh):
    return jax.shard_map(
        shards,
        mesh=mesh,
        in_specs=(
            P("mem", "dom", None),
            P("dom", None, None),
            P(None, "dom"),
            P(None, "dom"),
            P(None, "dom"),
            P("dom"),
            P("dom"),
            P("dom", None),
            P(None, "dom"),
            P(),
            P(),
            P(),
            P(),
            P(),
        ),
        out_specs=(P("mem", "dom", None), P("dom", None, None)),
        check_vma=False,
    )
```

```python
import functools
import math

import jax
import jax.numpy as jnp
from jax import lax
from jax.experimental import pallas as pl
from jax.experimental.pallas import tpu as pltpu
from jax.sharding import PartitionSpec as P

RIM = 128
MIB = 1024 * 1024
F32 = jnp.float32
BF16 = jnp.bfloat16
VMEM = pltpu.VMEM


def dot(a, b):
    return jnp.dot(a, b, preferred_element_type=F32)


def dot_of(a, b, da, db):
    return lax.dot_general(a, b, (((da,), (db,)), ((), ())), preferred_element_type=F32)


def params(mib):
    return pltpu.CompilerParams(vmem_limit_bytes=mib * MIB)


def cost(flops, nbytes, trans=0):
    return pl.CostEstimate(flops=flops, bytes_accessed=nbytes, transcendentals=trans)


def columns(rows):
    pad = -rows.shape[0] % 8
    if pad:
        rows = jnp.concatenate([rows, jnp.zeros((pad, rows.shape[1]), rows.dtype)], axis=0)
    return rows.T


def in_hbm(*values):
    return [pltpu.with_memory_space_constraint(v, pltpu.HBM) for v in values]


def fetch(pairs, sems):
    copies = [pltpu.make_async_copy(src, dst, sems.at[i]) for i, (src, dst) in enumerate(pairs)]
    for copy in copies:
        copy.start()
    for copy in copies:
        copy.wait()


def slope(diff, inv_width):
    ratio = diff * inv_width
    return ratio * jnp.exp(ratio * ratio * -0.5)


def xor_permute(value, axis, step):
    count = lax.axis_size(axis)
    return lax.ppermute(value, axis, [(i, i ^ step) for i in range(count)])


def mem_trade(steps, values):
    return [v if s == 0 else xor_permute(v, "mem", s) for s, v in zip(steps, values)]


def mem_steps(members):
    return [0] + list(range(members - 1, 0, -1))


def one_hot(rows, length):
    cols = columns(rows.astype(F32))
    spots = lax.broadcasted_iota(jnp.int32, (rows.shape[1], length), 1).astype(F32)
    hot = [(cols[:, k : k + 1] == spots).astype(F32).astype(BF16) for k in range(rows.shape[0])]
    return jnp.concatenate(hot, axis=0)


def picked(rows, table, outs):
    found = dot(one_hot(rows, table.shape[0]), table).astype(BF16)
    start = 0
    for out in outs:
        out[...] = found[start : start + out.shape[0], :]
        start += out.shape[0]


def send_rows_of(ref, steps):
    me = lax.axis_index("dom")
    return jnp.concatenate([ref[0, pl.ds(me ^ s, 1), :] for s in steps], axis=0)


def first_pick_kernel(steps, send_ref, coarse_ref, out, rows_ref, table_ref, sems):
    rows_copy = pltpu.make_async_copy(send_ref, rows_ref, sems.at[0])
    table_copy = pltpu.make_async_copy(coarse_ref, table_ref, sems.at[1])
    rows_copy.start()
    table_copy.start()
    rows_copy.wait()
    hot = one_hot(send_rows_of(rows_ref, steps), table_ref.shape[1])
    table_copy.wait()
    out[...] = dot(hot, table_ref[0]).astype(BF16)


def first_pick(send_rows, coarse, steps):
    slots, width = send_rows.shape[2], coarse.shape[2]
    return pl.pallas_call(
        functools.partial(first_pick_kernel, steps),
        out_shape=[
            jax.ShapeDtypeStruct((len(steps) * slots, width), BF16),
            jax.ShapeDtypeStruct(send_rows.shape, jnp.int32),
            jax.ShapeDtypeStruct(coarse.shape, BF16),
        ],
        in_specs=[pl.BlockSpec(memory_space=pltpu.HBM)] * 2,
        out_specs=[pl.BlockSpec(memory_space=VMEM)] * 3,
        scratch_shapes=[pltpu.SemaphoreType.DMA((2,))],
        compiler_params=params(8),
        cost_estimate=cost(1, 1),
        name="pick_first",
    )(*in_hbm(send_rows, coarse))


def pick_kernel(steps, rows_ref, table_ref, *outs):
    picked(send_rows_of(rows_ref, steps), table_ref[0], outs)


def pick(rows, table, groups):
    slots, width = rows.shape[2], table.shape[2]
    steps = [s for group in groups for s in group]
    return pl.pallas_call(
        functools.partial(pick_kernel, steps),
        out_shape=[jax.ShapeDtypeStruct((len(group) * slots, width), BF16) for group in groups],
        in_specs=[pl.BlockSpec(memory_space=VMEM)] * 2,
        out_specs=[pl.BlockSpec(memory_space=VMEM)] * len(groups),
        compiler_params=params(8),
        cost_estimate=cost(1, 1),
        name="pick",
    )(rows, table)


def best_scale(weight, counted):
    best = scale = jnp.ones((1, weight.shape[1]), F32)
    for c in range(24):
        factor = 1.0 + 0.0017 * c
        part = weight * (1.0 / factor)
        miss = jnp.where(counted, part - part.astype(BF16).astype(F32), 0.0)
        miss = miss * miss
        miss = miss[0:1] + miss[1:2] + miss[2:3]
        scale = jnp.where(miss < best, factor, scale)
        best = jnp.minimum(miss, best)
    return scale


def spread_kernel(tile, steps, live_ref, *refs):
    sources, outs, scratch = refs[:7], refs[8:17], refs[17:]
    first_ref, mid_ref, last_ref, scale_ref, count_ref, head_ref, area_ref, inv_ref, target_ref = outs
    held, kw_rows, sems = scratch[:7], scratch[7], scratch[8]
    fetch(list(zip(sources, held)), sems)
    index_ref, weight_ref, nb_ref, head_in_ref, area_in_ref, target_in_ref, kw_ref = held
    padded, piece = target_ref.shape
    num_vars = target_in_ref.shape[0]
    start = pl.multiple_of(lax.axis_index("mem") * piece, piece)
    place = start + lax.broadcasted_iota(jnp.int32, (1, piece), 1)
    area_ref[...] = jnp.where(place < live_ref[0], area_in_ref[:, pl.ds(start, piece)], 0.0)
    kw_rows[...] = jnp.ones(kw_rows.shape, F32)
    kw_rows[0:1, :num_vars] = kw_ref[...]
    width = kw_rows[...].T[:padded, 0:1]
    inv_ref[...] = 1.0 / width
    target_ref[...] = jnp.zeros(target_ref.shape, F32)
    target_ref[:num_vars, :] = target_in_ref[:, pl.ds(start, piece)].astype(F32)
    me = lax.axis_index("dom")
    rows = first_ref.shape[0]
    near = first_ref.shape[1] // 2
    cut = near + mid_ref.shape[1] // 2
    slots = cut + last_ref.shape[1]
    span = count_ref.shape[2]
    part = 32
    head_ref[...] = jnp.zeros(head_ref.shape, BF16)
    head_ref[: head_in_ref.shape[0], :] = head_in_ref[...]
    zero, one = jnp.zeros((), BF16), jnp.ones((), BF16)
    spots = lax.broadcasted_iota(jnp.int16, (part, slots), 1)
    places = lax.broadcasted_iota(jnp.int16, (part, span), 1)

    def narrow(value):
        return columns(value.astype(F32)).astype(jnp.int32).astype(jnp.int16)

    def step(t, carry):
        start = pl.multiple_of(t * tile, tile)
        lanes = pl.ds(start, tile)
        wanted = index_ref[:, lanes]
        step_of = lax.shift_right_logical(wanted, 7) ^ me
        place = jnp.zeros(wanted.shape, jnp.int32)
        for i, s in enumerate(steps):
            place = jnp.where(step_of == s, i * 128, place)
        found = place + (wanted & 127)
        i0, i1, i2 = found[0:1], found[1:2], found[2:3]
        w = weight_ref[:, lanes]
        w0, w1, w2 = w[0:1], w[1:2], w[2:3]
        same01, same02, same12 = i0 == i1, i0 == i2, (i1 == i2) & (i0 != i1)
        w0 = w0 + jnp.where(same01, w1, 0.0) + jnp.where(same02, w2, 0.0)
        w1 = jnp.where(same01, 0.0, w1 + jnp.where(same12, w2, 0.0))
        w2 = jnp.where(same02 | same12, 0.0, w2)
        i1 = jnp.where(same01, -1, i1)
        i2 = jnp.where(same02 | same12, -1, i2)
        found = jnp.concatenate([i0, i1, i2], axis=0)
        w = jnp.concatenate([w0, w1, w2], axis=0)
        scale = best_scale(w, found >= cut)
        scale_ref[:, lanes] = scale
        index = narrow(found)
        weight = columns(w / scale)
        high = weight.astype(BF16)
        low = (weight - high.astype(F32)).astype(BF16)
        around = narrow(nb_ref[:, lanes] - start)
        for r in range(0, tile, part):
            here = slice(r, r + part)
            rows_here = pl.ds(pl.multiple_of(start + r, part), part)
            total = jnp.zeros((part, slots), BF16)
            rest = jnp.zeros((part, cut), BF16)
            for k in range(3):
                hit = index[here, k : k + 1] == spots
                total = jnp.where(hit, high[here, k : k + 1], total)
                rest = jnp.where(hit[:, :cut], low[here, k : k + 1], rest)
            first_ref[rows_here, :near] = total[:, :near]
            first_ref[rows_here, near:] = rest[:, :near]
            mid_ref[rows_here, : cut - near] = total[:, near:cut]
            mid_ref[rows_here, cut - near :] = rest[:, near:]
            last_ref[rows_here, :] = total[:, cut:]
            counts = jnp.zeros((part, span), BF16)
            for k in range(nb_ref.shape[0]):
                counts = counts + jnp.where(around[here, k : k + 1] == places, one, zero)
            count_ref[t, here, :] = counts
        return carry

    lax.fori_loop(0, rows // tile, step, 0)


def spread(token, live_counts, sources, steps, slots, near, split, tile, padded, piece):
    up_index, head = sources[0], sources[3]
    rows = up_index.shape[1]
    tiles = rows // tile
    span = tile + 2 * RIM
    cut, total = split * slots, len(steps) * slots
    return pl.pallas_call(
        functools.partial(spread_kernel, tile, steps),
        out_shape=[
            jax.ShapeDtypeStruct((rows, 2 * near * slots), BF16),
            jax.ShapeDtypeStruct((rows, 2 * (cut - near * slots)), BF16),
            jax.ShapeDtypeStruct((rows, total - cut), BF16),
            jax.ShapeDtypeStruct((1, rows), F32),
            jax.ShapeDtypeStruct((tiles, tile, span), BF16),
            jax.ShapeDtypeStruct((padded, head.shape[1]), BF16),
            jax.ShapeDtypeStruct((1, piece), F32),
            jax.ShapeDtypeStruct((padded, 1), F32),
            jax.ShapeDtypeStruct((padded, piece), F32),
        ],
        in_specs=[pl.BlockSpec(memory_space=pltpu.SMEM)]
        + [pl.BlockSpec(memory_space=pltpu.HBM)] * 7
        + [pl.BlockSpec(memory_space=VMEM)],
        out_specs=[pl.BlockSpec(memory_space=VMEM)] * 9,
        scratch_shapes=[VMEM(v.shape, v.dtype) for v in sources]
        + [VMEM((8, 128), F32), pltpu.SemaphoreType.DMA((7,))],
        compiler_params=params(16),
        cost_estimate=cost(1, 1),
        name="spread",
    )(live_counts, *in_hbm(*sources), token)


def pack_kernel(other_ref, *refs):
    count = len(refs) // 2
    for i in range(count):
        mine, out = refs[i], refs[count + i]
        slots = mine.shape[0]
        out[:slots, :] = mine[...]
        out[slots:, :] = other_ref[(i + 1) * slots : (i + 2) * slots, :]


def pack(other, mine):
    slots, width = mine[0].shape
    return pl.pallas_call(
        pack_kernel,
        out_shape=[jax.ShapeDtypeStruct((2 * slots, width), BF16)] * len(mine),
        in_specs=[pl.BlockSpec(memory_space=VMEM)] * (1 + len(mine)),
        out_specs=[pl.BlockSpec(memory_space=VMEM)] * len(mine),
        compiler_params=params(16),
        cost_estimate=cost(1, 1),
        name="pack",
    )(other, *mine)


def part_kernel(tile, lengths, spread_ref, scale_ref, base_ref, *refs):
    tables, out = refs[:-1], refs[-1]
    parts = [r[:length, :] for r, length in zip(tables, lengths)]
    table = jnp.concatenate(parts + parts, axis=0)

    def step(t, carry):
        start = pl.multiple_of(t * tile, tile)
        rows = pl.ds(start, tile)
        scale = columns(scale_ref[:, rows])[:, 0:1]
        out[rows, :] = base_ref[rows, :].astype(F32) + scale * dot(spread_ref[rows, :], table)
        return carry

    lax.fori_loop(0, out.shape[0] // tile, step, 0, unroll=4)


def add_part(spread_rows, scale, base, tables, lengths, tile, name):
    return pl.pallas_call(
        functools.partial(part_kernel, tile, lengths),
        out_shape=jax.ShapeDtypeStruct(base.shape, F32),
        in_specs=[pl.BlockSpec(memory_space=VMEM)] * (3 + len(tables)),
        out_specs=pl.BlockSpec(memory_space=VMEM),
        compiler_params=params(16),
        cost_estimate=cost(1, 1),
        name=name,
    )(spread_rows, scale, base, *tables)


def late_kernel(tile, sum_ref, spread_ref, scale_ref, *refs):
    tables, (x_ref, inner_ref, outer_ref) = refs[:-3], refs[-3:]
    table = jnp.concatenate([r[...] for r in tables], axis=0)
    count = x_ref.shape[0]

    def step(t, carry):
        start = pl.multiple_of(t * tile, tile)
        rows = pl.ds(start, tile)
        scale = columns(scale_ref[:, rows])[:, 0:1]
        x_ref[rows, :] = (sum_ref[rows, :] + scale * dot(spread_ref[rows, :], table)).astype(BF16)
        return carry

    lax.fori_loop(0, count // tile, step, 0, unroll=count // tile)
    odd = lax.rem(lax.axis_index("dom"), 2) == 1
    first, last = x_ref[:RIM, :], x_ref[count - RIM :, :]
    inner_ref[...] = jnp.where(odd, first, last)
    outer_ref[...] = jnp.where(odd, last, first)


def late(sums, spread_rows, scale, tables, tile):
    rows, width = sums.shape
    operands = (sums, spread_rows, scale, *tables)
    edge = jax.ShapeDtypeStruct((RIM, width), BF16)
    return pl.pallas_call(
        functools.partial(late_kernel, tile),
        out_shape=[jax.ShapeDtypeStruct((rows, width), BF16), edge, edge],
        in_specs=[pl.BlockSpec(memory_space=VMEM)] * len(operands),
        out_specs=[pl.BlockSpec(memory_space=VMEM)] * 3,
        compiler_params=params(16),
        cost_estimate=cost(2 * spread_rows.size * width, 8 * MIB),
        name="late",
    )(*operands)


def staged_update(x_ref, count_ref, w_in_ref, w_out_ref, gain_ref, head_ref, windows, places, agg_ref, act_ref, h_ref):
    tile = count_ref.shape[1]
    width = x_ref.shape[1]
    spans = [slice(i * tile, (i + 1) * tile) for i in range(len(places))]
    rows = [slice(t * tile, (t + 1) * tile) for t in places]
    for here, t, window in zip(spans, places, windows):
        agg_ref[here, :] = (dot(count_ref[t], window()) * (1.0 / 6.0)).astype(BF16)
    for here, there in zip(spans, rows):
        pre = dot(x_ref[there, :], w_in_ref[:width, :]) + dot(agg_ref[here, :], w_in_ref[width:, :])
        act_ref[here, :] = (0.5 * pre * (1.0 + jnp.tanh(0.5 * pre))).astype(BF16)
    for here, there in zip(spans, rows):
        upd = dot(act_ref[here, :], w_out_ref[...])
        mean = jnp.mean(upd, axis=1, keepdims=True)
        centred = upd - mean
        var = jnp.mean(centred * centred, axis=1, keepdims=True)
        change = centred * lax.rsqrt(var + 1e-05) * gain_ref[...]
        h_ref[here, :] = (x_ref[there, :].astype(F32) + change).astype(BF16)
    return [dot_of(head_ref[...], h_ref[here, :], 1, 1).astype(BF16) for here in spans]


def inner_kernel(x_ref, count_ref, w_in_ref, w_out_ref, gain_ref, head_ref, h_ref, pred_ref, agg_ref, act_ref):
    tiles, tile, _ = count_ref.shape
    places = range(1, tiles - 1)

    def window(t):
        return lambda: x_ref[t * tile - RIM : (t + 1) * tile + RIM, :]

    preds = staged_update(
        x_ref, count_ref, w_in_ref, w_out_ref, gain_ref, head_ref,
        [window(t) for t in places], places, agg_ref, act_ref, h_ref,
    )
    for i, pred in enumerate(preds):
        pred_ref[i] = pred


def outer_kernel(members, x_ref, count_ref, w_in_ref, w_out_ref, gain_ref, head_ref, inner_ref, outer_ref, done_ref, h_ref, *refs):
    outs, (all_ref, agg_ref, act_ref) = refs[:-3], refs[-3:]
    tiles, tile, _ = count_ref.shape
    odd = lax.rem(lax.axis_index("dom"), 2) == 1
    inner, outer = inner_ref[...], outer_ref[...]
    before, after = jnp.where(odd, inner, outer), jnp.where(odd, outer, inner)
    rows = tiles * tile
    windows = [
        lambda: jnp.concatenate([before, x_ref[: tile + RIM, :]], axis=0),
        lambda: jnp.concatenate([x_ref[rows - tile - RIM :, :], after], axis=0),
    ]
    preds = staged_update(
        x_ref, count_ref, w_in_ref, w_out_ref, gain_ref, head_ref,
        windows, (0, tiles - 1), agg_ref, act_ref, h_ref,
    )
    all_ref[0] = preds[0]
    all_ref[tiles - 1] = preds[1]
    all_ref[1 : tiles - 1] = done_ref[...]
    me = lax.axis_index("mem")
    per = tiles // members
    for s, out in zip(mem_steps(members), outs):
        for k in range(per):
            out[:, k * tile : (k + 1) * tile] = all_ref[(me ^ s) * per + k]


def update_call(kernel, operands, out_shape, scratch, flops, name):
    return pl.pallas_call(
        kernel,
        out_shape=out_shape,
        in_specs=[pl.BlockSpec(memory_space=VMEM)] * len(operands),
        out_specs=[pl.BlockSpec(memory_space=VMEM)] * len(out_shape),
        scratch_shapes=scratch,
        compiler_params=params(24),
        cost_estimate=cost(flops, 8 * MIB),
        name=name,
    )(*operands)


def update(members, x, counts, w_in, w_out, gain, head, inner, outer):
    tiles, tile, _ = counts.shape
    width = x.shape[1]
    padded = head.shape[0]
    shared = (x, counts, w_in, w_out, gain, head)
    h_mid, pred_mid = update_call(
        inner_kernel,
        shared,
        [
            jax.ShapeDtypeStruct(((tiles - 2) * tile, width), BF16),
            jax.ShapeDtypeStruct((tiles - 2, padded, tile), BF16),
        ],
        [VMEM(((tiles - 2) * tile, width), BF16)] * 2,
        (tiles - 2) * tile * width * width * 10,
        "inner",
    )
    h_end, *preds = update_call(
        functools.partial(outer_kernel, members),
        shared + (inner, outer, pred_mid),
        [jax.ShapeDtypeStruct((2 * tile, width), BF16)]
        + [jax.ShapeDtypeStruct((padded, tiles // members * tile), BF16)] * members,
        [VMEM((tiles, padded, tile), BF16)] + [VMEM((2 * tile, width), BF16)] * 2,
        2 * tile * width * width * 10,
        "outer",
    )
    return h_mid, h_end, preds


def score_kernel(members, weight_ref, inv_ref, target_ref, *refs):
    preds, outs = refs[:members], refs[members:]
    inv_width = inv_ref[...]
    for start in range(0, target_ref.shape[1], 128):
        lanes = slice(start, start + 128)
        weight = weight_ref[:, lanes] * -inv_width
        values = [r[:, lanes].astype(F32) for r in preds]
        sums = [jnp.zeros(v.shape, F32) for v in values]
        for i in range(members):
            for j in range(i + 1, members):
                phi = slope(values[i] - values[j], inv_width)
                sums[i] = sums[i] + phi
                sums[j] = sums[j] - phi
        for i in range(members):
            total = sums[i] * (1.0 / members) - slope(values[i] - target_ref[:, lanes], inv_width)
            outs[i][:, lanes] = (weight * total).astype(BF16)


def score(weight, inv_width, target, preds):
    members = len(preds)
    shape = preds[0].shape
    return pl.pallas_call(
        functools.partial(score_kernel, members),
        out_shape=[jax.ShapeDtypeStruct(shape, BF16)] * members,
        in_specs=[pl.BlockSpec(memory_space=VMEM)] * (3 + members),
        out_specs=[pl.BlockSpec(memory_space=VMEM)] * members,
        compiler_params=params(16),
        cost_estimate=cost(10 * preds[0].size * members * members, MIB, preds[0].size * members * members),
        name="score",
    )(weight, inv_width, target, *preds)


def head_kernel(members, mid_ref, end_ref, *refs):
    scores, (out, all_ref) = refs[:-2], refs[-2:]
    tiles, _, tile = all_ref.shape
    me = lax.axis_index("mem")
    per = tiles // members
    for s, value in zip(mem_steps(members), scores):
        for k in range(per):
            all_ref[(me ^ s) * per + k] = value[:, k * tile : (k + 1) * tile]
    total = dot(all_ref[0], end_ref[:tile, :]) + dot(all_ref[tiles - 1], end_ref[tile:, :])
    for t in range(1, tiles - 1):
        total = total + dot(all_ref[t], mid_ref[(t - 1) * tile : t * tile, :])
    out[...] = total.astype(BF16)


def head_terms(members, mid, end, scores):
    width = end.shape[1]
    tile = end.shape[0] // 2
    tiles = members * scores[0].shape[1] // tile
    padded = scores[0].shape[0]
    return pl.pallas_call(
        functools.partial(head_kernel, members),
        out_shape=[
            jax.ShapeDtypeStruct((padded, width), BF16),
            jax.ShapeDtypeStruct((tiles, padded, tile), BF16),
        ],
        in_specs=[pl.BlockSpec(memory_space=VMEM)] * (2 + members),
        out_specs=[pl.BlockSpec(memory_space=VMEM)] * 2,
        compiler_params=params(16),
        cost_estimate=cost(2 * padded * tiles * tile * width, 3 * MIB),
        name="head_terms",
    )(mid, end, *scores)


def latent_kernel(head_ref, score_ref, out):
    tile = score_ref.shape[2]
    for t in range(score_ref.shape[0]):
        out[0, t * tile : (t + 1) * tile, :] = dot_of(score_ref[t], head_ref[...], 0, 0).astype(BF16)


def latent_grad(head, scores):
    tiles, padded, tile = scores.shape
    width = head.shape[1]
    return pl.pallas_call(
        latent_kernel,
        out_shape=jax.ShapeDtypeStruct((1, tiles * tile, width), BF16),
        in_specs=[pl.BlockSpec(memory_space=VMEM)] * 2,
        out_specs=pl.BlockSpec(memory_space=VMEM),
        compiler_params=params(16),
        cost_estimate=cost(2 * scores.size * width, 3 * MIB),
        name="latent_grad",
    )(head, scores)


def total_kernel(scale, *refs):
    terms, out = refs[:-1], refs[-1]
    total = terms[0][...].astype(F32)
    for term in terms[1:]:
        total = total + term[...].astype(F32)
    out[:, 0, :] = (total * scale)[: out.shape[0], :]


def head_total(terms, num_vars, scale):
    return pl.pallas_call(
        functools.partial(total_kernel, scale),
        out_shape=jax.ShapeDtypeStruct((num_vars, 1, terms[0].shape[1]), F32),
        in_specs=[pl.BlockSpec(memory_space=VMEM)] * len(terms),
        out_specs=pl.BlockSpec(memory_space=VMEM),
        compiler_params=params(16),
        cost_estimate=cost(terms[0].size * len(terms), MIB),
        name="head_total",
    )(*terms)


def shards(
    coarse_latents,
    send_rows,
    up_index,
    up_weight,
    neighbors,
    live_counts,
    area,
    fine_skip,
    targets,
    kernel_width,
    w_in,
    w_out,
    ln_gain,
    w_head,
):
    dom_count = lax.axis_size("dom")
    members = lax.axis_size("mem")
    slots = send_rows.shape[2]
    rows, width = fine_skip.shape
    num_vars = w_head.shape[1]
    padded = num_vars + -num_vars % 8
    tile = min(256, rows // members)

    even = list(range(4, dom_count, 2))
    steps = list(range(dom_count))
    one, sent, table = first_pick(send_rows, coarse_latents, [1] + [s + 1 for s in even])
    one = xor_permute(one, "dom", 1)
    own, two, three, *far = pick(sent, table, [[0], [2], [3]] + [[s] for s in even])
    far = [xor_permute(v, "dom", s) for v, s in zip(pack(one, far), even)]
    two, three = xor_permute(two, "dom", 2), xor_permute(three, "dom", 3)
    sources = (up_index, up_weight, neighbors, w_head.T, area[None, :], targets, kernel_width[None, :])
    split = dom_count - 2
    first_rows, mid_rows, last_rows, scale, counts, head, weight, inv_width, target = spread(
        own, live_counts, sources, steps, slots, 4, split, tile, padded, rows // members
    )
    sums = add_part(first_rows, scale, fine_skip, [own, one, two, three], [slots] * 4, tile, "early")
    sums = add_part(mid_rows, scale, sums, far[:-1], [2 * slots] * (len(far) - 1), tile, "middle")
    x, inner, outer = late(sums, last_rows, scale, far[-1:], tile)
    pairs = [(i, i + 1) for i in range(1, dom_count - 1, 2)]
    outer = lax.ppermute(outer, "dom", pairs + [(j, i) for i, j in pairs])
    inner = xor_permute(inner, "dom", 1)

    mid, end, preds = update(members, x, counts, w_in, w_out, ln_gain[None, :], head, inner, outer)
    trade = functools.partial(mem_trade, mem_steps(members))
    preds = trade(preds)
    scores = trade(score(weight, inv_width, target, preds))
    term, by_tile = head_terms(members, mid, end, scores)
    terms = trade([term] * members)
    grad_latent = latent_grad(head, by_tile)
    factor = 1.0 / math.sqrt(members * rows)
    return (grad_latent, head_total(terms, num_vars, factor).transpose(1, 2, 0))


def solution(mesh):
    return jax.shard_map(
        shards,
        mesh=mesh,
        in_specs=(
            P("mem", "dom", None),
            P("dom", None, None),
            P(None, "dom"),
            P(None, "dom"),
            P(None, "dom"),
            P("dom"),
            P("dom"),
            P("dom", None),
            P(None, "dom"),
            P(),
            P(),
            P(),
            P(),
            P(),
        ),
        out_specs=(P("mem", "dom", None), P("dom", None, None)),
        check_vma=False,
    )
```

```python
import functools
import math

import jax
import jax.numpy as jnp
from jax import lax
from jax.experimental import pallas as pl
from jax.experimental.pallas import tpu as pltpu
from jax.sharding import PartitionSpec as P

RIM = 128
MIB = 1024 * 1024
F32 = jnp.float32
BF16 = jnp.bfloat16
VMEM = pltpu.VMEM


def dot(a, b):
    return jnp.dot(a, b, preferred_element_type=F32)


def dot_of(a, b, da, db):
    return lax.dot_general(a, b, (((da,), (db,)), ((), ())), preferred_element_type=F32)


def params(mib):
    return pltpu.CompilerParams(vmem_limit_bytes=mib * MIB)


def cost(flops, nbytes, trans=0):
    return pl.CostEstimate(flops=flops, bytes_accessed=nbytes, transcendentals=trans)


def columns(rows):
    pad = -rows.shape[0] % 8
    if pad:
        rows = jnp.concatenate([rows, jnp.zeros((pad, rows.shape[1]), rows.dtype)], axis=0)
    return rows.T


def in_hbm(*values):
    return [pltpu.with_memory_space_constraint(v, pltpu.HBM) for v in values]


def fetch(pairs, sems):
    copies = [pltpu.make_async_copy(src, dst, sems.at[i]) for i, (src, dst) in enumerate(pairs)]
    for copy in copies:
        copy.start()
    for copy in copies:
        copy.wait()


def slope(diff, inv_width):
    ratio = diff * inv_width
    return ratio * jnp.exp(ratio * ratio * -0.5)


def xor_permute(value, axis, step):
    count = lax.axis_size(axis)
    return lax.ppermute(value, axis, [(i, i ^ step) for i in range(count)])


def mem_trade(steps, values):
    return [v if s == 0 else xor_permute(v, "mem", s) for s, v in zip(steps, values)]


def mem_steps(members):
    return [0] + list(range(members - 1, 0, -1))


def one_hot(rows, length):
    cols = columns(rows.astype(F32))
    spots = lax.broadcasted_iota(jnp.int32, (rows.shape[1], length), 1).astype(F32)
    hot = [(cols[:, k : k + 1] == spots).astype(F32).astype(BF16) for k in range(rows.shape[0])]
    return jnp.concatenate(hot, axis=0)


def picked(rows, table, outs):
    found = dot(one_hot(rows, table.shape[0]), table).astype(BF16)
    start = 0
    for out in outs:
        out[...] = found[start : start + out.shape[0], :]
        start += out.shape[0]


def send_rows_of(ref, steps):
    me = lax.axis_index("dom")
    return jnp.concatenate([ref[0, pl.ds(me ^ s, 1), :] for s in steps], axis=0)


def first_pick_kernel(steps, send_ref, coarse_ref, out, rows_ref, table_ref, sems):
    rows_copy = pltpu.make_async_copy(send_ref, rows_ref, sems.at[0])
    table_copy = pltpu.make_async_copy(coarse_ref, table_ref, sems.at[1])
    rows_copy.start()
    table_copy.start()
    rows_copy.wait()
    hot = one_hot(send_rows_of(rows_ref, steps), table_ref.shape[1])
    table_copy.wait()
    out[...] = dot(hot, table_ref[0]).astype(BF16)


def first_pick(send_rows, coarse, steps):
    slots, width = send_rows.shape[2], coarse.shape[2]
    return pl.pallas_call(
        functools.partial(first_pick_kernel, steps),
        out_shape=[
            jax.ShapeDtypeStruct((len(steps) * slots, width), BF16),
            jax.ShapeDtypeStruct(send_rows.shape, jnp.int32),
            jax.ShapeDtypeStruct(coarse.shape, BF16),
        ],
        in_specs=[pl.BlockSpec(memory_space=pltpu.HBM)] * 2,
        out_specs=[pl.BlockSpec(memory_space=VMEM)] * 3,
        scratch_shapes=[pltpu.SemaphoreType.DMA((2,))],
        compiler_params=params(8),
        cost_estimate=cost(1, 1),
        name="pick_first",
    )(*in_hbm(send_rows, coarse))


def pick_kernel(steps, rows_ref, table_ref, *outs):
    picked(send_rows_of(rows_ref, steps), table_ref[0], outs)


def pick(rows, table, groups):
    slots, width = rows.shape[2], table.shape[2]
    steps = [s for group in groups for s in group]
    return pl.pallas_call(
        functools.partial(pick_kernel, steps),
        out_shape=[jax.ShapeDtypeStruct((len(group) * slots, width), BF16) for group in groups],
        in_specs=[pl.BlockSpec(memory_space=VMEM)] * 2,
        out_specs=[pl.BlockSpec(memory_space=VMEM)] * len(groups),
        compiler_params=params(8),
        cost_estimate=cost(1, 1),
        name="pick",
    )(rows, table)


def best_scale(weight, counted):
    best = scale = jnp.ones((1, weight.shape[1]), F32)
    for c in range(24):
        factor = 1.0 + 0.0017 * c
        part = weight * (1.0 / factor)
        miss = jnp.where(counted, part - part.astype(BF16).astype(F32), 0.0)
        miss = miss * miss
        miss = miss[0:1] + miss[1:2] + miss[2:3]
        scale = jnp.where(miss < best, factor, scale)
        best = jnp.minimum(miss, best)
    return scale


def spread_kernel(tile, steps, live_ref, *refs):
    sources, outs, scratch = refs[:7], refs[8:17], refs[17:]
    first_ref, mid_ref, last_ref, scale_ref, count_ref, head_ref, area_ref, inv_ref, target_ref = outs
    held, kw_rows, sems = scratch[:7], scratch[7], scratch[8]
    fetch(list(zip(sources, held)), sems)
    index_ref, weight_ref, nb_ref, head_in_ref, area_in_ref, target_in_ref, kw_ref = held
    padded, piece = target_ref.shape
    num_vars = target_in_ref.shape[0]
    start = pl.multiple_of(lax.axis_index("mem") * piece, piece)
    place = start + lax.broadcasted_iota(jnp.int32, (1, piece), 1)
    area_ref[...] = jnp.where(place < live_ref[0], area_in_ref[:, pl.ds(start, piece)], 0.0)
    kw_rows[...] = jnp.ones(kw_rows.shape, F32)
    kw_rows[0:1, :num_vars] = kw_ref[...]
    width = kw_rows[...].T[:padded, 0:1]
    inv_ref[...] = 1.0 / width
    target_ref[...] = jnp.zeros(target_ref.shape, F32)
    target_ref[:num_vars, :] = target_in_ref[:, pl.ds(start, piece)].astype(F32)
    me = lax.axis_index("dom")
    rows = first_ref.shape[0]
    near = first_ref.shape[1] // 2
    cut = near + mid_ref.shape[1] // 2
    slots = cut + last_ref.shape[1]
    span = count_ref.shape[2]
    part = 32
    head_ref[...] = jnp.zeros(head_ref.shape, BF16)
    head_ref[: head_in_ref.shape[0], :] = head_in_ref[...]
    zero, one = jnp.zeros((), BF16), jnp.ones((), BF16)
    spots = lax.broadcasted_iota(jnp.int16, (part, slots), 1)
    places = lax.broadcasted_iota(jnp.int16, (part, span), 1)

    def narrow(value):
        return columns(value.astype(F32)).astype(jnp.int32).astype(jnp.int16)

    def step(t, carry):
        start = pl.multiple_of(t * tile, tile)
        lanes = pl.ds(start, tile)
        wanted = index_ref[:, lanes]
        step_of = lax.shift_right_logical(wanted, 7) ^ me
        place = jnp.zeros(wanted.shape, jnp.int32)
        for i, s in enumerate(steps):
            place = jnp.where(step_of == s, i * 128, place)
        found = place + (wanted & 127)
        i0, i1, i2 = found[0:1], found[1:2], found[2:3]
        w = weight_ref[:, lanes]
        w0, w1, w2 = w[0:1], w[1:2], w[2:3]
        same01, same02, same12 = i0 == i1, i0 == i2, (i1 == i2) & (i0 != i1)
        w0 = w0 + jnp.where(same01, w1, 0.0) + jnp.where(same02, w2, 0.0)
        w1 = jnp.where(same01, 0.0, w1 + jnp.where(same12, w2, 0.0))
        w2 = jnp.where(same02 | same12, 0.0, w2)
        i1 = jnp.where(same01, -1, i1)
        i2 = jnp.where(same02 | same12, -1, i2)
        found = jnp.concatenate([i0, i1, i2], axis=0)
        w = jnp.concatenate([w0, w1, w2], axis=0)
        scale = best_scale(w, found >= cut)
        scale_ref[:, lanes] = scale
        index = narrow(found)
        weight = columns(w / scale)
        high = weight.astype(BF16)
        low = (weight - high.astype(F32)).astype(BF16)
        around = narrow(nb_ref[:, lanes] - start)
        for r in range(0, tile, part):
            here = slice(r, r + part)
            rows_here = pl.ds(pl.multiple_of(start + r, part), part)
            total = jnp.zeros((part, slots), BF16)
            rest = jnp.zeros((part, cut), BF16)
            for k in range(3):
                hit = index[here, k : k + 1] == spots
                total = jnp.where(hit, high[here, k : k + 1], total)
                rest = jnp.where(hit[:, :cut], low[here, k : k + 1], rest)
            first_ref[rows_here, :near] = total[:, :near]
            first_ref[rows_here, near:] = rest[:, :near]
            mid_ref[rows_here, : cut - near] = total[:, near:cut]
            mid_ref[rows_here, cut - near :] = rest[:, near:]
            last_ref[rows_here, :] = total[:, cut:]
            counts = jnp.zeros((part, span), BF16)
            for k in range(nb_ref.shape[0]):
                counts = counts + jnp.where(around[here, k : k + 1] == places, one, zero)
            count_ref[t, here, :] = counts
        return carry

    lax.fori_loop(0, rows // tile, step, 0)


def spread(token, live_counts, sources, steps, slots, near, split, tile, padded, piece):
    up_index, head = sources[0], sources[3]
    rows = up_index.shape[1]
    tiles = rows // tile
    span = tile + 2 * RIM
    cut, total = split * slots, len(steps) * slots
    return pl.pallas_call(
        functools.partial(spread_kernel, tile, steps),
        out_shape=[
            jax.ShapeDtypeStruct((rows, 2 * near * slots), BF16),
            jax.ShapeDtypeStruct((rows, 2 * (cut - near * slots)), BF16),
            jax.ShapeDtypeStruct((rows, total - cut), BF16),
            jax.ShapeDtypeStruct((1, rows), F32),
            jax.ShapeDtypeStruct((tiles, tile, span), BF16),
            jax.ShapeDtypeStruct((padded, head.shape[1]), BF16),
            jax.ShapeDtypeStruct((1, piece), F32),
            jax.ShapeDtypeStruct((padded, 1), F32),
            jax.ShapeDtypeStruct((padded, piece), F32),
        ],
        in_specs=[pl.BlockSpec(memory_space=pltpu.SMEM)]
        + [pl.BlockSpec(memory_space=pltpu.HBM)] * 7
        + [pl.BlockSpec(memory_space=VMEM)],
        out_specs=[pl.BlockSpec(memory_space=VMEM)] * 9,
        scratch_shapes=[VMEM(v.shape, v.dtype) for v in sources]
        + [VMEM((8, 128), F32), pltpu.SemaphoreType.DMA((7,))],
        compiler_params=params(16),
        cost_estimate=cost(1, 1),
        name="spread",
    )(live_counts, *in_hbm(*sources), token)


def pack_kernel(other_ref, *refs):
    count = len(refs) // 2
    for i in range(count):
        mine, out = refs[i], refs[count + i]
        slots = mine.shape[0]
        out[:slots, :] = mine[...]
        out[slots:, :] = other_ref[(i + 1) * slots : (i + 2) * slots, :]


def pack(other, mine):
    slots, width = mine[0].shape
    return pl.pallas_call(
        pack_kernel,
        out_shape=[jax.ShapeDtypeStruct((2 * slots, width), BF16)] * len(mine),
        in_specs=[pl.BlockSpec(memory_space=VMEM)] * (1 + len(mine)),
        out_specs=[pl.BlockSpec(memory_space=VMEM)] * len(mine),
        compiler_params=params(16),
        cost_estimate=cost(1, 1),
        name="pack",
    )(other, *mine)


def part_kernel(tile, lengths, spread_ref, scale_ref, base_ref, *refs):
    tables, out = refs[:-1], refs[-1]
    parts = [r[:length, :] for r, length in zip(tables, lengths)]
    table = jnp.concatenate(parts + parts, axis=0)

    def step(t, carry):
        start = pl.multiple_of(t * tile, tile)
        rows = pl.ds(start, tile)
        scale = columns(scale_ref[:, rows])[:, 0:1]
        out[rows, :] = base_ref[rows, :].astype(F32) + scale * dot(spread_ref[rows, :], table)
        return carry

    lax.fori_loop(0, out.shape[0] // tile, step, 0, unroll=4)


def add_part(spread_rows, scale, base, tables, lengths, tile, name):
    return pl.pallas_call(
        functools.partial(part_kernel, tile, lengths),
        out_shape=jax.ShapeDtypeStruct(base.shape, F32),
        in_specs=[pl.BlockSpec(memory_space=VMEM)] * (3 + len(tables)),
        out_specs=pl.BlockSpec(memory_space=VMEM),
        compiler_params=params(16),
        cost_estimate=cost(1, 1),
        name=name,
    )(spread_rows, scale, base, *tables)


def late_kernel(tile, sum_ref, spread_ref, scale_ref, *refs):
    tables, (x_ref, inner_ref, outer_ref) = refs[:-3], refs[-3:]
    table = jnp.concatenate([r[...] for r in tables], axis=0)
    count = x_ref.shape[0]

    def step(t, carry):
        start = pl.multiple_of(t * tile, tile)
        rows = pl.ds(start, tile)
        scale = columns(scale_ref[:, rows])[:, 0:1]
        x_ref[rows, :] = (sum_ref[rows, :] + scale * dot(spread_ref[rows, :], table)).astype(BF16)
        return carry

    lax.fori_loop(0, count // tile, step, 0, unroll=count // tile)
    odd = lax.rem(lax.axis_index("dom"), 2) == 1
    first, last = x_ref[:RIM, :], x_ref[count - RIM :, :]
    inner_ref[...] = jnp.where(odd, first, last)
    outer_ref[...] = jnp.where(odd, last, first)


def late(sums, spread_rows, scale, tables, tile):
    rows, width = sums.shape
    operands = (sums, spread_rows, scale, *tables)
    edge = jax.ShapeDtypeStruct((RIM, width), BF16)
    return pl.pallas_call(
        functools.partial(late_kernel, tile),
        out_shape=[jax.ShapeDtypeStruct((rows, width), BF16), edge, edge],
        in_specs=[pl.BlockSpec(memory_space=VMEM)] * len(operands),
        out_specs=[pl.BlockSpec(memory_space=VMEM)] * 3,
        compiler_params=params(16),
        cost_estimate=cost(2 * spread_rows.size * width, 8 * MIB),
        name="late",
    )(*operands)


def staged_update(x_ref, count_ref, w_in_ref, w_out_ref, gain_ref, head_ref, windows, places, agg_ref, act_ref, h_ref):
    tile = count_ref.shape[1]
    width = x_ref.shape[1]
    spans = [slice(i * tile, (i + 1) * tile) for i in range(len(places))]
    rows = [slice(t * tile, (t + 1) * tile) for t in places]
    for here, t, window in zip(spans, places, windows):
        agg_ref[here, :] = (dot(count_ref[t], window()) * (1.0 / 6.0)).astype(BF16)
    for here, there in zip(spans, rows):
        pre = dot(x_ref[there, :], w_in_ref[:width, :]) + dot(agg_ref[here, :], w_in_ref[width:, :])
        act_ref[here, :] = (0.5 * pre * (1.0 + jnp.tanh(0.5 * pre))).astype(BF16)
    for here, there in zip(spans, rows):
        upd = dot(act_ref[here, :], w_out_ref[...])
        mean = jnp.mean(upd, axis=1, keepdims=True)
        centred = upd - mean
        var = jnp.mean(centred * centred, axis=1, keepdims=True)
        change = centred * lax.rsqrt(var + 1e-05) * gain_ref[...]
        h_ref[here, :] = (x_ref[there, :].astype(F32) + change).astype(BF16)
    return [dot_of(head_ref[...], h_ref[here, :], 1, 1).astype(BF16) for here in spans]


def inner_kernel(x_ref, count_ref, w_in_ref, w_out_ref, gain_ref, head_ref, h_ref, pred_ref, agg_ref, act_ref):
    tiles, tile, _ = count_ref.shape
    places = range(1, tiles - 1)

    def window(t):
        return lambda: x_ref[t * tile - RIM : (t + 1) * tile + RIM, :]

    preds = staged_update(
        x_ref, count_ref, w_in_ref, w_out_ref, gain_ref, head_ref,
        [window(t) for t in places], places, agg_ref, act_ref, h_ref,
    )
    for i, pred in enumerate(preds):
        pred_ref[i] = pred


def outer_kernel(members, x_ref, count_ref, w_in_ref, w_out_ref, gain_ref, head_ref, inner_ref, outer_ref, done_ref, h_ref, *refs):
    outs, (all_ref, agg_ref, act_ref) = refs[:-3], refs[-3:]
    tiles, tile, _ = count_ref.shape
    odd = lax.rem(lax.axis_index("dom"), 2) == 1
    inner, outer = inner_ref[...], outer_ref[...]
    before, after = jnp.where(odd, inner, outer), jnp.where(odd, outer, inner)
    rows = tiles * tile
    windows = [
        lambda: jnp.concatenate([before, x_ref[: tile + RIM, :]], axis=0),
        lambda: jnp.concatenate([x_ref[rows - tile - RIM :, :], after], axis=0),
    ]
    preds = staged_update(
        x_ref, count_ref, w_in_ref, w_out_ref, gain_ref, head_ref,
        windows, (0, tiles - 1), agg_ref, act_ref, h_ref,
    )
    all_ref[0] = preds[0]
    all_ref[tiles - 1] = preds[1]
    all_ref[1 : tiles - 1] = done_ref[...]
    me = lax.axis_index("mem")
    per = tiles // members
    for s, out in zip(mem_steps(members), outs):
        for k in range(per):
            out[:, k * tile : (k + 1) * tile] = all_ref[(me ^ s) * per + k]


def update_call(kernel, operands, out_shape, scratch, flops, name):
    return pl.pallas_call(
        kernel,
        out_shape=out_shape,
        in_specs=[pl.BlockSpec(memory_space=VMEM)] * len(operands),
        out_specs=[pl.BlockSpec(memory_space=VMEM)] * len(out_shape),
        scratch_shapes=scratch,
        compiler_params=params(24),
        cost_estimate=cost(flops, 8 * MIB),
        name=name,
    )(*operands)


def update(members, x, counts, w_in, w_out, gain, head, inner, outer):
    tiles, tile, _ = counts.shape
    width = x.shape[1]
    padded = head.shape[0]
    shared = (x, counts, w_in, w_out, gain, head)
    h_mid, pred_mid = update_call(
        inner_kernel,
        shared,
        [
            jax.ShapeDtypeStruct(((tiles - 2) * tile, width), BF16),
            jax.ShapeDtypeStruct((tiles - 2, padded, tile), BF16),
        ],
        [VMEM(((tiles - 2) * tile, width), BF16)] * 2,
        (tiles - 2) * tile * width * width * 10,
        "inner",
    )
    h_end, *preds = update_call(
        functools.partial(outer_kernel, members),
        shared + (inner, outer, pred_mid),
        [jax.ShapeDtypeStruct((2 * tile, width), BF16)]
        + [jax.ShapeDtypeStruct((padded, tiles // members * tile), BF16)] * members,
        [VMEM((tiles, padded, tile), BF16)] + [VMEM((2 * tile, width), BF16)] * 2,
        2 * tile * width * width * 10,
        "outer",
    )
    return h_mid, h_end, preds


def score_kernel(members, weight_ref, inv_ref, target_ref, *refs):
    preds, outs = refs[:members], refs[members:]
    inv_width = inv_ref[...]
    for start in range(0, target_ref.shape[1], 128):
        lanes = slice(start, start + 128)
        weight = weight_ref[:, lanes] * -inv_width
        values = [r[:, lanes].astype(F32) for r in preds]
        sums = [jnp.zeros(v.shape, F32) for v in values]
        for i in range(members):
            for j in range(i + 1, members):
                phi = slope(values[i] - values[j], inv_width)
                sums[i] = sums[i] + phi
                sums[j] = sums[j] - phi
        for i in range(members):
            total = sums[i] * (1.0 / members) - slope(values[i] - target_ref[:, lanes], inv_width)
            outs[i][:, lanes] = (weight * total).astype(BF16)


def score(weight, inv_width, target, preds):
    members = len(preds)
    shape = preds[0].shape
    return pl.pallas_call(
        functools.partial(score_kernel, members),
        out_shape=[jax.ShapeDtypeStruct(shape, BF16)] * members,
        in_specs=[pl.BlockSpec(memory_space=VMEM)] * (3 + members),
        out_specs=[pl.BlockSpec(memory_space=VMEM)] * members,
        compiler_params=params(16),
        cost_estimate=cost(10 * preds[0].size * members * members, MIB, preds[0].size * members * members),
        name="score",
    )(weight, inv_width, target, *preds)


def head_kernel(members, mid_ref, end_ref, *refs):
    scores, (out, all_ref) = refs[:-2], refs[-2:]
    tiles, _, tile = all_ref.shape
    me = lax.axis_index("mem")
    per = tiles // members
    for s, value in zip(mem_steps(members), scores):
        for k in range(per):
            all_ref[(me ^ s) * per + k] = value[:, k * tile : (k + 1) * tile]
    total = dot(all_ref[0], end_ref[:tile, :]) + dot(all_ref[tiles - 1], end_ref[tile:, :])
    for t in range(1, tiles - 1):
        total = total + dot(all_ref[t], mid_ref[(t - 1) * tile : t * tile, :])
    out[...] = total.astype(BF16)


def head_terms(members, mid, end, scores):
    width = end.shape[1]
    tile = end.shape[0] // 2
    tiles = members * scores[0].shape[1] // tile
    padded = scores[0].shape[0]
    return pl.pallas_call(
        functools.partial(head_kernel, members),
        out_shape=[
            jax.ShapeDtypeStruct((padded, width), BF16),
            jax.ShapeDtypeStruct((tiles, padded, tile), BF16),
        ],
        in_specs=[pl.BlockSpec(memory_space=VMEM)] * (2 + members),
        out_specs=[pl.BlockSpec(memory_space=VMEM)] * 2,
        compiler_params=params(16),
        cost_estimate=cost(2 * padded * tiles * tile * width, 3 * MIB),
        name="head_terms",
    )(mid, end, *scores)


def latent_kernel(head_ref, score_ref, out):
    tile = score_ref.shape[2]
    for t in range(score_ref.shape[0]):
        out[0, t * tile : (t + 1) * tile, :] = dot_of(score_ref[t], head_ref[...], 0, 0).astype(BF16)


def latent_grad(head, scores):
    tiles, padded, tile = scores.shape
    width = head.shape[1]
    return pl.pallas_call(
        latent_kernel,
        out_shape=jax.ShapeDtypeStruct((1, tiles * tile, width), BF16),
        in_specs=[pl.BlockSpec(memory_space=VMEM)] * 2,
        out_specs=pl.BlockSpec(memory_space=VMEM),
        compiler_params=params(16),
        cost_estimate=cost(2 * scores.size * width, 3 * MIB),
        name="latent_grad",
    )(head, scores)


def total_kernel(scale, *refs):
    terms, out = refs[:-1], refs[-1]
    total = terms[0][...].astype(F32)
    for term in terms[1:]:
        total = total + term[...].astype(F32)
    out[:, 0, :] = (total * scale)[: out.shape[0], :]


def head_total(terms, num_vars, scale):
    return pl.pallas_call(
        functools.partial(total_kernel, scale),
        out_shape=jax.ShapeDtypeStruct((num_vars, 1, terms[0].shape[1]), F32),
        in_specs=[pl.BlockSpec(memory_space=VMEM)] * len(terms),
        out_specs=pl.BlockSpec(memory_space=VMEM),
        compiler_params=params(16),
        cost_estimate=cost(terms[0].size * len(terms), MIB),
        name="head_total",
    )(*terms)


def shards(
    coarse_latents,
    send_rows,
    up_index,
    up_weight,
    neighbors,
    live_counts,
    area,
    fine_skip,
    targets,
    kernel_width,
    w_in,
    w_out,
    ln_gain,
    w_head,
):
    dom_count = lax.axis_size("dom")
    members = lax.axis_size("mem")
    slots = send_rows.shape[2]
    rows, width = fine_skip.shape
    num_vars = w_head.shape[1]
    padded = num_vars + -num_vars % 8
    tile = min(256, rows // members)

    even = list(range(4, dom_count, 2))
    steps = list(range(dom_count))
    one, sent, table = first_pick(send_rows, coarse_latents, [1] + [s + 1 for s in even])
    one = xor_permute(one, "dom", 1)
    own, two, three, *far = pick(sent, table, [[0], [2], [3]] + [[s] for s in even])
    far = [xor_permute(v, "dom", s) for v, s in zip(pack(one, far), even)]
    two, three = xor_permute(two, "dom", 2), xor_permute(three, "dom", 3)
    sources = (up_index, up_weight, neighbors, w_head.T, area[None, :], targets, kernel_width[None, :])
    split = dom_count - 2
    first_rows, mid_rows, last_rows, scale, counts, head, weight, inv_width, target = spread(
        own, live_counts, sources, steps, slots, 4, split, tile, padded, rows // members
    )
    sums = add_part(first_rows, scale, fine_skip, [own, one, two, three], [slots] * 4, tile, "early")
    sums = add_part(mid_rows, scale, sums, far[:-1], [2 * slots] * (len(far) - 1), tile, "middle")
    x, inner, outer = late(sums, last_rows, scale, far[-1:], 2 * tile)
    pairs = [(i, i + 1) for i in range(1, dom_count - 1, 2)]
    outer = lax.ppermute(outer, "dom", pairs + [(j, i) for i, j in pairs])
    inner = xor_permute(inner, "dom", 1)

    mid, end, preds = update(members, x, counts, w_in, w_out, ln_gain[None, :], head, inner, outer)
    trade = functools.partial(mem_trade, mem_steps(members))
    preds = trade(preds)
    scores = trade(score(weight, inv_width, target, preds))
    term, by_tile = head_terms(members, mid, end, scores)
    terms = mem_trade([0] + mem_steps(members)[1:2] + sorted(mem_steps(members)[2:]), [term] * members)
    grad_latent = latent_grad(head, by_tile)
    factor = 1.0 / math.sqrt(members * rows)
    return (grad_latent, head_total(terms, num_vars, factor).transpose(1, 2, 0))


def solution(mesh):
    return jax.shard_map(
        shards,
        mesh=mesh,
        in_specs=(
            P("mem", "dom", None),
            P("dom", None, None),
            P(None, "dom"),
            P(None, "dom"),
            P(None, "dom"),
            P("dom"),
            P("dom"),
            P("dom", None),
            P(None, "dom"),
            P(),
            P(),
            P(),
            P(),
            P(),
        ),
        out_specs=(P("mem", "dom", None), P("dom", None, None)),
        check_vma=False,
    )
```
